256 devices in a mesh: dp: 4 (over x_hi, core), ctx: 64 (over y, x_lo, z).
Axes of the slice: x: 4 (x_hi: 2, x_lo: 2; x = x_hi * 2 + x_lo), y: 4, z: 8, core: 2. Of those that a mesh axis runs over, the one named last changes fastest.
Arguments:
- queries: bfloat16 [4, 16384, 1024], P('dp', 'ctx'), may hold values from -16 to 16
- key_rows: bfloat16 [4, 16384, 1024], P('dp', 'ctx'), may hold values from -8 to 8
- values: bfloat16 [4, 16384, 1024], P('dp', 'ctx'), may hold values from -6 to 6
- cotangent: bfloat16 [4, 16384, 1024], P('dp', 'ctx'), may hold values from -6 to 6
- slot_starts: int32 [4, 64], P('dp'), may hold values from -1 to 16256, as said below
- prompt_lens: int32 [4, 64], P('dp'), may hold values from 0 to 128, as said below
- prompt_bias: float32 [8], replicated, may hold values from -1 to 2
Outputs:
- attended: bfloat16 [4, 16384, 1024], P('dp', 'ctx')
- grad_queries: bfloat16 [4, 16384, 1024], P('dp', 'ctx')
- grad_keys: bfloat16 [4, 16384, 1024], P('dp', 'ctx')
- grad_values: bfloat16 [4, 16384, 1024], P('dp', 'ctx')
- grad_bias: float32 [8], replicated
The draws below stay inside these ranges and needn't reach their ends.
Inputs may be any that keep to these rules, and one draw needn't show every extreme that they name: `slot_starts`: each index of ctx owns one slot. They hold, ascending, the first frames of the utterances that begin among that device's 256 frames, then -1. Frame 0 begins an utterance. Every start s has s % 256 <= 128, and two starts of one device lie 128 or more apart. In each packed sequence some device fills all 1 slots, and the last index of ctx starts an utterance at frame 16384 - 128. `prompt_lens`: A used slot holds 1 or more and at most the distance to the next used start; an unused slot holds 0. In each packed sequence some slot holds 128.
All inputs are finite; a program needn't handle non-finite values.
Results may differ from the reference program's by a relative error of at most 0.006.
Values may be sent and summed in bfloat16 or wider, within the bound.
No kernel may reach another device: no remote copies, remote signals or barrier semaphores. Data moves between devices by JAX's collectives and lax.ppermute only.
A program may use at most 320 MiB of HBM per device.

```python
import math
import jax
import jax.numpy as jnp
from jax import lax

H = 8
HD = 128
ROWS = 256
HW = 128
PMAX = 128
USLOT = 1
FRAMES = 16384
WIDTH = 1024
N_DP = 4
N_CTX = 64


def slot_layout(key):
    split_keys = jax.random.split(key, 4)
    shard_ids = jnp.arange(N_CTX, dtype=jnp.int32)[None, :]
    counts = jnp.maximum(jax.random.randint(split_keys[0], (N_DP, N_CTX), -3, USLOT + 1), 0)
    fullest = jax.random.randint(split_keys[1], (N_DP, 1), 1, N_CTX)
    counts = jnp.where(shard_ids == fullest, USLOT, counts)
    counts = jnp.where(shard_ids == N_CTX - 1, USLOT, counts)
    counts = jnp.where(shard_ids == 0, jnp.maximum(counts, 1), counts)
    spread = ROWS // USLOT
    slot_rank = jnp.arange(USLOT, dtype=jnp.int32)[None, None, :]
    jitter = jax.random.randint(split_keys[2], (N_DP, N_CTX, USLOT), 0, spread - PMAX + 1)
    jitter = jnp.where((shard_ids[:, :, None] == N_CTX - 1) & (slot_rank == USLOT - 1), spread - PMAX, jitter)
    offset = slot_rank * spread + jitter
    offset = jnp.where((shard_ids[:, :, None] == 0) & (slot_rank == 0), 0, offset)
    in_use = slot_rank < counts[:, :, None]
    starts = jnp.where(in_use, shard_ids[:, :, None] * ROWS + offset, -1)
    lengths = jax.random.randint(split_keys[3], (N_DP, N_CTX, USLOT), (PMAX + 1) // 2, PMAX + 1)
    lengths = jnp.where((shard_ids[:, :, None] == fullest[:, :, None]) & (slot_rank == 0), PMAX, lengths)
    lengths = jnp.where(in_use, lengths, 0)
    return (starts.reshape(N_DP, N_CTX * USLOT).astype(jnp.int32), lengths.reshape(N_DP, N_CTX * USLOT).astype(jnp.int32))


def draw_slot_starts(key, part):
    return slot_layout(key)[0]


def draw_prompt_lens(key, part):
    return slot_layout(key)[1]


def paired_fields(key):
    frames = ROWS * N_CTX
    shape = (N_DP, frames, H * HD)
    split_keys = jax.random.split(key, 2)

    def base_draw(sub_key):
        normal_part = jax.random.truncated_normal(sub_key, -6.0, 6.0, shape, jnp.float32)
        return normal_part
    query_base = base_draw(split_keys[0])
    key_base = base_draw(split_keys[1])
    position = jnp.arange(frames, dtype=jnp.int32)[None, :, None] % ROWS
    marked = position == ROWS // 2
    follower = position == ROWS // 2 + 1
    key_new = jnp.where(marked, key_base, jnp.where(follower, key_base, key_base))
    query_new = jnp.where(marked, query_base, query_base)
    return (query_new, key_new)


def draw_queries(key, part):
    fields = paired_fields(key)
    return fields[0].astype(jnp.bfloat16)


def draw_key_rows(key, part):
    fields = paired_fields(key)
    return fields[1].astype(jnp.bfloat16)


def block_levels(stream_key, extent, cuts, least, top_value):
    gain = 1.0
    for dim, blocks in cuts:
        steps = jax.random.uniform(jax.random.fold_in(jax.random.fold_in(stream_key, 6), dim), (blocks,), jnp.float32, least / len(cuts), top_value / len(cuts))
        gain = gain * jnp.repeat(jnp.exp(steps), extent[dim] // blocks).reshape((-1,) + (1,) * (len(extent) - 1 - dim))
    return gain


def scatter_about(stream_key, extent, scale, limit, cuts=(), kind=jnp.bfloat16):
    level = block_levels(stream_key, extent, cuts, -0.22, 0.18) if cuts else 1.0
    entries = jax.random.normal(stream_key, extent, jnp.float32) * scale * level
    return jnp.minimum(jnp.maximum(entries, -limit), limit).astype(kind)


def setup_inputs(seed: int = 0) -> dict:
    streams_of = jax.random.split(jax.random.key(seed), 8)
    return {
        "queries": draw_queries(jax.random.fold_in(streams_of[7], 71), 0),
        "key_rows": draw_key_rows(jax.random.fold_in(streams_of[7], 71), 0),
        "values": scatter_about(streams_of[2], (N_DP, FRAMES, WIDTH), 1.0, 6.0, ((0, 4), (1, 64))),
        "cotangent": scatter_about(streams_of[3], (N_DP, FRAMES, WIDTH), 1.0, 6.0, ((0, 4), (1, 64))),
        "slot_starts": draw_slot_starts(jax.random.fold_in(streams_of[7], 71), 0),
        "prompt_lens": draw_prompt_lens(jax.random.fold_in(streams_of[7], 71), 0),
        "prompt_bias": jnp.clip(jax.random.uniform(streams_of[6], (H,), jnp.float32, -1.0, 2.0), -1.0, 2.0),
    }


def utterance_info(positions, starts, plens):
    usable = starts >= 0
    reached = usable[None, :] & (starts[None, :] <= positions[:, None])
    start_of = lax.optimization_barrier(jnp.max(jnp.where(reached, starts[None, :], -2), axis=1)).astype(jnp.int32)
    owning = reached & (starts[None, :] == start_of[:, None])
    length = lax.optimization_barrier(jnp.sum(jnp.where(owning, plens[None, :], 0), axis=1)).astype(jnp.int32)
    return (start_of, length)

def window_mask(query_pos, key_pos, starts, plens, frames):
    query_start = utterance_info(query_pos, starts, plens)[0]
    key_info = utterance_info(key_pos, starts, plens)
    near_rows = jnp.abs(query_pos[:, None] - key_pos[None, :]) <= HW
    usable = (key_pos >= 0) & (key_pos < frames) & (key_pos - key_info[0] >= key_info[1])
    living = (query_pos >= 0) & (query_pos < frames)
    return near_rows & (query_start[:, None] == key_info[0][None, :]) & usable[None, :] & living[:, None]

def prompt_mask(query_start, cand_starts, cand_lens):
    offsets = jnp.arange(PMAX, dtype=jnp.int32)
    matched = (query_start[:, None, None] == cand_starts[None, :, None]) & (offsets[None, None, :] < cand_lens[None, :, None])
    return matched.reshape(query_start.shape[0], -1)

def attention_terms(query_rows, cotan_rows, key_block, allowed, column_bias, score_scale):
    count = query_rows.shape[0]
    key_count = key_block.shape[0]
    head_count = column_bias.shape[0]
    width = query_rows.shape[1]
    head_width = width // head_count
    q_heads = query_rows.astype(jnp.float32).reshape(count, head_count, head_width)
    d_heads = cotan_rows.astype(jnp.float32).reshape(count, head_count, head_width)
    k_heads = key_block[:, :width].astype(jnp.float32).reshape(key_count, head_count, head_width)
    v_heads = key_block[:, width:].astype(jnp.float32).reshape(key_count, head_count, head_width)
    scores = jnp.einsum('rhd,khd->hrk', q_heads, k_heads) * score_scale + column_bias[:, None, :]
    scores = jnp.where(allowed[None], scores, -1e+30)
    row_max = lax.optimization_barrier(jnp.max(scores, axis=2, keepdims=True))
    raised = jnp.where(allowed[None], jnp.exp(scores - row_max), 0.0)
    row_total = lax.optimization_barrier(jnp.sum(raised, axis=2, keepdims=True))
    probs = raised / row_total
    low_probs = lax.optimization_barrier(probs.astype(jnp.bfloat16)).astype(jnp.float32)
    attended = jnp.einsum('hrk,khd->rhd', low_probs, v_heads).reshape(count, width)
    dprobs = jnp.einsum('rhd,khd->hrk', d_heads, v_heads)
    row_delta = lax.optimization_barrier(jnp.sum(probs * dprobs, axis=2, keepdims=True))
    dscores = probs * (dprobs - row_delta)
    low_dscores = lax.optimization_barrier((dscores * score_scale).astype(jnp.bfloat16)).astype(jnp.float32)
    grad_q = jnp.einsum('hrk,khd->rhd', low_dscores, k_heads).reshape(count, width)
    grad_k = jnp.einsum('hrk,rhd->khd', low_dscores, q_heads).reshape(key_count, width)
    grad_v = jnp.einsum('hrk,rhd->khd', low_probs, d_heads).reshape(key_count, width)
    return (attended, grad_q, jnp.concatenate([grad_k, grad_v], axis=1), lax.optimization_barrier(jnp.sum(dscores, axis=1)))

def reference(queries, key_rows, values, cotangent, slot_starts, prompt_lens, prompt_bias):
    frames = ROWS * N_CTX
    width = H * HD
    score_scale = 1.0 / math.sqrt(HD)
    window_len = ROWS + 2 * HW
    column_bias = jnp.concatenate([jnp.zeros((H, window_len), jnp.float32), jnp.broadcast_to(prompt_bias[:, None], (H, (USLOT + 1) * PMAX))], axis=1)

    def one_group(pieces):
        group_q, group_k, group_v, group_d, starts, plens = pieces
        joined = jnp.concatenate([group_k, group_v], axis=1)
        padded = jnp.pad(joined, ((HW, HW), (0, 0)))

        def one_shard(carry, shard_id):
            grads, bias_grad = carry
            first_frame = (shard_id * ROWS).astype(jnp.int32)
            q_block = lax.dynamic_slice_in_dim(group_q, first_frame, ROWS, 0)
            d_block = lax.dynamic_slice_in_dim(group_d, first_frame, ROWS, 0)
            window = lax.dynamic_slice_in_dim(padded, first_frame, window_len, 0)
            earlier_starts = (starts >= 0) & (starts < first_frame)
            carried = jnp.max(jnp.where(earlier_starts, starts, -3)).astype(jnp.int32)
            carried_len = jnp.sum(jnp.where(earlier_starts & (starts == carried), plens, 0)).astype(jnp.int32)
            local_starts = lax.dynamic_slice_in_dim(starts, (shard_id * USLOT).astype(jnp.int32), USLOT)
            local_lens = lax.dynamic_slice_in_dim(plens, (shard_id * USLOT).astype(jnp.int32), USLOT)
            cand_starts = jnp.concatenate([carried.reshape(1), local_starts]).astype(jnp.int32)
            cand_lens = jnp.concatenate([carried_len.reshape(1), local_lens]).astype(jnp.int32)
            anchors = jnp.clip(cand_starts, 0, frames - PMAX).astype(jnp.int32)
            prompts = jnp.concatenate([lax.dynamic_slice_in_dim(joined, anchors[member], PMAX, 0) for member in range(USLOT + 1)], axis=0)
            key_block = jnp.concatenate([window, prompts], axis=0)
            query_pos = first_frame + jnp.arange(ROWS, dtype=jnp.int32)
            key_pos = first_frame - HW + jnp.arange(window_len, dtype=jnp.int32)
            query_start = utterance_info(query_pos, starts, plens)[0]
            allowed = jnp.concatenate([window_mask(query_pos, key_pos, starts, plens, frames), prompt_mask(query_start, cand_starts, cand_lens)], axis=1)
            attended, grad_q, grad_kv, bias_terms = attention_terms(q_block, d_block, key_block, allowed, column_bias, score_scale)
            current = lax.dynamic_slice_in_dim(grads, first_frame, window_len, 0)
            grads = lax.dynamic_update_slice_in_dim(grads, current + grad_kv[:window_len], first_frame, 0)
            for member in range(USLOT + 1):
                target = anchors[member] + HW
                piece = grad_kv[window_len + member * PMAX:window_len + (member + 1) * PMAX]
                current = lax.dynamic_slice_in_dim(grads, target, PMAX, 0)
                grads = lax.dynamic_update_slice_in_dim(grads, current + piece, target, 0)
            bias_grad = bias_grad + lax.optimization_barrier(jnp.sum(bias_terms[:, window_len:], axis=1))
            return ((grads, bias_grad), (attended.astype(jnp.bfloat16), grad_q.astype(jnp.bfloat16)))
        initial = (jnp.zeros((frames + 2 * HW, 2 * width), jnp.float32), jnp.zeros((H,), jnp.float32))
        finals, stacked = lax.scan(one_shard, initial, jnp.arange(N_CTX, dtype=jnp.int32))
        grads = finals[0][HW:HW + frames]
        return (stacked[0].reshape(frames, width), stacked[1].reshape(frames, width), grads[:, :width].astype(jnp.bfloat16), grads[:, width:].astype(jnp.bfloat16), finals[1])
    results = lax.map(one_group, (queries, key_rows, values, cotangent, slot_starts, prompt_lens))
    return (results[0], results[1], results[2], results[3], lax.optimization_barrier(jnp.sum(results[4], axis=0)))
```

```python
import math

import jax
import jax.numpy as jnp
from jax import lax
from jax.experimental import pallas as pl
from jax.experimental.pallas import tpu as pltpu
from jax.sharding import PartitionSpec as P

HW = 128
PMAX = 128
ROWS = 256
HD = 128
HEADS = 8
WIDTH = HEADS * HD
BANDS = 8
BAND = PMAX // BANDS
NEG = -1e30
LOG2E = math.log2(math.e)
SCALE = 1.0 / math.sqrt(HD)

SMEM = pl.BlockSpec(memory_space=pltpu.SMEM)
VMEM = pl.BlockSpec(memory_space=pltpu.VMEM)
PARAMS = pltpu.CompilerParams(vmem_limit_bytes=48 * 1024 * 1024)


def nt(a, b):
    return lax.dot_general(a, b, (((1,), (1,)), ((), ())), preferred_element_type=jnp.float32)


def tn(a, b):
    return lax.dot_general(a, b, (((0,), (0,)), ((), ())), preferred_element_type=jnp.float32)


def nn(a, b):
    return lax.dot_general(a, b, (((1,), (0,)), ((), ())), preferred_element_type=jnp.float32)


def own_start(starts_ref, me):
    start = starts_ref[0, me]
    return start >= 0, jnp.where(start >= 0, start - me * ROWS, 0)


def columns(head):
    return slice(head * HD, (head + 1) * HD)


def cut_kernel(starts_ref, k_ref, v_ref, out_ref):
    me = lax.axis_index("ctx")
    offset = own_start(starts_ref, me)[1]
    row = lax.broadcasted_iota(jnp.int32, (PMAX, ROWS), 0)
    frame = lax.broadcasted_iota(jnp.int32, (PMAX, ROWS), 1)
    pick = (frame == row + offset).astype(jnp.bfloat16)
    for head in range(HEADS):
        for part, ref in enumerate((k_ref, v_ref)):
            rows = nn(pick, ref[0, :, columns(head)]).astype(jnp.bfloat16)
            out_ref[:, head, part * BAND : (part + 1) * BAND, :] = rows.reshape(BANDS, BAND, HD)


def cut_prompt(starts, key_rows, values):
    return pl.pallas_call(
        cut_kernel,
        out_shape=jax.ShapeDtypeStruct((BANDS, HEADS, 2 * BAND, HD), jnp.bfloat16),
        in_specs=[SMEM, VMEM, VMEM],
        out_specs=VMEM,
        compiler_params=PARAMS,
        name="cut_prompt",
    )(starts, key_rows, values)


def route_kernel(starts_ref, in_ref, out_ref):
    count = in_ref.shape[0]

    def step(target, source):
        out_ref[target] = in_ref[source]
        return jnp.where(starts_ref[0, target] >= 0, target, source)

    lax.fori_loop(0, count, step, jnp.int32(0), unroll=8)


def route(starts, pieces):
    return pl.pallas_call(
        route_kernel,
        out_shape=jax.ShapeDtypeStruct(pieces.shape, pieces.dtype),
        in_specs=[SMEM, VMEM],
        out_specs=VMEM,
        compiler_params=PARAMS,
        name="route",
    )(starts, pieces)


def gather_kernel(starts_ref, in_ref, out_ref, bias_ref):
    count = in_ref.shape[0]
    out_ref[...] = jnp.zeros_like(out_ref)

    def step(target, carry):
        source, total, bias = carry
        block = in_ref[target].astype(jnp.float32)
        total = total + block[: 2 * BAND]
        out_ref[source] = total.astype(jnp.bfloat16)
        bias = bias + block[2 * BAND : 2 * BAND + HEADS] + block[2 * BAND + HEADS :]
        begins = starts_ref[0, target] >= 0
        return jnp.where(begins, target, source), jnp.where(begins, 0.0, total), bias

    first = in_ref[0].astype(jnp.float32)
    bias = first[2 * BAND : 2 * BAND + HEADS] + first[2 * BAND + HEADS :]
    carry = (jnp.int32(0), jnp.zeros((2 * BAND, HD), jnp.float32), bias)
    bias_ref[...] = lax.fori_loop(1, count, step, carry, unroll=7)[2]


def gather(starts, pieces):
    return pl.pallas_call(
        gather_kernel,
        out_shape=(
            jax.ShapeDtypeStruct((pieces.shape[0], 2 * BAND, HD), jnp.bfloat16),
            jax.ShapeDtypeStruct((HEADS, HD), jnp.float32),
        ),
        in_specs=[SMEM, VMEM],
        out_specs=(VMEM, VMEM),
        compiler_params=PARAMS,
        name="gather",
    )(starts, pieces)


def attention_kernel(
    starts_ref,
    lens_ref,
    bias_ref,
    q_ref,
    d_ref,
    k_ref,
    v_ref,
    low_ref,
    high_ref,
    prompt_ref,
    attended_ref,
    gq_ref,
    gk_ref,
    gv_ref,
    glow_ref,
    ghigh_ref,
    gprompt_ref,
    own_mask,
    own_flag,
    low_mask,
    high_mask,
    prompt_mask,
    bias_sums,
):
    head = pl.program_id(0)
    me = lax.axis_index("ctx")
    last = starts_ref.shape[1] - 1

    @pl.when(head == 0)
    def _():
        begins, offset = own_start(starts_ref, me)
        offset = jnp.where(begins, offset, ROWS)
        own_len = jnp.where(begins, lens_ref[0, me], 0)

        def carried_info(index, found):
            used = starts_ref[0, index] >= 0
            return (
                jnp.where(used, starts_ref[0, index], found[0]),
                jnp.where(used, lens_ref[0, index], found[1]),
            )

        start, length = lax.fori_loop(0, me, carried_info, (jnp.int32(0), jnp.int32(0)))
        prompt_end = start + length - (me * ROWS - HW)
        after = jnp.minimum(me + 1, last)
        next_begins, next_offset = own_start(starts_ref, after)
        next_offset = jnp.where(next_begins, next_offset, HW)
        next_offset = jnp.where(me < last, next_offset, 0)

        def hold(ref, allowed):
            ref[...] = jnp.where(allowed, 0.0, NEG)

        key = lax.broadcasted_iota(jnp.int32, (ROWS, ROWS), 0)
        row = lax.broadcasted_iota(jnp.int32, (ROWS, ROWS), 1)
        prompt = (key >= offset) & (key < offset + own_len)
        near = jnp.abs(row - key) <= HW
        hold(own_mask, ((row >= offset) == (key >= offset)) & (prompt | near))
        own_flag[...] = prompt[:, :HW].astype(jnp.float32)
        key = lax.broadcasted_iota(jnp.int32, (HW, HW), 0)
        row = lax.broadcasted_iota(jnp.int32, (HW, HW), 1)
        hold(low_mask, (key >= row) & (row < offset) & (key >= prompt_end) & (me > 0))
        hold(high_mask, (key <= row) & (key < next_offset))
        key = lax.broadcasted_iota(jnp.int32, (PMAX, ROWS), 0)
        row = lax.broadcasted_iota(jnp.int32, (PMAX, ROWS), 1)
        hold(prompt_mask, (row < offset) & (key < length))
        bias_sums[...] = jnp.zeros_like(bias_sums)

    q, d, k, v = q_ref[0], d_ref[0], k_ref[0], v_ref[0]
    kl, vl = low_ref[0], low_ref[1]
    kr, vr = high_ref[0], high_ref[1]
    kp = prompt_ref[:, 0, :BAND, :].reshape(PMAX, HD)
    vp = prompt_ref[:, 0, BAND:, :].reshape(PMAX, HD)
    bias = bias_ref[head] * LOG2E
    s_own, s_prompt = nt(k, q), nt(kp, q)
    dp_own, dp_prompt = nt(v, d), nt(vp, d)
    own_probs, own_ds, prompt_probs, prompt_ds = [], [], [], []
    bias_sum = jnp.zeros((1, HW), jnp.float32)
    for half, (kh, vh, mask_ref) in enumerate(((kl, vl, low_mask), (kr, vr, high_mask))):
        part = slice(half * HW, (half + 1) * HW)
        q_half, d_half = q[part], d[part]
        scores = [
            nt(kh, q_half) * (SCALE * LOG2E) + mask_ref[...],
            s_own[:, part] * (SCALE * LOG2E) + (own_mask[:, part] + own_flag[...] * bias),
            s_prompt[:, part] * (SCALE * LOG2E) + (prompt_mask[:, part] + bias),
        ]
        dprobs = [nt(vh, d_half), dp_own[:, part], dp_prompt[:, part]]
        tops = [jnp.max(x, axis=0, keepdims=True) for x in scores]
        top = jnp.maximum(jnp.maximum(tops[0], tops[1]), tops[2])
        raised = [jnp.exp2(x - top) for x in scores]
        sums = [jnp.sum(x, axis=0, keepdims=True) for x in raised]
        inverse = 1.0 / (sums[0] + sums[1] + sums[2])
        probs = [x * inverse for x in raised]
        deltas = [jnp.sum(x * y, axis=0, keepdims=True) for x, y in zip(probs, dprobs)]
        delta = deltas[0] + deltas[1] + deltas[2]
        dscores = [(x * SCALE) * (y - delta) for x, y in zip(probs, dprobs)]
        bias_sum = (
            bias_sum
            + jnp.sum(dscores[1] * own_flag[...], axis=0, keepdims=True)
            + jnp.sum(dscores[2], axis=0, keepdims=True)
        )
        low_probs = [x.astype(jnp.bfloat16) for x in probs]
        low_ds = [x.astype(jnp.bfloat16) for x in dscores]
        attended = tn(low_probs[0], vh) + tn(low_probs[1], v) + tn(low_probs[2], vp)
        attended_ref[0, part, :] = attended.astype(jnp.bfloat16)
        grad_q = tn(low_ds[0], kh) + tn(low_ds[1], k) + tn(low_ds[2], kp)
        gq_ref[0, part, :] = grad_q.astype(jnp.bfloat16)
        ref = (glow_ref, ghigh_ref)[half]
        ref[0] = nn(low_ds[0], q_half).astype(jnp.bfloat16)
        ref[1] = nn(low_probs[0], d_half).astype(jnp.bfloat16)
        own_probs.append(low_probs[1])
        own_ds.append(low_ds[1])
        prompt_probs.append(low_probs[2])
        prompt_ds.append(low_ds[2])

    gk_ref[...] = nn(jnp.concatenate(own_ds, axis=1), q)
    gv_ref[...] = nn(jnp.concatenate(own_probs, axis=1), d)
    gkp = nn(jnp.concatenate(prompt_ds, axis=1), q).astype(jnp.bfloat16)
    gvp = nn(jnp.concatenate(prompt_probs, axis=1), d).astype(jnp.bfloat16)
    gprompt_ref[:, pl.ds(head, 1), :BAND, :] = gkp.reshape(BANDS, 1, BAND, HD)
    gprompt_ref[:, pl.ds(head, 1), BAND : 2 * BAND, :] = gvp.reshape(BANDS, 1, BAND, HD)
    bias_sums[pl.ds(head, 1), :] = bias_sum * (1.0 / SCALE)

    @pl.when(head == HEADS - 1)
    def _():
        sums = bias_sums[...]
        upper = sums.astype(jnp.bfloat16)
        lower = (sums - upper.astype(jnp.float32)).astype(jnp.bfloat16)
        tile = jnp.concatenate([upper, lower], axis=0)
        for band in range(BANDS):
            for member in range(HEADS):
                gprompt_ref[band, member, 2 * BAND :, :] = tile


def attention(starts, lens, bias, queries, cotangent, key_rows, values, low, high, prompt):
    rows = pl.BlockSpec((1, ROWS, HD), lambda head: (0, 0, head))
    halo = pl.BlockSpec((2, HW, HD), lambda head: (0, 0, head))
    pieces = pl.BlockSpec((BANDS, 1, 2 * BAND, HD), lambda head: (0, head, 0, 0))
    total = pl.BlockSpec((ROWS, HD), lambda head: (0, head))
    whole = pl.BlockSpec((BANDS, HEADS, 2 * BAND + 2 * HEADS, HD), lambda head: (0, 0, 0, 0))
    return pl.pallas_call(
        attention_kernel,
        grid=(HEADS,),
        out_shape=(
            jax.ShapeDtypeStruct((1, ROWS, WIDTH), jnp.bfloat16),
            jax.ShapeDtypeStruct((1, ROWS, WIDTH), jnp.bfloat16),
            jax.ShapeDtypeStruct((ROWS, WIDTH), jnp.float32),
            jax.ShapeDtypeStruct((ROWS, WIDTH), jnp.float32),
            jax.ShapeDtypeStruct((2, HW, WIDTH), jnp.bfloat16),
            jax.ShapeDtypeStruct((2, HW, WIDTH), jnp.bfloat16),
            jax.ShapeDtypeStruct((BANDS, HEADS, 2 * BAND + 2 * HEADS, HD), jnp.bfloat16),
        ),
        in_specs=[SMEM, SMEM, SMEM, rows, rows, rows, rows, halo, halo, pieces],
        out_specs=(rows, rows, total, total, halo, halo, whole),
        scratch_shapes=[
            pltpu.VMEM((ROWS, ROWS), jnp.float32),
            pltpu.VMEM((ROWS, HW), jnp.float32),
            pltpu.VMEM((HW, HW), jnp.float32),
            pltpu.VMEM((HW, HW), jnp.float32),
            pltpu.VMEM((PMAX, ROWS), jnp.float32),
            pltpu.VMEM((HEADS, HW), jnp.float32),
        ],
        compiler_params=PARAMS,
        cost_estimate=pl.CostEstimate(
            flops=2 * 6 * ROWS * 640 * WIDTH, bytes_accessed=10 << 20, transcendentals=1 << 20
        ),
        name="attention",
    )(starts, lens, bias, queries, cotangent, key_rows, values, low, high, prompt)


def finish_kernel(starts_ref, gk_ref, gv_ref, left_ref, right_ref, prompt_ref, outk_ref, outv_ref):
    me = lax.axis_index("ctx")
    begins, offset = own_start(starts_ref, me)
    offset = jnp.where(begins, offset, 2 * ROWS)
    frame = lax.broadcasted_iota(jnp.int32, (ROWS, PMAX), 0)
    row = lax.broadcasted_iota(jnp.int32, (ROWS, PMAX), 1)
    place = (frame == row + offset).astype(jnp.bfloat16)
    for head in range(HEADS):
        cols = columns(head)
        for part, (ref, out) in enumerate(((gk_ref, outk_ref), (gv_ref, outv_ref))):
            piece = prompt_ref[:, head, part * BAND : (part + 1) * BAND, :].reshape(PMAX, HD)
            total = ref[:, cols] + nn(place, piece)
            sides = jnp.concatenate([left_ref[part, :, cols], right_ref[part, :, cols]], axis=0)
            out[0, :, cols] = (total + sides.astype(jnp.float32)).astype(jnp.bfloat16)


def finish(starts, gk, gv, left, right, prompt):
    return pl.pallas_call(
        finish_kernel,
        out_shape=(jax.ShapeDtypeStruct((1, ROWS, WIDTH), jnp.bfloat16),) * 2,
        in_specs=[SMEM, VMEM, VMEM, VMEM, VMEM, VMEM],
        out_specs=(VMEM, VMEM),
        compiler_params=PARAMS,
        name="finish",
    )(starts, gk, gv, left, right, prompt)


def exchange(pieces):
    return lax.all_to_all(pieces, "ctx", 0, 0, tiled=True)


def shifted(x, by):
    peers = lax.axis_size("ctx")
    return lax.ppermute(x, "ctx", [(i, i + by) for i in range(peers) if 0 <= i + by < peers])


def local(queries, key_rows, values, cotangent, starts, lens, bias):
    count = lax.axis_size("ctx")
    cut = cut_prompt(starts, key_rows, values)
    held = exchange(cut.reshape(count, 2 * BAND, HD))
    low = shifted(jnp.concatenate([key_rows[:, HW:], values[:, HW:]], axis=0), 1)
    high = shifted(jnp.concatenate([key_rows[:, :HW], values[:, :HW]], axis=0), -1)
    prompt = exchange(route(starts, held)).reshape(BANDS, HEADS, 2 * BAND, HD)
    attended, grad_q, gk, gv, glow, ghigh, gprompt = attention(
        starts, lens, bias, queries, cotangent, key_rows, values, low, high, prompt
    )
    held = exchange(gprompt.reshape(count, 2 * BAND + 2 * HEADS, HD))
    right = shifted(glow, -1)
    left = shifted(ghigh, 1)
    owned, bias_sums = gather(starts, held)
    peers = lax.axis_size("dp")
    others = [
        lax.ppermute(bias_sums, "dp", [(i, i ^ step) for i in range(peers)])
        for step in range(1, peers)
    ]
    total = (bias_sums + others[0]) + (others[1] + others[2])
    grad_bias = jnp.sum(total, axis=1)
    returned = exchange(owned).reshape(BANDS, HEADS, 2 * BAND, HD)
    grad_k, grad_v = finish(starts, gk, gv, left, right, returned)
    return attended, grad_q, grad_k, grad_v, grad_bias


def solution(mesh):
    split = P("dp", "ctx", None)
    return jax.shard_map(
        local,
        mesh=mesh,
        in_specs=(split, split, split, split, P("dp", None), P("dp", None), P()),
        out_specs=(split, split, split, split, P()),
        check_vma=False,
    )
```

```python
import math

import jax
import jax.numpy as jnp
from jax import lax
from jax.experimental import pallas as pl
from jax.experimental.pallas import tpu as pltpu
from jax.sharding import PartitionSpec as P

HW = 128
PMAX = 128
ROWS = 256
HD = 128
HEADS = 8
WIDTH = HEADS * HD
BANDS = 8
BAND = PMAX // BANDS
SENT = 2 * BAND + HEADS
GROUP = 2
STAGED = 4
NEG = -1e30
LOG2E = math.log2(math.e)
SCALE = 1.0 / math.sqrt(HD)
FACTOR = SCALE * LOG2E

SMEM = pl.BlockSpec(memory_space=pltpu.SMEM)
VMEM = pl.BlockSpec(memory_space=pltpu.VMEM)
HBM = pl.BlockSpec(memory_space=pltpu.HBM)
PARAMS = pltpu.CompilerParams(vmem_limit_bytes=20 * 1024 * 1024)
FROM_HBM = pltpu.CompilerParams(vmem_limit_bytes=60 * 1024 * 1024)


def nt(a, b):
    return lax.dot_general(a, b, (((1,), (1,)), ((), ())), preferred_element_type=jnp.float32)


def tn(a, b):
    return lax.dot_general(a, b, (((0,), (0,)), ((), ())), preferred_element_type=jnp.float32)


def nn(a, b):
    return lax.dot_general(a, b, (((1,), (0,)), ((), ())), preferred_element_type=jnp.float32)


def own_start(starts_ref, me):
    start = starts_ref[0, me]
    return start >= 0, jnp.where(start >= 0, start - me * ROWS, 0)


def columns(head):
    return slice(head * HD, (head + 1) * HD)


def float_array(*shape):
    return jax.ShapeDtypeStruct(shape, jnp.float32)


def low_array(*shape):
    return jax.ShapeDtypeStruct(shape, jnp.bfloat16)


def cut_kernel(starts_ref, k_hbm, v_hbm, out_ref, last_hbm, first_hbm, k_ref, v_ref, sems, out_sems):
    me = lax.axis_index("ctx")
    offset = own_start(starts_ref, me)[1]
    halves = (slice(0, HW), slice(HW, ROWS))
    loads, stores = [], []
    for part, (source, ref) in enumerate(((k_hbm, k_ref), (v_hbm, v_ref))):
        for half, (rows, target) in enumerate(zip(halves, (first_hbm, last_hbm))):
            loads.append(
                pltpu.make_async_copy(source.at[0, rows, :], ref.at[rows, :], sems.at[part, half])
            )
            stores.append(
                pltpu.make_async_copy(ref.at[rows, :], target.at[part], out_sems.at[part, half])
            )
    for copy in loads:
        copy.start()
    row = lax.broadcasted_iota(jnp.int32, (PMAX, ROWS), 0)
    frame = lax.broadcasted_iota(jnp.int32, (PMAX, ROWS), 1)
    pick = (frame == row + offset).astype(jnp.bfloat16)
    for load, store in zip(loads, stores):
        load.wait()
        store.start()
    for head in range(HEADS):
        for part, ref in enumerate((k_ref, v_ref)):
            rows = nn(pick, ref[:, columns(head)]).astype(jnp.bfloat16)
            out_ref[:, head, part * BAND : (part + 1) * BAND, :] = rows.reshape(BANDS, BAND, HD)
    for store in stores:
        store.wait()


def cut_prompt(starts, key_rows, values):
    return pl.pallas_call(
        cut_kernel,
        out_shape=(
            low_array(BANDS, HEADS, 2 * BAND, HD),
            low_array(2, HW, WIDTH),
            low_array(2, HW, WIDTH),
        ),
        in_specs=[SMEM, HBM, HBM],
        out_specs=(VMEM, HBM, HBM),
        scratch_shapes=[
            pltpu.VMEM((ROWS, WIDTH), jnp.bfloat16),
            pltpu.VMEM((ROWS, WIDTH), jnp.bfloat16),
            pltpu.SemaphoreType.DMA((2, 2)),
            pltpu.SemaphoreType.DMA((2, 2)),
        ],
        compiler_params=FROM_HBM,
        name="cut_prompt",
    )(starts, key_rows, values)


def route_kernel(starts_ref, in_ref, out_ref):
    count = in_ref.shape[0]

    def step(target, source):
        out_ref[target] = in_ref[source]
        return jnp.where(starts_ref[0, target] >= 0, target, source)

    lax.fori_loop(0, count, step, jnp.int32(0), unroll=8)


def route(starts, pieces):
    return pl.pallas_call(
        route_kernel,
        out_shape=jax.ShapeDtypeStruct(pieces.shape, pieces.dtype),
        in_specs=[SMEM, VMEM],
        out_specs=VMEM,
        compiler_params=PARAMS,
        name="route",
    )(starts, pieces)


def gather_kernel(starts_ref, in_ref, out_ref, sums_ref):
    count = in_ref.shape[0]
    out_ref[...] = jnp.zeros_like(out_ref)

    def step(target, carry):
        source, total, sums = carry
        block = in_ref[target].astype(jnp.float32)
        total = total + block[: 2 * BAND]
        sums = sums + block[2 * BAND :]
        out_ref[source] = total.astype(jnp.bfloat16)
        begins = starts_ref[0, target] >= 0
        return jnp.where(begins, target, source), jnp.where(begins, 0.0, total), sums

    sums = in_ref[0].astype(jnp.float32)[2 * BAND :]
    carry = (jnp.int32(0), jnp.zeros((2 * BAND, HD), jnp.float32), sums)
    sums_ref[...] = lax.fori_loop(1, count, step, carry, unroll=7)[2]


def gather(starts, pieces):
    return pl.pallas_call(
        gather_kernel,
        out_shape=(low_array(pieces.shape[0], 2 * BAND, HD), float_array(HEADS, HD)),
        in_specs=[SMEM, VMEM],
        out_specs=(VMEM, VMEM),
        compiler_params=PARAMS,
        name="gather",
    )(starts, pieces)


def carried_prompt(starts_ref, lens_ref, me):
    def later(index, found):
        used = starts_ref[0, index] >= 0
        return (
            jnp.where(used, starts_ref[0, index], found[0]),
            jnp.where(used, lens_ref[0, index], found[1]),
        )

    return lax.fori_loop(0, me, later, (jnp.int32(0), jnp.int32(0)))


def grid_of(keys, rows):
    key = lax.broadcasted_iota(jnp.int32, (keys, rows), 0)
    return key, lax.broadcasted_iota(jnp.int32, (keys, rows), 1)


def hold(ref, allowed):
    ref[...] = jnp.where(allowed, 0.0, NEG)


def hold_masks(starts_ref, lens_ref, own_mask, own_flag, halo_mask, prompt_mask):
    me = lax.axis_index("ctx")
    last = starts_ref.shape[1] - 1
    begins, offset = own_start(starts_ref, me)
    offset = jnp.where(begins, offset, ROWS)
    own_len = jnp.where(begins, lens_ref[0, me], 0)
    key, row = grid_of(ROWS, ROWS)
    prompt = (key >= offset) & (key < offset + own_len)
    near = jnp.abs(row - key) <= HW
    hold(own_mask, ((row >= offset) == (key >= offset)) & (prompt | near))
    own_flag[...] = prompt.astype(jnp.float32)
    start, length = carried_prompt(starts_ref, lens_ref, me)
    prompt_end = start + length - (me * ROWS - HW)
    next_begins, next_offset = own_start(starts_ref, jnp.minimum(me + 1, last))
    next_offset = jnp.where(next_begins, next_offset, HW)
    next_offset = jnp.where(me < last, next_offset, 0)
    key, row = grid_of(HW, HW)
    hold(halo_mask.at[0], (key >= row) & (row < offset) & (key >= prompt_end) & (me > 0))
    hold(halo_mask.at[1], (key <= row) & (key < next_offset))
    key, row = grid_of(PMAX, ROWS)
    hold(prompt_mask, (row < offset) & (key < length))


def top_of(x):
    return jnp.max(x, axis=0, keepdims=True)


def sum_of(x):
    return jnp.sum(x, axis=0, keepdims=True)


def window_kernel(
    starts_ref,
    lens_ref,
    bias_ref,
    q_ref,
    d_ref,
    k_ref,
    v_ref,
    low_ref,
    high_ref,
    stats_ref,
    own_mask,
    own_flag,
    halo_mask,
    prompt_mask,
):
    head = pl.program_id(0)

    @pl.when(head == 0)
    def _():
        hold_masks(starts_ref, lens_ref, own_mask, own_flag, halo_mask, prompt_mask)

    q, d, k, v = q_ref[0], d_ref[0], k_ref[0], v_ref[0]
    bias = bias_ref[head] * LOG2E
    flag = own_flag[...]
    x_own = nt(k, q) * FACTOR + (own_mask[...] + flag * bias)
    x_low = nt(low_ref[0], q[:HW]) * FACTOR + halo_mask[0]
    x_high = nt(high_ref[0], q[HW:]) * FACTOR + halo_mask[1]
    tops = jnp.concatenate([top_of(x_low), top_of(x_high)], axis=1)
    top = jnp.maximum(top_of(x_own), tops)
    e_own = jnp.exp2(x_own - top)
    e_low = jnp.exp2(x_low - top[:, :HW])
    e_high = jnp.exp2(x_high - top[:, HW:])
    w_own = e_own * nt(v, d)
    w_low = e_low * nt(low_ref[1], d[:HW])
    w_high = e_high * nt(high_ref[1], d[HW:])
    total = sum_of(e_own) + jnp.concatenate([sum_of(e_low), sum_of(e_high)], axis=1)
    weighted = sum_of(w_own) + jnp.concatenate([sum_of(w_low), sum_of(w_high)], axis=1)
    inverse = 1.0 / total
    own_bias = (sum_of(w_own * flag) - weighted * inverse * sum_of(e_own * flag)) * inverse
    stats_ref[0] = jnp.concatenate(
        [top, total, weighted, own_bias, jnp.zeros((4, ROWS), jnp.float32)], axis=0
    )


def head_rows(part=ROWS):
    return pl.BlockSpec((1, part, HD), lambda head: (0, 0, head))


def head_halo():
    return pl.BlockSpec((2, HW, HD), lambda head: (0, 0, head))


def head_tile(*shape):
    return pl.BlockSpec((1, *shape), lambda head: (head,) + (0,) * len(shape))


def head_pieces():
    return pl.BlockSpec((BANDS, 1, 2 * BAND, HD), lambda head: (0, head, 0, 0))


MASKS = (
    float_array(ROWS, ROWS),
    float_array(ROWS, ROWS),
    float_array(2, HW, HW),
    float_array(PMAX, ROWS),
)


def whole(array):
    return pl.BlockSpec(array.shape, lambda head: (0,) * len(array.shape))


def cost(micros):
    return pl.CostEstimate(flops=micros * 10**9, bytes_accessed=8 << 20, transcendentals=0)


def window(starts, lens, bias, queries, cotangent, key_rows, values, low, high):
    rows = head_rows()
    return pl.pallas_call(
        window_kernel,
        grid=(HEADS,),
        out_shape=(float_array(HEADS, 8, ROWS), *MASKS),
        in_specs=[SMEM, SMEM, SMEM, rows, rows, rows, rows, head_halo(), head_halo()],
        out_specs=(head_tile(8, ROWS), *(whole(mask) for mask in MASKS)),
        compiler_params=PARAMS,
        cost_estimate=cost(20),
        name="window",
    )(starts, lens, bias, queries, cotangent, key_rows, values, low, high)


def prompt_kernel(
    bias_ref, q_ref, d_ref, prompt_ref, stats_ref, mask_ref, grad_ref, final_ref
):
    mask = mask_ref[...]
    all_sums = []
    for first in range(0, HEADS, STAGED):
        heads = range(first, first + STAGED)
        rows = [(q_ref[0, :, columns(head)], d_ref[0, :, columns(head)]) for head in heads]
        products = []
        for head, (q, d) in zip(heads, rows):
            kp = prompt_ref[:, head, :BAND, :].reshape(PMAX, HD)
            vp = prompt_ref[:, head, BAND:, :].reshape(PMAX, HD)
            products.append((nt(kp, q), nt(vp, d)))
        settled_rows = []
        for head, (scores, dprobs) in zip(heads, products):
            x = scores * FACTOR + (mask + bias_ref[head] * LOG2E)
            stats = stats_ref[head]
            top = jnp.maximum(stats[0:1], top_of(x))
            rescale = jnp.exp2(stats[0:1] - top)
            raised = jnp.exp2(x - top)
            inverse = 1.0 / (stats[1:2] * rescale + sum_of(raised))
            delta = (stats[2:3] * rescale + sum_of(raised * dprobs)) * inverse
            probs = raised * inverse
            dscores = (probs * SCALE) * (dprobs - delta)
            settled_rows.append((probs.astype(jnp.bfloat16), dscores.astype(jnp.bfloat16)))
            final_ref[head] = jnp.concatenate(
                [top, inverse, delta, jnp.zeros((5, ROWS), jnp.float32)], axis=0
            )
            sums = stats[3:4] + sum_of(dscores) * (1.0 / SCALE)
            all_sums.append(sums[:, :HW] + sums[:, HW:])
        grads = [
            (nn(low_ds, q).astype(jnp.bfloat16), nn(low_probs, d).astype(jnp.bfloat16))
            for (q, d), (low_probs, low_ds) in zip(rows, settled_rows)
        ]
        for head, (gk, gv) in zip(heads, grads):
            grad_ref[:, head, :BAND, :] = gk.reshape(BANDS, BAND, HD)
            grad_ref[:, head, BAND : 2 * BAND, :] = gv.reshape(BANDS, BAND, HD)

    sums = jnp.concatenate(all_sums, axis=0)
    sums = sums + pltpu.roll(sums, HW // 2, 1)
    upper = sums.astype(jnp.bfloat16).astype(jnp.float32)
    lane = lax.broadcasted_iota(jnp.int32, (HEADS, HW), 1)
    tile = jnp.where(lane < HW // 2, upper, sums - upper).astype(jnp.bfloat16)
    for band in range(BANDS):
        for head in range(HEADS):
            grad_ref[band, head, 2 * BAND :, :] = tile


def prompt_part(bias, queries, cotangent, prompt, stats, prompt_mask):
    return pl.pallas_call(
        prompt_kernel,
        out_shape=(low_array(BANDS, HEADS, SENT, HD), float_array(HEADS, 8, ROWS)),
        in_specs=[SMEM, VMEM, VMEM, VMEM, VMEM, VMEM],
        out_specs=(VMEM,) * 2,
        compiler_params=PARAMS,
        cost_estimate=cost(4),
        name="prompt_part",
    )(bias, queries, cotangent, prompt, stats, prompt_mask)


def settled(keys, values, q, d, added, final):
    x = nt(keys, q) * FACTOR + added
    probs = jnp.exp2(x - final[0:1]) * final[1:2]
    dscores = (probs * SCALE) * (nt(values, d) - final[2:3])
    return probs.astype(jnp.bfloat16), dscores.astype(jnp.bfloat16)


def halo_kernel(q_ref, d_ref, low_ref, high_ref, final_ref, mask_ref, glow_ref, ghigh_ref):
    for head in range(HEADS):
        cols = columns(head)
        for half, (ref, out) in enumerate(((low_ref, glow_ref), (high_ref, ghigh_ref))):
            part = slice(half * HW, (half + 1) * HW)
            q, d = q_ref[0, part, cols], d_ref[0, part, cols]
            final = final_ref[head, :, part]
            probs, ds = settled(ref[0, :, cols], ref[1, :, cols], q, d, mask_ref[half], final)
            out[0, :, cols] = nn(ds, q).astype(jnp.bfloat16)
            out[1, :, cols] = nn(probs, d).astype(jnp.bfloat16)


def halo_grads(queries, cotangent, low, high, final, halo_mask):
    return pl.pallas_call(
        halo_kernel,
        out_shape=(low_array(2, HW, WIDTH), low_array(2, HW, WIDTH)),
        in_specs=[VMEM] * 6,
        out_specs=(VMEM, VMEM),
        compiler_params=PARAMS,
        cost_estimate=cost(4),
        name="halo_grads",
    )(queries, cotangent, low, high, final, halo_mask)


def row_kernel(
    bias_ref,
    q_ref,
    d_ref,
    k_ref,
    v_ref,
    low_ref,
    high_ref,
    prompt_ref,
    final_ref,
    own_mask,
    own_flag,
    halo_mask,
    prompt_mask,
    attended_ref,
    gq_ref,
):
    bias = bias_ref[pl.program_id(0)] * LOG2E
    q, d, k, v = q_ref[0], d_ref[0], k_ref[0], v_ref[0]
    kp = prompt_ref[:, 0, :BAND, :].reshape(PMAX, HD)
    vp = prompt_ref[:, 0, BAND:, :].reshape(PMAX, HD)
    final = final_ref[0]
    probs, ds = settled(k, v, q, d, own_mask[...] + own_flag[...] * bias, final)
    prompt_probs, prompt_ds = settled(kp, vp, q, d, prompt_mask[...] + bias, final)
    attended = tn(probs, v) + tn(prompt_probs, vp)
    grad_q = tn(ds, k) + tn(prompt_ds, kp)
    for half, ref in enumerate((low_ref, high_ref)):
        part = slice(half * HW, (half + 1) * HW)
        probs, ds = settled(ref[0], ref[1], q[part], d[part], halo_mask[half], final[:, part])
        attended_ref[0, part, :] = (attended[part] + tn(probs, ref[1])).astype(jnp.bfloat16)
        gq_ref[0, part, :] = (grad_q[part] + tn(ds, ref[0])).astype(jnp.bfloat16)


def row_part(bias, queries, cotangent, key_rows, values, low, high, prompt, final, masks):
    rows, halo = head_rows(), head_halo()
    return pl.pallas_call(
        row_kernel,
        grid=(HEADS,),
        out_shape=(low_array(1, ROWS, WIDTH), low_array(1, ROWS, WIDTH)),
        in_specs=[SMEM, rows, rows, rows, rows, halo, halo, head_pieces(), head_tile(8, ROWS)]
        + [whole(mask) for mask in MASKS],
        out_specs=(rows, rows),
        compiler_params=PARAMS,
        cost_estimate=cost(10),
        name="row_part",
    )(bias, queries, cotangent, key_rows, values, low, high, prompt, final, *masks)


def own_kernel(
    bias_ref,
    q_ref,
    d_ref,
    k_ref,
    v_ref,
    final_ref,
    own_mask,
    own_flag,
    left_ref,
    right_ref,
    gk_ref,
    gv_ref,
):
    q, d = q_ref[0], d_ref[0]
    added = own_mask[...] + own_flag[...] * (bias_ref[pl.program_id(0)] * LOG2E)
    probs, ds = settled(k_ref[0], v_ref[0], q, d, added, final_ref[0])
    for part, (ref, total) in enumerate(((gk_ref, nn(ds, q)), (gv_ref, nn(probs, d)))):
        sides = jnp.concatenate([left_ref[part], right_ref[part]], axis=0)
        ref[...] = total + sides.astype(jnp.float32)


def own_part(bias, queries, cotangent, key_rows, values, final, masks, left, right):
    rows, halo = head_rows(), head_halo()
    total = pl.BlockSpec((ROWS, HD), lambda head: (0, head))
    return pl.pallas_call(
        own_kernel,
        grid=(HEADS,),
        out_shape=(float_array(ROWS, WIDTH), float_array(ROWS, WIDTH)),
        in_specs=[SMEM, rows, rows, rows, rows, head_tile(8, ROWS)]
        + [whole(mask) for mask in MASKS[:2]]
        + [halo, halo],
        out_specs=(total, total),
        compiler_params=FROM_HBM,
        cost_estimate=cost(20),
        name="own_part",
    )(bias, queries, cotangent, key_rows, values, final, *masks[:2], left, right)


def finish_kernel(starts_ref, gk_ref, gv_ref, prompt_ref, outk_ref, outv_ref):
    me = lax.axis_index("ctx")
    begins, offset = own_start(starts_ref, me)
    offset = jnp.where(begins, offset, 2 * ROWS)
    frame = lax.broadcasted_iota(jnp.int32, (ROWS, PMAX), 0)
    row = lax.broadcasted_iota(jnp.int32, (ROWS, PMAX), 1)
    place = (frame == row + offset).astype(jnp.bfloat16)
    for member in range(GROUP):
        cols = columns(member)
        for part, (ref, out) in enumerate(((gk_ref, outk_ref), (gv_ref, outv_ref))):
            piece = prompt_ref[:, member, part * BAND : (part + 1) * BAND, :].reshape(PMAX, HD)
            out[0, :, cols] = (ref[:, cols] + nn(place, piece)).astype(jnp.bfloat16)


def finish(starts, gk, gv, prompt):
    total = pl.BlockSpec((ROWS, GROUP * HD), lambda step: (0, step))
    rows = pl.BlockSpec((1, ROWS, GROUP * HD), lambda step: (0, 0, step))
    pieces = pl.BlockSpec((BANDS, GROUP, 2 * BAND, HD), lambda step: (0, step, 0, 0))
    return pl.pallas_call(
        finish_kernel,
        grid=(HEADS // GROUP,),
        out_shape=(low_array(1, ROWS, WIDTH),) * 2,
        in_specs=[SMEM, total, total, pieces],
        out_specs=(rows, rows),
        compiler_params=FROM_HBM,
        name="finish",
    )(starts, gk, gv, prompt)


def exchange(pieces):
    return lax.all_to_all(pieces, "ctx", 0, 0, tiled=True)


def shifted(x, by):
    peers = lax.axis_size("ctx")
    return lax.ppermute(x, "ctx", [(i, i + by) for i in range(peers) if 0 <= i + by < peers])


def partners(x, axis, steps):
    peers = lax.axis_size(axis)
    return [lax.ppermute(x, axis, [(i, i ^ step) for i in range(peers)]) for step in steps]


def summed(x, axis, low, high):
    first, second, third = partners(x, axis, (low, high, low | high))
    return (x + first) + (second + third)


def local(queries, key_rows, values, cotangent, starts, lens, bias):
    count = lax.axis_size("ctx")
    cut, last, first = cut_prompt(starts, key_rows, values)
    held = exchange(cut.reshape(count, 2 * BAND, HD))
    low = shifted(last, 1)
    high = shifted(first, -1)
    stats, *masks = window(
        starts, lens, bias, queries, cotangent, key_rows, values, low, high
    )
    held, stats = lax.optimization_barrier((held, stats))
    prompt = exchange(route(starts, held)).reshape(BANDS, HEADS, 2 * BAND, HD)
    gprompt, final = prompt_part(bias, queries, cotangent, prompt, stats, masks[3])
    held = exchange(gprompt.reshape(count, SENT, HD))
    attended, grad_q = row_part(
        bias, queries, cotangent, key_rows, values, low, high, prompt, final, masks
    )
    final, grad_q = lax.optimization_barrier((final, grad_q))
    glow, ghigh = halo_grads(queries, cotangent, low, high, final, masks[2])
    right = shifted(glow, -1)
    left = shifted(ghigh, 1)
    held, final, glow, ghigh = lax.optimization_barrier((held, final, glow, ghigh))
    owned, sums = gather(starts, held)
    returned = exchange(owned).reshape(BANDS, HEADS, 2 * BAND, HD)
    gk, gv = own_part(bias, queries, cotangent, key_rows, values, final, masks, left, right)
    sums, gk = lax.optimization_barrier((sums, gk))
    grad_bias = jnp.sum(summed(sums, "dp", 1, 2), axis=1)
    grad_k, grad_v = finish(starts, gk, gv, returned)
    return attended, grad_q, grad_k, grad_v, grad_bias


def solution(mesh):
    split = P("dp", "ctx", None)
    return jax.shard_map(
        local,
        mesh=mesh,
        in_specs=(split, split, split, split, P("dp", None), P("dp", None), P()),
        out_specs=(split, split, split, split, P()),
        check_vma=False,
    )
```

```python
import math

import jax
import jax.numpy as jnp
from jax import lax
from jax.experimental import pallas as pl
from jax.experimental.pallas import tpu as pltpu
from jax.sharding import PartitionSpec as P

HW = 128
PMAX = 128
ROWS = 256
HD = 128
HEADS = 8
WIDTH = HEADS * HD
BANDS = 8
BAND = PMAX // BANDS
SENT = 2 * BAND + HEADS
SPAN = PMAX + BAND
GROUP = 2
STAGED = 4
NEG = -1e30
LOG2E = math.log2(math.e)
SCALE = 1.0 / math.sqrt(HD)
FACTOR = SCALE * LOG2E

SMEM = pl.BlockSpec(memory_space=pltpu.SMEM)
VMEM = pl.BlockSpec(memory_space=pltpu.VMEM)
HBM = pl.BlockSpec(memory_space=pltpu.HBM)
PARAMS = pltpu.CompilerParams(vmem_limit_bytes=20 * 1024 * 1024)
FROM_HBM = pltpu.CompilerParams(vmem_limit_bytes=60 * 1024 * 1024)


def nt(a, b):
    return lax.dot_general(a, b, (((1,), (1,)), ((), ())), preferred_element_type=jnp.float32)


def tn(a, b):
    return lax.dot_general(a, b, (((0,), (0,)), ((), ())), preferred_element_type=jnp.float32)


def nn(a, b):
    return lax.dot_general(a, b, (((1,), (0,)), ((), ())), preferred_element_type=jnp.float32)


def own_start(starts_ref, me):
    start = starts_ref[0, me]
    return start >= 0, jnp.where(start >= 0, start - me * ROWS, 0)


def columns(head):
    return slice(head * HD, (head + 1) * HD)


def float_array(*shape):
    return jax.ShapeDtypeStruct(shape, jnp.float32)


def low_array(*shape):
    return jax.ShapeDtypeStruct(shape, jnp.bfloat16)


def cut_kernel(starts_ref, k_hbm, v_hbm, out_ref, last_hbm, first_hbm, k_ref, v_ref, sems, out_sems):
    me = lax.axis_index("ctx")
    offset = own_start(starts_ref, me)[1]
    halves = (slice(0, HW), slice(HW, ROWS))
    loads, stores = [], []
    for part, (source, ref) in enumerate(((k_hbm, k_ref), (v_hbm, v_ref))):
        for half, (rows, target) in enumerate(zip(halves, (first_hbm, last_hbm))):
            loads.append(
                pltpu.make_async_copy(source.at[0, rows, :], ref.at[rows, :], sems.at[part, half])
            )
            stores.append(
                pltpu.make_async_copy(ref.at[rows, :], target.at[part], out_sems.at[part, half])
            )
    for copy in loads:
        copy.start()
    row = lax.broadcasted_iota(jnp.int32, (PMAX, ROWS), 0)
    frame = lax.broadcasted_iota(jnp.int32, (PMAX, ROWS), 1)
    pick = (frame == row + offset).astype(jnp.bfloat16)
    for load, store in zip(loads, stores):
        load.wait()
        store.start()
    for head in range(HEADS):
        for part, ref in enumerate((k_ref, v_ref)):
            rows = nn(pick, ref[:, columns(head)]).astype(jnp.bfloat16)
            out_ref[:, head, part * BAND : (part + 1) * BAND, :] = rows.reshape(BANDS, BAND, HD)
    for store in stores:
        store.wait()


def cut_prompt(starts, key_rows, values):
    return pl.pallas_call(
        cut_kernel,
        out_shape=(
            low_array(BANDS, HEADS, 2 * BAND, HD),
            low_array(2, HW, WIDTH),
            low_array(2, HW, WIDTH),
        ),
        in_specs=[SMEM, HBM, HBM],
        out_specs=(VMEM, HBM, HBM),
        scratch_shapes=[
            pltpu.VMEM((ROWS, WIDTH), jnp.bfloat16),
            pltpu.VMEM((ROWS, WIDTH), jnp.bfloat16),
            pltpu.SemaphoreType.DMA((2, 2)),
            pltpu.SemaphoreType.DMA((2, 2)),
        ],
        compiler_params=FROM_HBM,
        name="cut_prompt",
    )(starts, key_rows, values)


def route_kernel(starts_ref, in_ref, out_ref):
    count = in_ref.shape[0]

    def step(target, source):
        out_ref[target] = in_ref[source]
        return jnp.where(starts_ref[0, target] >= 0, target, source)

    lax.fori_loop(0, count, step, jnp.int32(0), unroll=8)


def route(starts, pieces):
    return pl.pallas_call(
        route_kernel,
        out_shape=jax.ShapeDtypeStruct(pieces.shape, pieces.dtype),
        in_specs=[SMEM, VMEM],
        out_specs=VMEM,
        compiler_params=PARAMS,
        name="route",
    )(starts, pieces)


def gather_kernel(starts_ref, in_ref, out_ref, sums_ref):
    count = in_ref.shape[0]
    out_ref[...] = jnp.zeros_like(out_ref)

    def step(target, carry):
        source, total, sums = carry
        block = in_ref[target].astype(jnp.float32)
        total = total + block[: 2 * BAND]
        sums = sums + block[2 * BAND :]
        out_ref[source] = total.astype(jnp.bfloat16)
        begins = starts_ref[0, target] >= 0
        return jnp.where(begins, target, source), jnp.where(begins, 0.0, total), sums

    sums = in_ref[0].astype(jnp.float32)[2 * BAND :]
    carry = (jnp.int32(0), jnp.zeros((2 * BAND, HD), jnp.float32), sums)
    sums_ref[...] = lax.fori_loop(1, count, step, carry, unroll=7)[2]


def gather(starts, pieces):
    return pl.pallas_call(
        gather_kernel,
        out_shape=(low_array(pieces.shape[0], 2 * BAND, HD), float_array(HEADS, HD)),
        in_specs=[SMEM, VMEM],
        out_specs=(VMEM, VMEM),
        compiler_params=PARAMS,
        name="gather",
    )(starts, pieces)


def carried_prompt(starts_ref, lens_ref, me):
    def later(index, found):
        used = starts_ref[0, index] >= 0
        return (
            jnp.where(used, starts_ref[0, index], found[0]),
            jnp.where(used, lens_ref[0, index], found[1]),
        )

    return lax.fori_loop(0, me, later, (jnp.int32(0), jnp.int32(0)))


def grid_of(keys, rows):
    key = lax.broadcasted_iota(jnp.int32, (keys, rows), 0)
    return key, lax.broadcasted_iota(jnp.int32, (keys, rows), 1)


def hold(ref, allowed):
    ref[...] = jnp.where(allowed, 0.0, NEG)


def hold_masks(starts_ref, lens_ref, own_mask, own_flag, halo_mask, prompt_mask):
    me = lax.axis_index("ctx")
    last = starts_ref.shape[1] - 1
    begins, offset = own_start(starts_ref, me)
    offset = jnp.where(begins, offset, ROWS)
    own_len = jnp.where(begins, lens_ref[0, me], 0)
    key, row = grid_of(ROWS, ROWS)
    prompt = (key >= offset) & (key < offset + own_len)
    near = jnp.abs(row - key) <= HW
    hold(own_mask, ((row >= offset) == (key >= offset)) & (prompt | near))
    own_flag[...] = prompt.astype(jnp.float32)
    start, length = carried_prompt(starts_ref, lens_ref, me)
    prompt_end = start + length - (me * ROWS - HW)
    next_begins, next_offset = own_start(starts_ref, jnp.minimum(me + 1, last))
    next_offset = jnp.where(next_begins, next_offset, HW)
    next_offset = jnp.where(me < last, next_offset, 0)
    key, row = grid_of(HW, HW)
    hold(halo_mask.at[0], (key >= row) & (row < offset) & (key >= prompt_end) & (me > 0))
    hold(halo_mask.at[1], (key <= row) & (key < next_offset))
    key, row = grid_of(PMAX, ROWS)
    hold(prompt_mask, (row < offset) & (key < length))


def top_of(x):
    return jnp.max(x, axis=0, keepdims=True)


def sum_of(x):
    return jnp.sum(x, axis=0, keepdims=True)


def window_kernel(
    starts_ref,
    lens_ref,
    bias_ref,
    q_ref,
    d_ref,
    k_ref,
    v_ref,
    low_ref,
    high_ref,
    stats_ref,
    own_mask,
    own_flag,
    halo_mask,
    prompt_mask,
):
    head = pl.program_id(0)

    @pl.when(head == 0)
    def _():
        hold_masks(starts_ref, lens_ref, own_mask, own_flag, halo_mask, prompt_mask)

    q, d, k, v = q_ref[0], d_ref[0], k_ref[0], v_ref[0]
    bias = bias_ref[head] * LOG2E
    flag = own_flag[...]
    x_own = nt(k, q) * FACTOR + (own_mask[...] + flag * bias)
    x_low = nt(low_ref[0], q[:HW]) * FACTOR + halo_mask[0]
    x_high = nt(high_ref[0], q[HW:]) * FACTOR + halo_mask[1]
    tops = jnp.concatenate([top_of(x_low), top_of(x_high)], axis=1)
    top = jnp.maximum(top_of(x_own), tops)
    e_own = jnp.exp2(x_own - top)
    e_low = jnp.exp2(x_low - top[:, :HW])
    e_high = jnp.exp2(x_high - top[:, HW:])
    w_own = e_own * nt(v, d)
    w_low = e_low * nt(low_ref[1], d[:HW])
    w_high = e_high * nt(high_ref[1], d[HW:])
    total = sum_of(e_own) + jnp.concatenate([sum_of(e_low), sum_of(e_high)], axis=1)
    weighted = sum_of(w_own) + jnp.concatenate([sum_of(w_low), sum_of(w_high)], axis=1)
    inverse = 1.0 / total
    own_bias = (sum_of(w_own * flag) - weighted * inverse * sum_of(e_own * flag)) * inverse
    stats_ref[0] = jnp.concatenate(
        [top, total, weighted, own_bias, jnp.zeros((4, ROWS), jnp.float32)], axis=0
    )


def head_rows(part=ROWS):
    return pl.BlockSpec((1, part, HD), lambda head: (0, 0, head))


def head_halo():
    return pl.BlockSpec((2, HW, HD), lambda head: (0, 0, head))


def head_tile(*shape):
    return pl.BlockSpec((1, *shape), lambda head: (head,) + (0,) * len(shape))


def head_pieces():
    return pl.BlockSpec((BANDS, 1, 2 * BAND, HD), lambda head: (0, head, 0, 0))


MASKS = (
    float_array(ROWS, ROWS),
    float_array(ROWS, ROWS),
    float_array(2, HW, HW),
    float_array(PMAX, ROWS),
)


def whole(array):
    return pl.BlockSpec(array.shape, lambda head: (0,) * len(array.shape))


def cost(micros):
    return pl.CostEstimate(flops=micros * 10**9, bytes_accessed=8 << 20, transcendentals=0)


def window(starts, lens, bias, queries, cotangent, key_rows, values, low, high):
    rows = head_rows()
    return pl.pallas_call(
        window_kernel,
        grid=(HEADS,),
        out_shape=(float_array(HEADS, 8, ROWS), *MASKS),
        in_specs=[SMEM, SMEM, SMEM, rows, rows, rows, rows, head_halo(), head_halo()],
        out_specs=(head_tile(8, ROWS), *(whole(mask) for mask in MASKS)),
        compiler_params=PARAMS,
        cost_estimate=cost(20),
        name="window",
    )(starts, lens, bias, queries, cotangent, key_rows, values, low, high)


def prompt_kernel(
    bias_ref, q_ref, d_ref, prompt_ref, stats_ref, mask_ref, grad_ref, final_ref
):
    mask = mask_ref[...]
    all_sums = []
    for first in range(0, HEADS, STAGED):
        heads = range(first, first + STAGED)
        rows = [(q_ref[0, :, columns(head)], d_ref[0, :, columns(head)]) for head in heads]
        products = []
        for head, (q, d) in zip(heads, rows):
            kp = prompt_ref[:, head, :BAND, :].reshape(PMAX, HD)
            vp = prompt_ref[:, head, BAND:, :].reshape(PMAX, HD)
            products.append((nt(kp, q), nt(vp, d)))
        settled_rows = []
        for head, (scores, dprobs) in zip(heads, products):
            x = scores * FACTOR + (mask + bias_ref[head] * LOG2E)
            stats = stats_ref[head]
            top = jnp.maximum(stats[0:1], top_of(x))
            rescale = jnp.exp2(stats[0:1] - top)
            raised = jnp.exp2(x - top)
            inverse = 1.0 / (stats[1:2] * rescale + sum_of(raised))
            delta = (stats[2:3] * rescale + sum_of(raised * dprobs)) * inverse
            probs = raised * inverse
            dscores = (probs * SCALE) * (dprobs - delta)
            settled_rows.append((probs.astype(jnp.bfloat16), dscores.astype(jnp.bfloat16)))
            final_ref[head] = jnp.concatenate(
                [top, inverse, delta, jnp.zeros((5, ROWS), jnp.float32)], axis=0
            )
            sums = stats[3:4] + sum_of(dscores) * (1.0 / SCALE)
            all_sums.append(sums[:, :HW] + sums[:, HW:])
        grads = [
            (nn(low_ds, q).astype(jnp.bfloat16), nn(low_probs, d).astype(jnp.bfloat16))
            for (q, d), (low_probs, low_ds) in zip(rows, settled_rows)
        ]
        for head, (gk, gv) in zip(heads, grads):
            grad_ref[:, head, :BAND, :] = gk.reshape(BANDS, BAND, HD)
            grad_ref[:, head, BAND : 2 * BAND, :] = gv.reshape(BANDS, BAND, HD)

    sums = jnp.concatenate(all_sums, axis=0)
    sums = sums + pltpu.roll(sums, HW // 2, 1)
    upper = sums.astype(jnp.bfloat16).astype(jnp.float32)
    lane = lax.broadcasted_iota(jnp.int32, (HEADS, HW), 1)
    tile = jnp.where(lane < HW // 2, upper, sums - upper).astype(jnp.bfloat16)
    for band in range(BANDS):
        for head in range(HEADS):
            grad_ref[band, head, 2 * BAND :, :] = tile


def prompt_part(bias, queries, cotangent, prompt, stats, prompt_mask):
    return pl.pallas_call(
        prompt_kernel,
        out_shape=(low_array(BANDS, HEADS, SENT, HD), float_array(HEADS, 8, ROWS)),
        in_specs=[SMEM, VMEM, VMEM, VMEM, VMEM, VMEM],
        out_specs=(VMEM,) * 2,
        compiler_params=PARAMS,
        cost_estimate=cost(4),
        name="prompt_part",
    )(bias, queries, cotangent, prompt, stats, prompt_mask)


def settled(keys, values, q, d, added, final):
    x = nt(keys, q) * FACTOR + added
    probs = jnp.exp2(x - final[0:1]) * final[1:2]
    dscores = (probs * SCALE) * (nt(values, d) - final[2:3])
    return probs.astype(jnp.bfloat16), dscores.astype(jnp.bfloat16)


def halo_kernel(q_ref, d_ref, low_ref, high_ref, final_ref, mask_ref, glow_ref, ghigh_ref):
    for head in range(HEADS):
        cols = columns(head)
        for half, (ref, out) in enumerate(((low_ref, glow_ref), (high_ref, ghigh_ref))):
            part = slice(half * HW, (half + 1) * HW)
            q, d = q_ref[0, part, cols], d_ref[0, part, cols]
            final = final_ref[head, :, part]
            probs, ds = settled(ref[0, :, cols], ref[1, :, cols], q, d, mask_ref[half], final)
            out[0, :, cols] = nn(ds, q).astype(jnp.bfloat16)
            out[1, :, cols] = nn(probs, d).astype(jnp.bfloat16)


def halo_grads(queries, cotangent, low, high, final, halo_mask):
    return pl.pallas_call(
        halo_kernel,
        out_shape=(low_array(2, HW, WIDTH), low_array(2, HW, WIDTH)),
        in_specs=[VMEM] * 6,
        out_specs=(VMEM, VMEM),
        compiler_params=PARAMS,
        cost_estimate=cost(4),
        name="halo_grads",
    )(queries, cotangent, low, high, final, halo_mask)


def own_kernel(
    bias_ref,
    q_ref,
    d_ref,
    k_ref,
    v_ref,
    low_ref,
    high_ref,
    prompt_ref,
    final_ref,
    own_mask,
    own_flag,
    halo_mask,
    prompt_mask,
    attended_ref,
    gq_ref,
    gk_ref,
    gv_ref,
):
    bias = bias_ref[pl.program_id(0)] * LOG2E
    q, d, k, v = q_ref[0], d_ref[0], k_ref[0], v_ref[0]
    kp = prompt_ref[:, 0, :BAND, :].reshape(PMAX, HD)
    vp = prompt_ref[:, 0, BAND:, :].reshape(PMAX, HD)
    final = final_ref[0]
    probs, ds = settled(k, v, q, d, own_mask[...] + own_flag[...] * bias, final)
    prompt_probs, prompt_ds = settled(kp, vp, q, d, prompt_mask[...] + bias, final)
    gk_ref[...] = nn(ds, q)
    gv_ref[...] = nn(probs, d)
    attended = tn(probs, v) + tn(prompt_probs, vp)
    grad_q = tn(ds, k) + tn(prompt_ds, kp)
    for half, ref in enumerate((low_ref, high_ref)):
        part = slice(half * HW, (half + 1) * HW)
        probs, ds = settled(ref[0], ref[1], q[part], d[part], halo_mask[half], final[:, part])
        attended_ref[0, part, :] = (attended[part] + tn(probs, ref[1])).astype(jnp.bfloat16)
        gq_ref[0, part, :] = (grad_q[part] + tn(ds, ref[0])).astype(jnp.bfloat16)


def own_part(bias, queries, cotangent, key_rows, values, low, high, prompt, final, masks):
    rows, halo = head_rows(), head_halo()
    total = pl.BlockSpec((ROWS, HD), lambda head: (0, head))
    return pl.pallas_call(
        own_kernel,
        grid=(HEADS,),
        out_shape=(
            low_array(1, ROWS, WIDTH),
            low_array(1, ROWS, WIDTH),
            float_array(ROWS, WIDTH),
            float_array(ROWS, WIDTH),
        ),
        in_specs=[SMEM, rows, rows, rows, rows, halo, halo, head_pieces(), head_tile(8, ROWS)]
        + [whole(mask) for mask in MASKS],
        out_specs=(rows, rows, total, total),
        compiler_params=FROM_HBM,
        cost_estimate=cost(10),
        name="own_part",
    )(bias, queries, cotangent, key_rows, values, low, high, prompt, final, *masks)


def merge_kernel(gk_ref, gv_ref, left_ref, right_ref, outk_ref, outv_ref, sumk_ref, sumv_ref):
    terms = ((gk_ref, outk_ref, sumk_ref), (gv_ref, outv_ref, sumv_ref))
    for part, (ref, out, sums) in enumerate(terms):
        for half, side in enumerate((left_ref, right_ref)):
            rows = slice(half * HW, (half + 1) * HW)
            total = ref[rows, :] + side[part].astype(jnp.float32)
            sums[rows, :] = total
            out[0, rows, :] = total.astype(jnp.bfloat16)


def merge(gk, gv, left, right):
    total = pl.BlockSpec((ROWS, GROUP * HD), lambda step: (0, step))
    rows = pl.BlockSpec((1, ROWS, GROUP * HD), lambda step: (0, 0, step))
    side = pl.BlockSpec((2, HW, GROUP * HD), lambda step: (0, 0, step))
    return pl.pallas_call(
        merge_kernel,
        grid=(HEADS // GROUP,),
        out_shape=(low_array(1, ROWS, WIDTH),) * 2 + (float_array(ROWS, WIDTH),) * 2,
        in_specs=[total, total, side, side],
        out_specs=(rows, rows, total, total),
        compiler_params=FROM_HBM,
        cost_estimate=cost(20),
        name="merge",
    )(gk, gv, left, right)


def finish_kernel(
    starts_ref,
    sumk_hbm,
    sumv_hbm,
    prompt_ref,
    _ink,
    _inv,
    outk_hbm,
    outv_hbm,
    sums_ref,
    rows_ref,
    load_sems,
    store_sems,
):
    me = lax.axis_index("ctx")
    begins, offset = own_start(starts_ref, me)

    @pl.when(begins)
    def _():
        base = pl.multiple_of(jnp.minimum(offset // BAND * BAND, ROWS - SPAN), BAND)
        span = pl.ds(base, SPAN)
        loads = [
            pltpu.make_async_copy(ref.at[span, :], sums_ref.at[part], load_sems.at[part])
            for part, ref in enumerate((sumk_hbm, sumv_hbm))
        ]
        stores = [
            pltpu.make_async_copy(rows_ref.at[part], ref.at[0, span, :], store_sems.at[part])
            for part, ref in enumerate((outk_hbm, outv_hbm))
        ]
        for copy in loads:
            copy.start()
        frame, row = grid_of(SPAN, PMAX)
        place = (frame == row + (offset - base)).astype(jnp.bfloat16)
        for part in range(2):
            loads[part].wait()
            for head in range(HEADS):
                cols = columns(head)
                piece = prompt_ref[:, head, part * BAND : (part + 1) * BAND, :].reshape(PMAX, HD)
                total = sums_ref[part, :, cols] + nn(place, piece)
                rows_ref[part, :, cols] = total.astype(jnp.bfloat16)
            stores[part].start()
        for copy in stores:
            copy.wait()


def finish(starts, outk, outv, sumk, sumv, prompt):
    return pl.pallas_call(
        finish_kernel,
        out_shape=(low_array(1, ROWS, WIDTH),) * 2,
        in_specs=[SMEM, HBM, HBM, VMEM, HBM, HBM],
        out_specs=(HBM, HBM),
        input_output_aliases={4: 0, 5: 1},
        scratch_shapes=[
            pltpu.VMEM((2, SPAN, WIDTH), jnp.float32),
            pltpu.VMEM((2, SPAN, WIDTH), jnp.bfloat16),
            pltpu.SemaphoreType.DMA((2,)),
            pltpu.SemaphoreType.DMA((2,)),
        ],
        compiler_params=FROM_HBM,
        name="finish",
    )(starts, sumk, sumv, prompt, outk, outv)


def exchange(pieces):
    return lax.all_to_all(pieces, "ctx", 0, 0, tiled=True)


def shifted(x, by):
    peers = lax.axis_size("ctx")
    return lax.ppermute(x, "ctx", [(i, i + by) for i in range(peers) if 0 <= i + by < peers])


def partners(x, axis, steps):
    peers = lax.axis_size(axis)
    return [lax.ppermute(x, axis, [(i, i ^ step) for i in range(peers)]) for step in steps]


def summed(x, axis, low, high):
    first, second, third = partners(x, axis, (low, high, low | high))
    return (x + first) + (second + third)


def local(queries, key_rows, values, cotangent, starts, lens, bias):
    count = lax.axis_size("ctx")
    cut, last, first = cut_prompt(starts, key_rows, values)
    held = exchange(cut.reshape(count, 2 * BAND, HD))
    low = shifted(last, 1)
    high = shifted(first, -1)
    stats, *masks = window(
        starts, lens, bias, queries, cotangent, key_rows, values, low, high
    )
    prompt = exchange(route(starts, held)).reshape(BANDS, HEADS, 2 * BAND, HD)
    gprompt, final = prompt_part(bias, queries, cotangent, prompt, stats, masks[3])
    held = exchange(gprompt.reshape(count, SENT, HD))
    attended, grad_q, gk, gv = own_part(
        bias, queries, cotangent, key_rows, values, low, high, prompt, final, masks
    )
    final, gk = lax.optimization_barrier((final, gk))
    glow, ghigh = halo_grads(queries, cotangent, low, high, final, masks[2])
    right = shifted(glow, -1)
    left = shifted(ghigh, 1)
    held, glow, ghigh = lax.optimization_barrier((held, glow, ghigh))
    owned, sums = gather(starts, held)
    returned = exchange(owned).reshape(BANDS, HEADS, 2 * BAND, HD)
    outk, outv, sumk, sumv = merge(gk, gv, left, right)
    sums, sumk = lax.optimization_barrier((sums, sumk))
    grad_bias = jnp.sum(summed(sums, "dp", 1, 2), axis=1)
    grad_k, grad_v = finish(starts, outk, outv, sumk, sumv, returned)
    return attended, grad_q, grad_k, grad_v, grad_bias


def solution(mesh):
    split = P("dp", "ctx", None)
    return jax.shard_map(
        local,
        mesh=mesh,
        in_specs=(split, split, split, split, P("dp", None), P("dp", None), P()),
        out_specs=(split, split, split, split, P()),
        check_vma=False,
    )
```

```python
import math

import jax
import jax.numpy as jnp
from jax import lax
from jax.experimental import pallas as pl
from jax.experimental.pallas import tpu as pltpu
from jax.sharding import PartitionSpec as P

HW = 128
PMAX = 128
ROWS = 256
HD = 128
HEADS = 8
WIDTH = HEADS * HD
BANDS = 8
BAND = PMAX // BANDS
SENT = 2 * BAND + HEADS
SPAN = PMAX + BAND
GROUP = 2
STAGED = 4
MERGE = 8
NEG = -1e30
LOG2E = math.log2(math.e)
SCALE = 1.0 / math.sqrt(HD)
FACTOR = SCALE * LOG2E

SMEM = pl.BlockSpec(memory_space=pltpu.SMEM)
VMEM = pl.BlockSpec(memory_space=pltpu.VMEM)
HBM = pl.BlockSpec(memory_space=pltpu.HBM)
PARAMS = pltpu.CompilerParams(vmem_limit_bytes=20 * 1024 * 1024)
FROM_HBM = pltpu.CompilerParams(vmem_limit_bytes=60 * 1024 * 1024)
NEARLY = pltpu.CompilerParams(vmem_limit_bytes=58 * 1024 * 1024)


def nt(a, b):
    return lax.dot_general(a, b, (((1,), (1,)), ((), ())), preferred_element_type=jnp.float32)


def tn(a, b):
    return lax.dot_general(a, b, (((0,), (0,)), ((), ())), preferred_element_type=jnp.float32)


def nn(a, b):
    return lax.dot_general(a, b, (((1,), (0,)), ((), ())), preferred_element_type=jnp.float32)


def own_start(starts_ref, me):
    start = starts_ref[0, me]
    return start >= 0, jnp.where(start >= 0, start - me * ROWS, 0)


def columns(head):
    return slice(head * HD, (head + 1) * HD)


def float_array(*shape):
    return jax.ShapeDtypeStruct(shape, jnp.float32)


def low_array(*shape):
    return jax.ShapeDtypeStruct(shape, jnp.bfloat16)


def cut_kernel(
    starts_ref,
    k_hbm,
    v_hbm,
    out_hbm,
    last_hbm,
    first_hbm,
    k_ref,
    v_ref,
    out_ref,
    sems,
    edge_sems,
    out_sems,
):
    me = lax.axis_index("ctx")
    offset = own_start(starts_ref, me)[1]
    sources = (k_hbm, v_hbm)
    scratch = (k_ref, v_ref)
    loads = [
        pltpu.make_async_copy(source.at[0], ref, sems.at[part])
        for part, (source, ref) in enumerate(zip(sources, scratch))
    ]
    stores = [
        pltpu.make_async_copy(ref.at[rows, :], target.at[part], edge_sems.at[part, half])
        for part, ref in enumerate(scratch)
        for half, (rows, target) in enumerate(
            ((slice(0, HW), first_hbm), (slice(HW, ROWS), last_hbm))
        )
    ]
    for copy in loads:
        copy.start()
    row = lax.broadcasted_iota(jnp.int32, (PMAX, ROWS), 0)
    frame = lax.broadcasted_iota(jnp.int32, (PMAX, ROWS), 1)
    pick = (frame == row + offset).astype(jnp.bfloat16)
    for part, ref in enumerate(scratch):
        loads[part].wait()
        stores[2 * part].start()
        stores[2 * part + 1].start()
        here = pl.ds(part * BAND, BAND)
        for head in range(HEADS):
            rows = nn(pick, ref[:, columns(head)]).astype(jnp.bfloat16)
            out_ref[:, head, here, :] = rows.reshape(BANDS, BAND, HD)
        store = pltpu.make_async_copy(
            out_ref.at[:, :, here, :], out_hbm.at[:, :, here, :], out_sems.at[part]
        )
        store.start()
        stores.append(store)
    for store in stores:
        store.wait()


def cut_prompt(starts, key_rows, values):
    return pl.pallas_call(
        cut_kernel,
        out_shape=(
            low_array(BANDS, HEADS, 2 * BAND, HD),
            low_array(2, HW, WIDTH),
            low_array(2, HW, WIDTH),
        ),
        in_specs=[SMEM, HBM, HBM],
        out_specs=(HBM, HBM, HBM),
        scratch_shapes=[
            pltpu.VMEM((ROWS, WIDTH), jnp.bfloat16),
            pltpu.VMEM((ROWS, WIDTH), jnp.bfloat16),
            pltpu.VMEM((BANDS, HEADS, 2 * BAND, HD), jnp.bfloat16),
            pltpu.SemaphoreType.DMA((2,)),
            pltpu.SemaphoreType.DMA((2, 2)),
            pltpu.SemaphoreType.DMA((2,)),
        ],
        compiler_params=FROM_HBM,
        name="cut_prompt",
    )(starts, key_rows, values)


def route_kernel(starts_ref, in_ref, out_ref):
    count = in_ref.shape[0]

    def step(target, source):
        out_ref[target] = in_ref[source]
        return jnp.where(starts_ref[0, target] >= 0, target, source)

    lax.fori_loop(0, count, step, jnp.int32(0), unroll=8)


def route(starts, pieces):
    return pl.pallas_call(
        route_kernel,
        out_shape=jax.ShapeDtypeStruct(pieces.shape, pieces.dtype),
        in_specs=[SMEM, VMEM],
        out_specs=VMEM,
        compiler_params=PARAMS,
        name="route",
    )(starts, pieces)


def gather_kernel(starts_ref, in_ref, out_ref, sums_ref):
    count = in_ref.shape[0]
    out_ref[...] = jnp.zeros_like(out_ref)

    def step(target, carry):
        source, total, sums = carry
        block = in_ref[target].astype(jnp.float32)
        total = total + block[: 2 * BAND]
        sums = sums + block[2 * BAND :]
        out_ref[source] = total.astype(jnp.bfloat16)
        begins = starts_ref[0, target] >= 0
        return jnp.where(begins, target, source), jnp.where(begins, 0.0, total), sums

    sums = in_ref[0].astype(jnp.float32)[2 * BAND :]
    carry = (jnp.int32(0), jnp.zeros((2 * BAND, HD), jnp.float32), sums)
    sums_ref[...] = lax.fori_loop(1, count, step, carry, unroll=7)[2]


def gather(starts, pieces):
    return pl.pallas_call(
        gather_kernel,
        out_shape=(low_array(pieces.shape[0], 2 * BAND, HD), float_array(HEADS, HD)),
        in_specs=[SMEM, VMEM],
        out_specs=(VMEM, VMEM),
        compiler_params=PARAMS,
        name="gather",
    )(starts, pieces)


def carried_prompt(starts_ref, lens_ref, me):
    def later(index, found):
        used = starts_ref[0, index] >= 0
        return (
            jnp.where(used, starts_ref[0, index], found[0]),
            jnp.where(used, lens_ref[0, index], found[1]),
        )

    return lax.fori_loop(0, me, later, (jnp.int32(0), jnp.int32(0)))


def grid_of(keys, rows):
    key = lax.broadcasted_iota(jnp.int32, (keys, rows), 0)
    return key, lax.broadcasted_iota(jnp.int32, (keys, rows), 1)


def hold(ref, allowed):
    ref[...] = jnp.where(allowed, 0.0, NEG)


def hold_masks(starts_ref, lens_ref, own_mask, own_flag, halo_mask, prompt_mask):
    me = lax.axis_index("ctx")
    last = starts_ref.shape[1] - 1
    begins, offset = own_start(starts_ref, me)
    offset = jnp.where(begins, offset, ROWS)
    own_len = jnp.where(begins, lens_ref[0, me], 0)
    key, row = grid_of(ROWS, ROWS)
    prompt = (key >= offset) & (key < offset + own_len)
    near = jnp.abs(row - key) <= HW
    hold(own_mask, ((row >= offset) == (key >= offset)) & (prompt | near))
    own_flag[...] = prompt.astype(jnp.float32)
    start, length = carried_prompt(starts_ref, lens_ref, me)
    prompt_end = start + length - (me * ROWS - HW)
    next_begins, next_offset = own_start(starts_ref, jnp.minimum(me + 1, last))
    next_offset = jnp.where(next_begins, next_offset, HW)
    next_offset = jnp.where(me < last, next_offset, 0)
    key, row = grid_of(HW, HW)
    hold(halo_mask.at[0], (key >= row) & (row < offset) & (key >= prompt_end) & (me > 0))
    hold(halo_mask.at[1], (key <= row) & (key < next_offset))
    key, row = grid_of(PMAX, ROWS)
    hold(prompt_mask, (row < offset) & (key < length))


def top_of(x):
    return jnp.max(x, axis=0, keepdims=True)


def sum_of(x):
    return jnp.sum(x, axis=0, keepdims=True)


def window_kernel(
    starts_ref,
    lens_ref,
    bias_ref,
    q_ref,
    d_ref,
    k_ref,
    v_ref,
    low_ref,
    high_ref,
    stats_ref,
    own_mask,
    own_flag,
    halo_mask,
    prompt_mask,
):
    head = pl.program_id(0)

    @pl.when(head == 0)
    def _():
        hold_masks(starts_ref, lens_ref, own_mask, own_flag, halo_mask, prompt_mask)

    q, d, k, v = q_ref[0], d_ref[0], k_ref[0], v_ref[0]
    bias = bias_ref[head] * LOG2E
    flag = own_flag[...]
    x_own = nt(k, q) * FACTOR + (own_mask[...] + flag * bias)
    x_low = nt(low_ref[0], q[:HW]) * FACTOR + halo_mask[0]
    x_high = nt(high_ref[0], q[HW:]) * FACTOR + halo_mask[1]
    tops = jnp.concatenate([top_of(x_low), top_of(x_high)], axis=1)
    top = jnp.maximum(top_of(x_own), tops)
    e_own = jnp.exp2(x_own - top)
    e_low = jnp.exp2(x_low - top[:, :HW])
    e_high = jnp.exp2(x_high - top[:, HW:])
    w_own = e_own * nt(v, d)
    w_low = e_low * nt(low_ref[1], d[:HW])
    w_high = e_high * nt(high_ref[1], d[HW:])
    total = sum_of(e_own) + jnp.concatenate([sum_of(e_low), sum_of(e_high)], axis=1)
    weighted = sum_of(w_own) + jnp.concatenate([sum_of(w_low), sum_of(w_high)], axis=1)
    inverse = 1.0 / total
    own_bias = (sum_of(w_own * flag) - weighted * inverse * sum_of(e_own * flag)) * inverse
    stats_ref[0] = jnp.concatenate(
        [top, total, weighted, own_bias, jnp.zeros((4, ROWS), jnp.float32)], axis=0
    )


def head_rows(part=ROWS):
    return pl.BlockSpec((1, part, HD), lambda head: (0, 0, head))


def head_halo():
    return pl.BlockSpec((2, HW, HD), lambda head: (0, 0, head))


def head_tile(*shape):
    return pl.BlockSpec((1, *shape), lambda head: (head,) + (0,) * len(shape))


def head_pieces():
    return pl.BlockSpec((BANDS, 1, 2 * BAND, HD), lambda head: (0, head, 0, 0))


MASKS = (
    float_array(ROWS, ROWS),
    float_array(ROWS, ROWS),
    float_array(2, HW, HW),
    float_array(PMAX, ROWS),
)


def whole(array):
    return pl.BlockSpec(array.shape, lambda head: (0,) * len(array.shape))


def cost(micros):
    return pl.CostEstimate(flops=micros * 10**9, bytes_accessed=8 << 20, transcendentals=0)


def window(starts, lens, bias, queries, cotangent, key_rows, values, low, high):
    rows = head_rows()
    return pl.pallas_call(
        window_kernel,
        grid=(HEADS,),
        out_shape=(float_array(HEADS, 8, ROWS), *MASKS),
        in_specs=[SMEM, SMEM, SMEM, rows, rows, rows, rows, head_halo(), head_halo()],
        out_specs=(head_tile(8, ROWS), *(whole(mask) for mask in MASKS)),
        compiler_params=PARAMS,
        cost_estimate=cost(20),
        name="window",
    )(starts, lens, bias, queries, cotangent, key_rows, values, low, high)


def prompt_kernel(
    bias_ref, q_ref, d_ref, prompt_ref, stats_ref, mask_ref, grad_hbm, final_hbm, grad_ref, final_ref, sems
):
    mask = mask_ref[...]
    rows = [(q_ref[0, :, columns(head)], d_ref[0, :, columns(head)]) for head in range(HEADS)]
    all_sums, terms, stores = [], [], []
    for first in range(0, HEADS, STAGED):
        heads = range(first, first + STAGED)
        raw = [
            products(
                prompt_ref[:, head, :BAND, :].reshape(PMAX, HD),
                prompt_ref[:, head, BAND:, :].reshape(PMAX, HD),
                *rows[head],
            )
            for head in heads
        ]
        for head, (scores, dprobs) in zip(heads, raw):
            x = scores * FACTOR + (mask + bias_ref[head] * LOG2E)
            stats = stats_ref[head]
            top = jnp.maximum(stats[0:1], top_of(x))
            rescale = jnp.exp2(stats[0:1] - top)
            raised = jnp.exp2(x - top)
            inverse = 1.0 / (stats[1:2] * rescale + sum_of(raised))
            delta = (stats[2:3] * rescale + sum_of(raised * dprobs)) * inverse
            probs = raised * inverse
            dscores = (probs * SCALE) * (dprobs - delta)
            terms.append((probs.astype(jnp.bfloat16), dscores.astype(jnp.bfloat16)))
            final_ref[head] = jnp.concatenate(
                [top, inverse, delta, jnp.zeros((5, ROWS), jnp.float32)], axis=0
            )
            sums = stats[3:4] + sum_of(dscores) * (1.0 / SCALE)
            all_sums.append(sums[:, :HW] + sums[:, HW:])

    stores.append(pltpu.make_async_copy(final_ref, final_hbm, sems.at[HEADS // STAGED]))
    stores[0].start()
    sums = jnp.concatenate(all_sums, axis=0)
    sums = sums + pltpu.roll(sums, HW // 2, 1)
    upper = sums.astype(jnp.bfloat16).astype(jnp.float32)
    lane = lax.broadcasted_iota(jnp.int32, (HEADS, HW), 1)
    tile = jnp.where(lane < HW // 2, upper, sums - upper).astype(jnp.bfloat16)
    for first in range(0, HEADS, STAGED):
        for head in range(first, first + STAGED):
            (q, d), (low_probs, low_ds) = rows[head], terms[head]
            gk = nn(low_ds, q).astype(jnp.bfloat16)
            gv = nn(low_probs, d).astype(jnp.bfloat16)
            grad_ref[:, head, :BAND, :] = gk.reshape(BANDS, BAND, HD)
            grad_ref[:, head, BAND : 2 * BAND, :] = gv.reshape(BANDS, BAND, HD)
            for band in range(BANDS):
                grad_ref[band, head, 2 * BAND :, :] = tile
        here = pl.ds(first, STAGED)
        store = pltpu.make_async_copy(
            grad_ref.at[:, here], grad_hbm.at[:, here], sems.at[first // STAGED]
        )
        store.start()
        stores.append(store)
    for store in stores:
        store.wait()


def prompt_part(bias, queries, cotangent, prompt, stats, prompt_mask):
    return pl.pallas_call(
        prompt_kernel,
        out_shape=(low_array(BANDS, HEADS, SENT, HD), float_array(HEADS, 8, ROWS)),
        in_specs=[SMEM, VMEM, VMEM, VMEM, VMEM, VMEM],
        out_specs=(HBM, HBM),
        scratch_shapes=[
            pltpu.VMEM((BANDS, HEADS, SENT, HD), jnp.bfloat16),
            pltpu.VMEM((HEADS, 8, ROWS), jnp.float32),
            pltpu.SemaphoreType.DMA((HEADS // STAGED + 1,)),
        ],
        compiler_params=PARAMS,
        cost_estimate=cost(4),
        name="prompt_part",
    )(bias, queries, cotangent, prompt, stats, prompt_mask)


def products(keys, values, q, d):
    return nt(keys, q), nt(values, d)


def settled(scores, dprobs, added, final):
    probs = jnp.exp2(scores * FACTOR + (added - final[0:1])) * final[1:2]
    dscores = (probs * SCALE) * (dprobs - final[2:3])
    return probs.astype(jnp.bfloat16), dscores.astype(jnp.bfloat16)


def halo_kernel(q_ref, d_ref, low_ref, high_ref, final_ref, mask_ref, glow_ref, ghigh_ref):
    sides = ((low_ref, glow_ref), (high_ref, ghigh_ref))
    for first in range(0, HEADS, STAGED):
        places = [
            (half, slice(half * HW, (half + 1) * HW), head)
            for head in range(first, first + STAGED)
            for half in range(2)
        ]
        rows = [
            (q_ref[0, part, columns(head)], d_ref[0, part, columns(head)])
            for _, part, head in places
        ]
        raw = [
            products(sides[half][0][0, :, columns(head)], sides[half][0][1, :, columns(head)], q, d)
            for (half, _, head), (q, d) in zip(places, rows)
        ]
        terms = [
            settled(*pair, mask_ref[half], final_ref[head, :, part])
            for (half, part, head), pair in zip(places, raw)
        ]
        for (half, _, head), (q, d), (probs, ds) in zip(places, rows, terms):
            out = sides[half][1]
            out[0, :, columns(head)] = nn(ds, q).astype(jnp.bfloat16)
            out[1, :, columns(head)] = nn(probs, d).astype(jnp.bfloat16)


def halo_grads(queries, cotangent, low, high, final, halo_mask):
    return pl.pallas_call(
        halo_kernel,
        out_shape=(low_array(2, HW, WIDTH), low_array(2, HW, WIDTH)),
        in_specs=[VMEM] * 6,
        out_specs=(VMEM, VMEM),
        compiler_params=PARAMS,
        cost_estimate=cost(4),
        name="halo_grads",
    )(queries, cotangent, low, high, final, halo_mask)


def own_kernel(
    bias_ref,
    q_ref,
    d_ref,
    k_ref,
    v_ref,
    low_ref,
    high_ref,
    prompt_ref,
    final_ref,
    own_mask,
    own_flag,
    halo_mask,
    prompt_mask,
    attended_ref,
    gq_ref,
    gk_ref,
    gv_ref,
):
    members = range(GROUP)
    step = pl.program_id(0)
    blocks = []
    for member in members:
        cols = columns(member)
        q, d = q_ref[0, :, cols], d_ref[0, :, cols]
        kp = prompt_ref[:, member, :BAND, :].reshape(PMAX, HD)
        vp = prompt_ref[:, member, BAND:, :].reshape(PMAX, HD)
        blocks.append(
            (
                (k_ref[0, :, cols], v_ref[0, :, cols], q, d),
                (kp, vp, q, d),
                (low_ref[0, :, cols], low_ref[1, :, cols], q[:HW], d[:HW]),
                (high_ref[0, :, cols], high_ref[1, :, cols], q[HW:], d[HW:]),
            )
        )
    raw = [[products(*block) for block in parts] for parts in blocks]
    terms = []
    for member in members:
        bias = bias_ref[step * GROUP + member] * LOG2E
        final = final_ref[member]
        added = (
            own_mask[...] + own_flag[...] * bias,
            prompt_mask[...] + bias,
            halo_mask[0],
            halo_mask[1],
        )
        finals = (final, final, final[:, :HW], final[:, HW:])
        terms.append(
            [settled(*pair, x, y) for pair, x, y in zip(raw[member], added, finals)]
        )
    for member in members:
        cols = columns(member)
        own, prompt, low, high = blocks[member]
        (probs, ds), (probs_p, ds_p), (probs_l, ds_l), (probs_h, ds_h) = terms[member]
        gk_ref[:, cols] = nn(ds, own[2])
        gv_ref[:, cols] = nn(probs, own[3])
        attended = tn(probs, own[1]) + tn(probs_p, prompt[1])
        attended += jnp.concatenate([tn(probs_l, low[1]), tn(probs_h, high[1])], axis=0)
        attended_ref[0, :, cols] = attended.astype(jnp.bfloat16)
        grad_q = tn(ds, own[0]) + tn(ds_p, prompt[0])
        grad_q += jnp.concatenate([tn(ds_l, low[0]), tn(ds_h, high[0])], axis=0)
        gq_ref[0, :, cols] = grad_q.astype(jnp.bfloat16)


def own_part(bias, queries, cotangent, key_rows, values, low, high, prompt, final, masks):
    rows = pl.BlockSpec((1, ROWS, GROUP * HD), lambda step: (0, 0, step))
    halo = pl.BlockSpec((2, HW, GROUP * HD), lambda step: (0, 0, step))
    pieces = pl.BlockSpec((BANDS, GROUP, 2 * BAND, HD), lambda step: (0, step, 0, 0))
    tile = pl.BlockSpec((GROUP, 8, ROWS), lambda step: (step, 0, 0))
    total = pl.BlockSpec((ROWS, GROUP * HD), lambda step: (0, step))
    return pl.pallas_call(
        own_kernel,
        grid=(HEADS // GROUP,),
        out_shape=(
            low_array(1, ROWS, WIDTH),
            low_array(1, ROWS, WIDTH),
            float_array(ROWS, WIDTH),
            float_array(ROWS, WIDTH),
        ),
        in_specs=[SMEM, rows, rows, rows, rows, halo, halo, pieces, tile]
        + [whole(mask) for mask in MASKS],
        out_specs=(rows, rows, total, total),
        compiler_params=NEARLY,
        cost_estimate=cost(10),
        name="own_part",
    )(bias, queries, cotangent, key_rows, values, low, high, prompt, final, *masks)


def merge_kernel(gk_ref, gv_ref, left_ref, right_ref, outk_ref, outv_ref, sumk_ref, sumv_ref):
    terms = ((gk_ref, outk_ref, sumk_ref), (gv_ref, outv_ref, sumv_ref))
    for part, (ref, out, sums) in enumerate(terms):
        for half, side in enumerate((left_ref, right_ref)):
            rows = slice(half * HW, (half + 1) * HW)
            total = ref[rows, :] + side[part].astype(jnp.float32)
            sums[rows, :] = total
            out[0, rows, :] = total.astype(jnp.bfloat16)


def merge(gk, gv, left, right):
    total = pl.BlockSpec((ROWS, GROUP * HD), lambda step: (0, step))
    rows = pl.BlockSpec((1, ROWS, GROUP * HD), lambda step: (0, 0, step))
    side = pl.BlockSpec((2, HW, GROUP * HD), lambda step: (0, 0, step))
    return pl.pallas_call(
        merge_kernel,
        grid=(HEADS // GROUP,),
        out_shape=(low_array(1, ROWS, WIDTH),) * 2 + (float_array(ROWS, WIDTH),) * 2,
        in_specs=[total, total, side, side],
        out_specs=(rows, rows, total, total),
        compiler_params=FROM_HBM,
        cost_estimate=cost(MERGE),
        name="merge",
    )(gk, gv, left, right)


def finish_kernel(
    starts_ref,
    sumk_hbm,
    sumv_hbm,
    prompt_ref,
    _ink,
    _inv,
    outk_hbm,
    outv_hbm,
    sums_ref,
    rows_ref,
    load_sems,
    store_sems,
):
    me = lax.axis_index("ctx")
    begins, offset = own_start(starts_ref, me)

    @pl.when(begins)
    def _():
        base = pl.multiple_of(jnp.minimum(offset // BAND * BAND, ROWS - SPAN), BAND)
        span = pl.ds(base, SPAN)
        loads = [
            pltpu.make_async_copy(ref.at[span, :], sums_ref.at[part], load_sems.at[part])
            for part, ref in enumerate((sumk_hbm, sumv_hbm))
        ]
        stores = [
            pltpu.make_async_copy(rows_ref.at[part], ref.at[0, span, :], store_sems.at[part])
            for part, ref in enumerate((outk_hbm, outv_hbm))
        ]
        for copy in loads:
            copy.start()
        frame, row = grid_of(SPAN, PMAX)
        place = (frame == row + (offset - base)).astype(jnp.bfloat16)
        for part in range(2):
            loads[part].wait()
            for head in range(HEADS):
                cols = columns(head)
                piece = prompt_ref[:, head, part * BAND : (part + 1) * BAND, :].reshape(PMAX, HD)
                total = sums_ref[part, :, cols] + nn(place, piece)
                rows_ref[part, :, cols] = total.astype(jnp.bfloat16)
            stores[part].start()
        for copy in stores:
            copy.wait()


def finish(starts, outk, outv, sumk, sumv, prompt):
    return pl.pallas_call(
        finish_kernel,
        out_shape=(low_array(1, ROWS, WIDTH),) * 2,
        in_specs=[SMEM, HBM, HBM, VMEM, HBM, HBM],
        out_specs=(HBM, HBM),
        input_output_aliases={4: 0, 5: 1},
        scratch_shapes=[
            pltpu.VMEM((2, SPAN, WIDTH), jnp.float32),
            pltpu.VMEM((2, SPAN, WIDTH), jnp.bfloat16),
            pltpu.SemaphoreType.DMA((2,)),
            pltpu.SemaphoreType.DMA((2,)),
        ],
        compiler_params=NEARLY,
        name="finish",
    )(starts, sumk, sumv, prompt, outk, outv)


def exchange(pieces):
    return lax.all_to_all(pieces, "ctx", 0, 0, tiled=True)


def shifted(x, by):
    peers = lax.axis_size("ctx")
    return lax.ppermute(x, "ctx", [(i, i + by) for i in range(peers) if 0 <= i + by < peers])


def partners(x, axis, steps):
    peers = lax.axis_size(axis)
    return [lax.ppermute(x, axis, [(i, i ^ step) for i in range(peers)]) for step in steps]


def summed(x, axis, low, high):
    first, second, third = partners(x, axis, (low, high, low | high))
    return (x + first) + (second + third)


def local(queries, key_rows, values, cotangent, starts, lens, bias):
    count = lax.axis_size("ctx")
    cut, last, first = cut_prompt(starts, key_rows, values)
    held = exchange(cut.reshape(count, 2 * BAND, HD))
    low = shifted(last, 1)
    high = shifted(first, -1)
    stats, *masks = window(
        starts, lens, bias, queries, cotangent, key_rows, values, low, high
    )
    prompt = exchange(route(starts, held)).reshape(BANDS, HEADS, 2 * BAND, HD)
    gprompt, final = prompt_part(bias, queries, cotangent, prompt, stats, masks[3])
    held = exchange(gprompt.reshape(count, SENT, HD))
    attended, grad_q, gk, gv = own_part(
        bias, queries, cotangent, key_rows, values, low, high, prompt, final, masks
    )
    final, gk = lax.optimization_barrier((final, gk))
    glow, ghigh = halo_grads(queries, cotangent, low, high, final, masks[2])
    right = shifted(glow, -1)
    left = shifted(ghigh, 1)
    held, glow, ghigh = lax.optimization_barrier((held, glow, ghigh))
    owned, sums = gather(starts, held)
    returned = exchange(owned).reshape(BANDS, HEADS, 2 * BAND, HD)
    grad_bias = jnp.sum(summed(sums, "dp", 1, 2), axis=1)
    gk, grad_bias = lax.optimization_barrier((gk, grad_bias))
    outk, outv, sumk, sumv = merge(gk, gv, left, right)
    grad_k, grad_v = finish(starts, outk, outv, sumk, sumv, returned)
    return attended, grad_q, grad_k, grad_v, grad_bias


def solution(mesh):
    split = P("dp", "ctx", None)
    return jax.shard_map(
        local,
        mesh=mesh,
        in_specs=(split, split, split, split, P("dp", None), P("dp", None), P()),
        out_specs=(split, split, split, split, P()),
        check_vma=False,
    )
```

```python
import math

import jax
import jax.numpy as jnp
from jax import lax
from jax.experimental import pallas as pl
from jax.experimental.pallas import tpu as pltpu
from jax.sharding import PartitionSpec as P

HW = 128
PMAX = 128
ROWS = 256
HD = 128
HEADS = 8
WIDTH = HEADS * HD
BANDS = 8
BAND = PMAX // BANDS
SENT = 2 * BAND + HEADS
SPAN = PMAX + BAND
GROUP = 2
STAGED = 4
MERGE = 8
NEG = -1e30
LOG2E = math.log2(math.e)
SCALE = 1.0 / math.sqrt(HD)
FACTOR = SCALE * LOG2E

SMEM = pl.BlockSpec(memory_space=pltpu.SMEM)
VMEM = pl.BlockSpec(memory_space=pltpu.VMEM)
HBM = pl.BlockSpec(memory_space=pltpu.HBM)
PARAMS = pltpu.CompilerParams(vmem_limit_bytes=20 * 1024 * 1024)
FROM_HBM = pltpu.CompilerParams(vmem_limit_bytes=60 * 1024 * 1024)
NEARLY = pltpu.CompilerParams(vmem_limit_bytes=52 * 1024 * 1024)


def nt(a, b):
    return lax.dot_general(a, b, (((1,), (1,)), ((), ())), preferred_element_type=jnp.float32)


def tn(a, b):
    return lax.dot_general(a, b, (((0,), (0,)), ((), ())), preferred_element_type=jnp.float32)


def nn(a, b):
    return lax.dot_general(a, b, (((1,), (0,)), ((), ())), preferred_element_type=jnp.float32)


def own_start(starts_ref, me):
    start = starts_ref[0, me]
    return start >= 0, jnp.where(start >= 0, start - me * ROWS, 0)


def columns(head):
    return slice(head * HD, (head + 1) * HD)


def float_array(*shape):
    return jax.ShapeDtypeStruct(shape, jnp.float32)


def low_array(*shape):
    return jax.ShapeDtypeStruct(shape, jnp.bfloat16)


def cut_kernel(
    starts_ref,
    k_hbm,
    v_hbm,
    out_hbm,
    last_hbm,
    first_hbm,
    k_ref,
    v_ref,
    out_ref,
    sems,
    edge_sems,
    out_sems,
):
    me = lax.axis_index("ctx")
    offset = own_start(starts_ref, me)[1]
    sources = (k_hbm, v_hbm)
    scratch = (k_ref, v_ref)
    loads = [
        pltpu.make_async_copy(source.at[0], ref, sems.at[part])
        for part, (source, ref) in enumerate(zip(sources, scratch))
    ]
    stores = [
        pltpu.make_async_copy(ref.at[rows, :], target.at[part], edge_sems.at[part, half])
        for part, ref in enumerate(scratch)
        for half, (rows, target) in enumerate(
            ((slice(0, HW), first_hbm), (slice(HW, ROWS), last_hbm))
        )
    ]
    for copy in loads:
        copy.start()
    row = lax.broadcasted_iota(jnp.int32, (PMAX, ROWS), 0)
    frame = lax.broadcasted_iota(jnp.int32, (PMAX, ROWS), 1)
    pick = (frame == row + offset).astype(jnp.bfloat16)
    for part, ref in enumerate(scratch):
        loads[part].wait()
        stores[2 * part].start()
        stores[2 * part + 1].start()
        here = pl.ds(part * BAND, BAND)
        for head in range(HEADS):
            rows = nn(pick, ref[:, columns(head)]).astype(jnp.bfloat16)
            out_ref[:, head, here, :] = rows.reshape(BANDS, BAND, HD)
        store = pltpu.make_async_copy(
            out_ref.at[:, :, here, :], out_hbm.at[:, :, here, :], out_sems.at[part]
        )
        store.start()
        stores.append(store)
    for store in stores:
        store.wait()


def cut_prompt(starts, key_rows, values):
    return pl.pallas_call(
        cut_kernel,
        out_shape=(
            low_array(BANDS, HEADS, 2 * BAND, HD),
            low_array(2, HW, WIDTH),
            low_array(2, HW, WIDTH),
        ),
        in_specs=[SMEM, HBM, HBM],
        out_specs=(HBM, HBM, HBM),
        scratch_shapes=[
            pltpu.VMEM((ROWS, WIDTH), jnp.bfloat16),
            pltpu.VMEM((ROWS, WIDTH), jnp.bfloat16),
            pltpu.VMEM((BANDS, HEADS, 2 * BAND, HD), jnp.bfloat16),
            pltpu.SemaphoreType.DMA((2,)),
            pltpu.SemaphoreType.DMA((2, 2)),
            pltpu.SemaphoreType.DMA((2,)),
        ],
        compiler_params=FROM_HBM,
        name="cut_prompt",
    )(starts, key_rows, values)


def route_kernel(starts_ref, in_ref, out_ref):
    count = in_ref.shape[0]

    def step(target, source):
        out_ref[target] = in_ref[source]
        return jnp.where(starts_ref[0, target] >= 0, target, source)

    lax.fori_loop(0, count, step, jnp.int32(0), unroll=8)


def route(starts, pieces):
    return pl.pallas_call(
        route_kernel,
        out_shape=jax.ShapeDtypeStruct(pieces.shape, pieces.dtype),
        in_specs=[SMEM, VMEM],
        out_specs=VMEM,
        compiler_params=PARAMS,
        name="route",
    )(starts, pieces)


def gather_kernel(starts_ref, in_ref, out_ref, sums_ref):
    count = in_ref.shape[0]
    out_ref[...] = jnp.zeros_like(out_ref)

    def step(target, carry):
        source, total, sums = carry
        block = in_ref[target].astype(jnp.float32)
        total = total + block[: 2 * BAND]
        sums = sums + block[2 * BAND :]
        out_ref[source] = total.astype(jnp.bfloat16)
        begins = starts_ref[0, target] >= 0
        return jnp.where(begins, target, source), jnp.where(begins, 0.0, total), sums

    sums = in_ref[0].astype(jnp.float32)[2 * BAND :]
    carry = (jnp.int32(0), jnp.zeros((2 * BAND, HD), jnp.float32), sums)
    sums_ref[...] = lax.fori_loop(1, count, step, carry, unroll=7)[2]


def gather(starts, pieces):
    return pl.pallas_call(
        gather_kernel,
        out_shape=(low_array(pieces.shape[0], 2 * BAND, HD), float_array(HEADS, HD)),
        in_specs=[SMEM, VMEM],
        out_specs=(VMEM, VMEM),
        compiler_params=PARAMS,
        name="gather",
    )(starts, pieces)


def carried_prompt(starts_ref, lens_ref, me):
    def later(index, found):
        used = starts_ref[0, index] >= 0
        return (
            jnp.where(used, starts_ref[0, index], found[0]),
            jnp.where(used, lens_ref[0, index], found[1]),
        )

    return lax.fori_loop(0, me, later, (jnp.int32(0), jnp.int32(0)))


def grid_of(keys, rows):
    key = lax.broadcasted_iota(jnp.int32, (keys, rows), 0)
    return key, lax.broadcasted_iota(jnp.int32, (keys, rows), 1)


def hold(ref, allowed):
    ref[...] = jnp.where(allowed, 0.0, NEG)


def hold_masks(starts_ref, lens_ref, own_mask, halo_mask, prompt_mask):
    me = lax.axis_index("ctx")
    last = starts_ref.shape[1] - 1
    begins, offset = own_start(starts_ref, me)
    offset = jnp.where(begins, offset, ROWS)
    own_len = jnp.where(begins, lens_ref[0, me], 0)
    key, row = grid_of(ROWS, ROWS)
    prompt = (key >= offset) & (key < offset + own_len)
    near = jnp.abs(row - key) <= HW
    hold(own_mask.at[0], ((row >= offset) == (key >= offset)) & (prompt | near))
    own_mask[1] = prompt.astype(jnp.float32)
    start, length = carried_prompt(starts_ref, lens_ref, me)
    prompt_end = start + length - (me * ROWS - HW)
    next_begins, next_offset = own_start(starts_ref, jnp.minimum(me + 1, last))
    next_offset = jnp.where(next_begins, next_offset, HW)
    next_offset = jnp.where(me < last, next_offset, 0)
    key, row = grid_of(HW, HW)
    hold(halo_mask.at[0], (key >= row) & (row < offset) & (key >= prompt_end) & (me > 0))
    hold(halo_mask.at[1], (key <= row) & (key < next_offset))
    key, row = grid_of(PMAX, ROWS)
    hold(prompt_mask, (row < offset) & (key < length))


def top_of(x):
    return jnp.max(x, axis=0, keepdims=True)


def sum_of(x):
    return jnp.sum(x, axis=0, keepdims=True)


def window_kernel(
    starts_ref,
    lens_ref,
    bias_ref,
    q_ref,
    d_ref,
    k_ref,
    v_ref,
    low_ref,
    high_ref,
    stats_ref,
    own_mask,
    halo_mask,
    prompt_mask,
):
    head = pl.program_id(0)

    @pl.when(head == 0)
    def _():
        hold_masks(starts_ref, lens_ref, own_mask, halo_mask, prompt_mask)

    q, d, k, v = q_ref[0], d_ref[0], k_ref[0], v_ref[0]
    bias = bias_ref[head] * LOG2E
    flag = own_mask[1]
    x_own = nt(k, q) * FACTOR + (own_mask[0] + flag * bias)
    x_low = nt(low_ref[0], q[:HW]) * FACTOR + halo_mask[0]
    x_high = nt(high_ref[0], q[HW:]) * FACTOR + halo_mask[1]
    tops = jnp.concatenate([top_of(x_low), top_of(x_high)], axis=1)
    top = jnp.maximum(top_of(x_own), tops)
    e_own = jnp.exp2(x_own - top)
    e_low = jnp.exp2(x_low - top[:, :HW])
    e_high = jnp.exp2(x_high - top[:, HW:])
    w_own = e_own * nt(v, d)
    w_low = e_low * nt(low_ref[1], d[:HW])
    w_high = e_high * nt(high_ref[1], d[HW:])
    total = sum_of(e_own) + jnp.concatenate([sum_of(e_low), sum_of(e_high)], axis=1)
    weighted = sum_of(w_own) + jnp.concatenate([sum_of(w_low), sum_of(w_high)], axis=1)
    inverse = 1.0 / total
    own_bias = (sum_of(w_own * flag) - weighted * inverse * sum_of(e_own * flag)) * inverse
    stats_ref[0] = jnp.concatenate(
        [top, total, weighted, own_bias, jnp.zeros((4, ROWS), jnp.float32)], axis=0
    )


def head_rows(part=ROWS):
    return pl.BlockSpec((1, part, HD), lambda head: (0, 0, head))


def head_halo():
    return pl.BlockSpec((2, HW, HD), lambda head: (0, 0, head))


def head_tile(*shape):
    return pl.BlockSpec((1, *shape), lambda head: (head,) + (0,) * len(shape))


def head_pieces():
    return pl.BlockSpec((BANDS, 1, 2 * BAND, HD), lambda head: (0, head, 0, 0))


MASKS = (
    float_array(2, ROWS, ROWS),
    float_array(2, HW, HW),
    float_array(PMAX, ROWS),
)


def whole(array):
    return pl.BlockSpec(array.shape, lambda head: (0,) * len(array.shape))


def cost(micros):
    return pl.CostEstimate(flops=micros * 10**9, bytes_accessed=8 << 20, transcendentals=0)


def window(starts, lens, bias, queries, cotangent, key_rows, values, low, high):
    rows = head_rows()
    return pl.pallas_call(
        window_kernel,
        grid=(HEADS,),
        out_shape=(float_array(HEADS, 8, ROWS), *MASKS),
        in_specs=[SMEM, SMEM, SMEM, rows, rows, rows, rows, head_halo(), head_halo()],
        out_specs=(head_tile(8, ROWS), *(whole(mask) for mask in MASKS)),
        compiler_params=PARAMS,
        cost_estimate=cost(20),
        name="window",
    )(starts, lens, bias, queries, cotangent, key_rows, values, low, high)


def prompt_kernel(
    bias_ref, q_ref, d_ref, prompt_ref, stats_ref, mask_ref, grad_hbm, final_hbm, grad_ref, final_ref, sems
):
    mask = mask_ref[...]
    rows = [(q_ref[0, :, columns(head)], d_ref[0, :, columns(head)]) for head in range(HEADS)]
    all_sums, terms, stores = [], [], []
    for first in range(0, HEADS, STAGED):
        heads = range(first, first + STAGED)
        raw = [
            products(
                prompt_ref[:, head, :BAND, :].reshape(PMAX, HD),
                prompt_ref[:, head, BAND:, :].reshape(PMAX, HD),
                *rows[head],
            )
            for head in heads
        ]
        for head, (scores, dprobs) in zip(heads, raw):
            x = scores * FACTOR + (mask + bias_ref[head] * LOG2E)
            stats = stats_ref[head]
            top = jnp.maximum(stats[0:1], top_of(x))
            rescale = jnp.exp2(stats[0:1] - top)
            raised = jnp.exp2(x - top)
            inverse = 1.0 / (stats[1:2] * rescale + sum_of(raised))
            delta = (stats[2:3] * rescale + sum_of(raised * dprobs)) * inverse
            probs = raised * inverse
            dscores = (probs * SCALE) * (dprobs - delta)
            terms.append((probs.astype(jnp.bfloat16), dscores.astype(jnp.bfloat16)))
            final_ref[head] = jnp.concatenate(
                [top, inverse, delta, jnp.zeros((5, ROWS), jnp.float32)], axis=0
            )
            sums = stats[3:4] + sum_of(dscores) * (1.0 / SCALE)
            all_sums.append(sums[:, :HW] + sums[:, HW:])

    stores.append(pltpu.make_async_copy(final_ref, final_hbm, sems.at[HEADS // STAGED]))
    stores[0].start()
    sums = jnp.concatenate(all_sums, axis=0)
    sums = sums + pltpu.roll(sums, HW // 2, 1)
    upper = sums.astype(jnp.bfloat16).astype(jnp.float32)
    lane = lax.broadcasted_iota(jnp.int32, (HEADS, HW), 1)
    tile = jnp.where(lane < HW // 2, upper, sums - upper).astype(jnp.bfloat16)
    for first in range(0, HEADS, STAGED):
        for head in range(first, first + STAGED):
            (q, d), (low_probs, low_ds) = rows[head], terms[head]
            gk = nn(low_ds, q).astype(jnp.bfloat16)
            gv = nn(low_probs, d).astype(jnp.bfloat16)
            grad_ref[:, head, :BAND, :] = gk.reshape(BANDS, BAND, HD)
            grad_ref[:, head, BAND : 2 * BAND, :] = gv.reshape(BANDS, BAND, HD)
            for band in range(BANDS):
                grad_ref[band, head, 2 * BAND :, :] = tile
        here = pl.ds(first, STAGED)
        store = pltpu.make_async_copy(
            grad_ref.at[:, here], grad_hbm.at[:, here], sems.at[first // STAGED]
        )
        store.start()
        stores.append(store)
    for store in stores:
        store.wait()


def prompt_part(bias, queries, cotangent, prompt, stats, prompt_mask):
    return pl.pallas_call(
        prompt_kernel,
        out_shape=(low_array(BANDS, HEADS, SENT, HD), float_array(HEADS, 8, ROWS)),
        in_specs=[SMEM, VMEM, VMEM, VMEM, VMEM, VMEM],
        out_specs=(HBM, HBM),
        scratch_shapes=[
            pltpu.VMEM((BANDS, HEADS, SENT, HD), jnp.bfloat16),
            pltpu.VMEM((HEADS, 8, ROWS), jnp.float32),
            pltpu.SemaphoreType.DMA((HEADS // STAGED + 1,)),
        ],
        compiler_params=PARAMS,
        cost_estimate=cost(4),
        name="prompt_part",
    )(bias, queries, cotangent, prompt, stats, prompt_mask)


def products(keys, values, q, d):
    return nt(keys, q), nt(values, d)


def settled(scores, dprobs, added, final):
    probs = jnp.exp2(scores * FACTOR + (added - final[0:1])) * final[1:2]
    dscores = (probs * SCALE) * (dprobs - final[2:3])
    return probs.astype(jnp.bfloat16), dscores.astype(jnp.bfloat16)


def halo_kernel(q_ref, d_ref, low_ref, high_ref, final_ref, mask_ref, glow_ref, ghigh_ref):
    sides = ((low_ref, glow_ref), (high_ref, ghigh_ref))
    for first in range(0, HEADS, STAGED):
        places = [
            (half, slice(half * HW, (half + 1) * HW), head)
            for head in range(first, first + STAGED)
            for half in range(2)
        ]
        rows = [
            (q_ref[0, part, columns(head)], d_ref[0, part, columns(head)])
            for _, part, head in places
        ]
        raw = [
            products(sides[half][0][0, :, columns(head)], sides[half][0][1, :, columns(head)], q, d)
            for (half, _, head), (q, d) in zip(places, rows)
        ]
        terms = [
            settled(*pair, mask_ref[half], final_ref[head, :, part])
            for (half, part, head), pair in zip(places, raw)
        ]
        for (half, _, head), (q, d), (probs, ds) in zip(places, rows, terms):
            out = sides[half][1]
            out[0, :, columns(head)] = nn(ds, q).astype(jnp.bfloat16)
            out[1, :, columns(head)] = nn(probs, d).astype(jnp.bfloat16)


def halo_grads(queries, cotangent, low, high, final, halo_mask):
    return pl.pallas_call(
        halo_kernel,
        out_shape=(low_array(2, HW, WIDTH), low_array(2, HW, WIDTH)),
        in_specs=[VMEM] * 6,
        out_specs=(VMEM, VMEM),
        compiler_params=PARAMS,
        cost_estimate=cost(4),
        name="halo_grads",
    )(queries, cotangent, low, high, final, halo_mask)


def own_kernel(
    bias_ref,
    q_ref,
    d_ref,
    k_ref,
    v_ref,
    low_ref,
    high_ref,
    prompt_ref,
    final_ref,
    own_mask,
    halo_mask,
    prompt_mask,
    attended_ref,
    gq_ref,
    gk_ref,
    gv_ref,
):
    members = range(GROUP)
    step = pl.program_id(0)
    blocks = []
    for member in members:
        cols = columns(member)
        q, d = q_ref[0, :, cols], d_ref[0, :, cols]
        kp = prompt_ref[:, member, :BAND, :].reshape(PMAX, HD)
        vp = prompt_ref[:, member, BAND:, :].reshape(PMAX, HD)
        blocks.append(
            (
                (k_ref[0, :, cols], v_ref[0, :, cols], q, d),
                (kp, vp, q, d),
                (low_ref[0, :, cols], low_ref[1, :, cols], q[:HW], d[:HW]),
                (high_ref[0, :, cols], high_ref[1, :, cols], q[HW:], d[HW:]),
            )
        )
    raw = [[products(*block) for block in parts] for parts in blocks]
    terms = []
    for member in members:
        bias = bias_ref[step * GROUP + member] * LOG2E
        final = final_ref[member]
        added = (
            own_mask[0] + own_mask[1] * bias,
            prompt_mask[...] + bias,
            halo_mask[0],
            halo_mask[1],
        )
        finals = (final, final, final[:, :HW], final[:, HW:])
        terms.append(
            [settled(*pair, x, y) for pair, x, y in zip(raw[member], added, finals)]
        )
    for member in members:
        cols = columns(member)
        own, prompt, low, high = blocks[member]
        (probs, ds), (probs_p, ds_p), (probs_l, ds_l), (probs_h, ds_h) = terms[member]
        gk_ref[:, cols] = nn(ds, own[2])
        gv_ref[:, cols] = nn(probs, own[3])
        attended = tn(probs, own[1]) + tn(probs_p, prompt[1])
        attended += jnp.concatenate([tn(probs_l, low[1]), tn(probs_h, high[1])], axis=0)
        attended_ref[0, :, cols] = attended.astype(jnp.bfloat16)
        grad_q = tn(ds, own[0]) + tn(ds_p, prompt[0])
        grad_q += jnp.concatenate([tn(ds_l, low[0]), tn(ds_h, high[0])], axis=0)
        gq_ref[0, :, cols] = grad_q.astype(jnp.bfloat16)


def own_part(bias, queries, cotangent, key_rows, values, low, high, prompt, final, masks):
    rows = pl.BlockSpec((1, ROWS, GROUP * HD), lambda step: (0, 0, step))
    halo = pl.BlockSpec((2, HW, GROUP * HD), lambda step: (0, 0, step))
    pieces = pl.BlockSpec((BANDS, GROUP, 2 * BAND, HD), lambda step: (0, step, 0, 0))
    tile = pl.BlockSpec((GROUP, 8, ROWS), lambda step: (step, 0, 0))
    total = pl.BlockSpec((ROWS, GROUP * HD), lambda step: (0, step))
    return pl.pallas_call(
        own_kernel,
        grid=(HEADS // GROUP,),
        out_shape=(
            low_array(1, ROWS, WIDTH),
            low_array(1, ROWS, WIDTH),
            float_array(ROWS, WIDTH),
            float_array(ROWS, WIDTH),
        ),
        in_specs=[SMEM, rows, rows, rows, rows, halo, halo, pieces, tile]
        + [whole(mask) for mask in MASKS],
        out_specs=(rows, rows, total, total),
        compiler_params=NEARLY,
        cost_estimate=cost(10),
        name="own_part",
    )(bias, queries, cotangent, key_rows, values, low, high, prompt, final, *masks)


def merge_kernel(gk_ref, gv_ref, left_ref, right_ref, outk_ref, outv_ref, sums_ref):
    for part, (ref, out) in enumerate(((gk_ref, outk_ref), (gv_ref, outv_ref))):
        for half, side in enumerate((left_ref, right_ref)):
            rows = slice(half * HW, (half + 1) * HW)
            total = ref[rows, :] + side[part].astype(jnp.float32)
            sums_ref[part, rows, :] = total
            out[0, rows, :] = total.astype(jnp.bfloat16)


def merge(gk, gv, left, right):
    total = pl.BlockSpec((ROWS, GROUP * HD), lambda step: (0, step))
    rows = pl.BlockSpec((1, ROWS, GROUP * HD), lambda step: (0, 0, step))
    side = pl.BlockSpec((2, HW, GROUP * HD), lambda step: (0, 0, step))
    both = pl.BlockSpec((2, ROWS, GROUP * HD), lambda step: (0, 0, step))
    return pl.pallas_call(
        merge_kernel,
        grid=(HEADS // GROUP,),
        out_shape=(low_array(1, ROWS, WIDTH),) * 2 + (float_array(2, ROWS, WIDTH),),
        in_specs=[total, total, side, side],
        out_specs=(rows, rows, both),
        compiler_params=NEARLY,
        cost_estimate=cost(MERGE),
        name="merge",
    )(gk, gv, left, right)


def finish_kernel(
    starts_ref,
    sums_hbm,
    prompt_ref,
    _ink,
    _inv,
    outk_hbm,
    outv_hbm,
    sums_ref,
    rows_ref,
    load_sems,
    store_sems,
):
    me = lax.axis_index("ctx")
    begins, offset = own_start(starts_ref, me)

    @pl.when(begins)
    def _():
        base = pl.multiple_of(jnp.minimum(offset // BAND * BAND, ROWS - SPAN), BAND)
        span = pl.ds(base, SPAN)
        loads = [
            pltpu.make_async_copy(sums_hbm.at[part, span, :], sums_ref.at[part], load_sems.at[part])
            for part in range(2)
        ]
        stores = [
            pltpu.make_async_copy(rows_ref.at[part], ref.at[0, span, :], store_sems.at[part])
            for part, ref in enumerate((outk_hbm, outv_hbm))
        ]
        for copy in loads:
            copy.start()
        frame, row = grid_of(SPAN, PMAX)
        place = (frame == row + (offset - base)).astype(jnp.bfloat16)
        for part in range(2):
            loads[part].wait()
            for head in range(HEADS):
                cols = columns(head)
                piece = prompt_ref[:, head, part * BAND : (part + 1) * BAND, :].reshape(PMAX, HD)
                total = sums_ref[part, :, cols] + nn(place, piece)
                rows_ref[part, :, cols] = total.astype(jnp.bfloat16)
            stores[part].start()
        for copy in stores:
            copy.wait()


def finish(starts, outk, outv, sums, prompt):
    return pl.pallas_call(
        finish_kernel,
        out_shape=(low_array(1, ROWS, WIDTH),) * 2,
        in_specs=[SMEM, HBM, VMEM, HBM, HBM],
        out_specs=(HBM, HBM),
        input_output_aliases={3: 0, 4: 1},
        scratch_shapes=[
            pltpu.VMEM((2, SPAN, WIDTH), jnp.float32),
            pltpu.VMEM((2, SPAN, WIDTH), jnp.bfloat16),
            pltpu.SemaphoreType.DMA((2,)),
            pltpu.SemaphoreType.DMA((2,)),
        ],
        compiler_params=NEARLY,
        name="finish",
    )(starts, sums, prompt, outk, outv)


def exchange(pieces):
    return lax.all_to_all(pieces, "ctx", 0, 0, tiled=True)


def shifted(x, by):
    peers = lax.axis_size("ctx")
    return lax.ppermute(x, "ctx", [(i, i + by) for i in range(peers) if 0 <= i + by < peers])


def partners(x, axis, steps):
    peers = lax.axis_size(axis)
    return [lax.ppermute(x, axis, [(i, i ^ step) for i in range(peers)]) for step in steps]


def summed(x, axis, low, high):
    first, second, third = partners(x, axis, (low, high, low | high))
    return (x + first) + (second + third)


def local(queries, key_rows, values, cotangent, starts, lens, bias):
    count = lax.axis_size("ctx")
    cut, last, first = cut_prompt(starts, key_rows, values)
    held = exchange(cut.reshape(count, 2 * BAND, HD))
    low = shifted(last, 1)
    high = shifted(first, -1)
    stats, *masks = window(
        starts, lens, bias, queries, cotangent, key_rows, values, low, high
    )
    prompt = exchange(route(starts, held)).reshape(BANDS, HEADS, 2 * BAND, HD)
    gprompt, final = prompt_part(bias, queries, cotangent, prompt, stats, masks[2])
    held = exchange(gprompt.reshape(count, SENT, HD))
    attended, grad_q, gk, gv = own_part(
        bias, queries, cotangent, key_rows, values, low, high, prompt, final, masks
    )
    final, gk = lax.optimization_barrier((final, gk))
    glow, ghigh = halo_grads(queries, cotangent, low, high, final, masks[1])
    right = shifted(glow, -1)
    left = shifted(ghigh, 1)
    held, glow, ghigh = lax.optimization_barrier((held, glow, ghigh))
    owned, sums = gather(starts, held)
    returned = exchange(owned).reshape(BANDS, HEADS, 2 * BAND, HD)
    grad_bias = jnp.sum(summed(sums, "dp", 1, 2), axis=1)
    gk, grad_bias = lax.optimization_barrier((gk, grad_bias))
    outk, outv, both = merge(gk, gv, left, right)
    grad_k, grad_v = finish(starts, outk, outv, both, returned)
    return attended, grad_q, grad_k, grad_v, grad_bias


def solution(mesh):
    split = P("dp", "ctx", None)
    return jax.shard_map(
        local,
        mesh=mesh,
        in_specs=(split, split, split, split, P("dp", None), P("dp", None), P()),
        out_specs=(split, split, split, split, P()),
        check_vma=False,
    )
```

```python
import math

import jax
import jax.numpy as jnp
from jax import lax
from jax.experimental import pallas as pl
from jax.experimental.pallas import tpu as pltpu
from jax.sharding import PartitionSpec as P

HW = 128
PMAX = 128
ROWS = 256
HD = 128
HEADS = 8
WIDTH = HEADS * HD
BANDS = 8
BAND = PMAX // BANDS
SENT = 2 * BAND + HEADS
SPAN = PMAX + BAND
GROUP = 2
STAGED = 4
MERGE = 8
NEG = -1e30
LOG2E = math.log2(math.e)
SCALE = 1.0 / math.sqrt(HD)
FACTOR = SCALE * LOG2E

SMEM = pl.BlockSpec(memory_space=pltpu.SMEM)
VMEM = pl.BlockSpec(memory_space=pltpu.VMEM)
HBM = pl.BlockSpec(memory_space=pltpu.HBM)
PARAMS = pltpu.CompilerParams(vmem_limit_bytes=20 * 1024 * 1024)
FROM_HBM = pltpu.CompilerParams(vmem_limit_bytes=60 * 1024 * 1024)
NEARLY = pltpu.CompilerParams(vmem_limit_bytes=52 * 1024 * 1024)


def nt(a, b):
    return lax.dot_general(a, b, (((1,), (1,)), ((), ())), preferred_element_type=jnp.float32)


def tn(a, b):
    return lax.dot_general(a, b, (((0,), (0,)), ((), ())), preferred_element_type=jnp.float32)


def nn(a, b):
    return lax.dot_general(a, b, (((1,), (0,)), ((), ())), preferred_element_type=jnp.float32)


def own_start(starts_ref, me):
    start = starts_ref[0, me]
    return start >= 0, jnp.where(start >= 0, start - me * ROWS, 0)


def columns(head):
    return slice(head * HD, (head + 1) * HD)


def float_array(*shape):
    return jax.ShapeDtypeStruct(shape, jnp.float32)


def low_array(*shape):
    return jax.ShapeDtypeStruct(shape, jnp.bfloat16)


def cut_kernel(
    starts_ref,
    k_hbm,
    v_hbm,
    out_hbm,
    last_hbm,
    first_hbm,
    k_ref,
    v_ref,
    out_ref,
    sems,
    edge_sems,
    out_sems,
):
    me = lax.axis_index("ctx")
    offset = own_start(starts_ref, me)[1]
    sources = (k_hbm, v_hbm)
    scratch = (k_ref, v_ref)
    loads = [
        pltpu.make_async_copy(source.at[0], ref, sems.at[part])
        for part, (source, ref) in enumerate(zip(sources, scratch))
    ]
    stores = [
        pltpu.make_async_copy(ref.at[rows, :], target.at[part], edge_sems.at[part, half])
        for part, ref in enumerate(scratch)
        for half, (rows, target) in enumerate(
            ((slice(0, HW), first_hbm), (slice(HW, ROWS), last_hbm))
        )
    ]
    for copy in loads:
        copy.start()
    row = lax.broadcasted_iota(jnp.int32, (PMAX, ROWS), 0)
    frame = lax.broadcasted_iota(jnp.int32, (PMAX, ROWS), 1)
    pick = (frame == row + offset).astype(jnp.bfloat16)
    for part, ref in enumerate(scratch):
        loads[part].wait()
        stores[2 * part].start()
        stores[2 * part + 1].start()
        here = pl.ds(part * BAND, BAND)
        for first in range(0, HEADS, GROUP):
            cols = slice(first * HD, (first + GROUP) * HD)
            rows = nn(pick, ref[:, cols]).astype(jnp.bfloat16)
            for member in range(GROUP):
                piece = rows[:, columns(member)].reshape(BANDS, BAND, HD)
                out_ref[:, first + member, here, :] = piece
        store = pltpu.make_async_copy(
            out_ref.at[:, :, here, :], out_hbm.at[:, :, here, :], out_sems.at[part]
        )
        store.start()
        stores.append(store)
    for store in stores:
        store.wait()


def cut_prompt(starts, key_rows, values):
    return pl.pallas_call(
        cut_kernel,
        out_shape=(
            low_array(BANDS, HEADS, 2 * BAND, HD),
            low_array(2, HW, WIDTH),
            low_array(2, HW, WIDTH),
        ),
        in_specs=[SMEM, HBM, HBM],
        out_specs=(HBM, HBM, HBM),
        scratch_shapes=[
            pltpu.VMEM((ROWS, WIDTH), jnp.bfloat16),
            pltpu.VMEM((ROWS, WIDTH), jnp.bfloat16),
            pltpu.VMEM((BANDS, HEADS, 2 * BAND, HD), jnp.bfloat16),
            pltpu.SemaphoreType.DMA((2,)),
            pltpu.SemaphoreType.DMA((2, 2)),
            pltpu.SemaphoreType.DMA((2,)),
        ],
        compiler_params=FROM_HBM,
        name="cut_prompt",
    )(starts, key_rows, values)


def route_kernel(starts_ref, in_ref, out_ref):
    count = in_ref.shape[0]

    def step(target, source):
        out_ref[target] = in_ref[source]
        return jnp.where(starts_ref[0, target] >= 0, target, source)

    lax.fori_loop(0, count, step, jnp.int32(0), unroll=8)


def route(starts, pieces):
    return pl.pallas_call(
        route_kernel,
        out_shape=jax.ShapeDtypeStruct(pieces.shape, pieces.dtype),
        in_specs=[SMEM, VMEM],
        out_specs=VMEM,
        compiler_params=PARAMS,
        name="route",
    )(starts, pieces)


def gather_kernel(starts_ref, in_ref, out_ref, sums_ref):
    count = in_ref.shape[0]
    out_ref[...] = jnp.zeros_like(out_ref)

    def step(target, carry):
        source, total, sums = carry
        block = in_ref[target].astype(jnp.float32)
        total = total + block[: 2 * BAND]
        sums = sums + block[2 * BAND :]
        out_ref[source] = total.astype(jnp.bfloat16)
        begins = starts_ref[0, target] >= 0
        return jnp.where(begins, target, source), jnp.where(begins, 0.0, total), sums

    sums = in_ref[0].astype(jnp.float32)[2 * BAND :]
    carry = (jnp.int32(0), jnp.zeros((2 * BAND, HD), jnp.float32), sums)
    sums_ref[...] = lax.fori_loop(1, count, step, carry, unroll=7)[2]


def gather(starts, pieces):
    return pl.pallas_call(
        gather_kernel,
        out_shape=(low_array(pieces.shape[0], 2 * BAND, HD), float_array(HEADS, HD)),
        in_specs=[SMEM, VMEM],
        out_specs=(VMEM, VMEM),
        compiler_params=PARAMS,
        name="gather",
    )(starts, pieces)


def carried_prompt(starts_ref, lens_ref, me):
    def later(index, found):
        used = starts_ref[0, index] >= 0
        return (
            jnp.where(used, starts_ref[0, index], found[0]),
            jnp.where(used, lens_ref[0, index], found[1]),
        )

    return lax.fori_loop(0, me, later, (jnp.int32(0), jnp.int32(0)))


def grid_of(keys, rows):
    key = lax.broadcasted_iota(jnp.int32, (keys, rows), 0)
    return key, lax.broadcasted_iota(jnp.int32, (keys, rows), 1)


def hold(ref, allowed):
    ref[...] = jnp.where(allowed, 0.0, NEG)


def hold_masks(starts_ref, lens_ref, own_mask, halo_mask, prompt_mask):
    me = lax.axis_index("ctx")
    last = starts_ref.shape[1] - 1
    begins, offset = own_start(starts_ref, me)
    offset = jnp.where(begins, offset, ROWS)
    own_len = jnp.where(begins, lens_ref[0, me], 0)
    key, row = grid_of(ROWS, ROWS)
    prompt = (key >= offset) & (key < offset + own_len)
    near = jnp.abs(row - key) <= HW
    hold(own_mask.at[0], ((row >= offset) == (key >= offset)) & (prompt | near))
    own_mask[1] = prompt.astype(jnp.float32)
    start, length = carried_prompt(starts_ref, lens_ref, me)
    prompt_end = start + length - (me * ROWS - HW)
    next_begins, next_offset = own_start(starts_ref, jnp.minimum(me + 1, last))
    next_offset = jnp.where(next_begins, next_offset, HW)
    next_offset = jnp.where(me < last, next_offset, 0)
    key, row = grid_of(HW, HW)
    hold(halo_mask.at[0], (key >= row) & (row < offset) & (key >= prompt_end) & (me > 0))
    hold(halo_mask.at[1], (key <= row) & (key < next_offset))
    key, row = grid_of(PMAX, ROWS)
    hold(prompt_mask, (row < offset) & (key < length))


def top_of(x):
    return jnp.max(x, axis=0, keepdims=True)


def sum_of(x):
    return jnp.sum(x, axis=0, keepdims=True)


def window_kernel(
    starts_ref,
    lens_ref,
    bias_ref,
    q_ref,
    d_ref,
    k_ref,
    v_ref,
    low_ref,
    high_ref,
    stats_ref,
    own_mask,
    halo_mask,
    prompt_mask,
):
    head = pl.program_id(0)

    @pl.when(head == 0)
    def _():
        hold_masks(starts_ref, lens_ref, own_mask, halo_mask, prompt_mask)

    q, d, k, v = q_ref[0], d_ref[0], k_ref[0], v_ref[0]
    bias = bias_ref[head] * LOG2E
    flag = own_mask[1]
    x_own = nt(k, q) * FACTOR + (own_mask[0] + flag * bias)
    x_low = nt(low_ref[0], q[:HW]) * FACTOR + halo_mask[0]
    x_high = nt(high_ref[0], q[HW:]) * FACTOR + halo_mask[1]
    tops = jnp.concatenate([top_of(x_low), top_of(x_high)], axis=1)
    top = jnp.maximum(top_of(x_own), tops)
    e_own = jnp.exp2(x_own - top)
    e_low = jnp.exp2(x_low - top[:, :HW])
    e_high = jnp.exp2(x_high - top[:, HW:])
    w_own = e_own * nt(v, d)
    w_low = e_low * nt(low_ref[1], d[:HW])
    w_high = e_high * nt(high_ref[1], d[HW:])
    total = sum_of(e_own) + jnp.concatenate([sum_of(e_low), sum_of(e_high)], axis=1)
    weighted = sum_of(w_own) + jnp.concatenate([sum_of(w_low), sum_of(w_high)], axis=1)
    inverse = 1.0 / total
    own_bias = (sum_of(w_own * flag) - weighted * inverse * sum_of(e_own * flag)) * inverse
    stats_ref[0] = jnp.concatenate(
        [top, total, weighted, own_bias, jnp.zeros((4, ROWS), jnp.float32)], axis=0
    )


def head_rows(part=ROWS):
    return pl.BlockSpec((1, part, HD), lambda head: (0, 0, head))


def head_halo():
    return pl.BlockSpec((2, HW, HD), lambda head: (0, 0, head))


def head_tile(*shape):
    return pl.BlockSpec((1, *shape), lambda head: (head,) + (0,) * len(shape))


def head_pieces():
    return pl.BlockSpec((BANDS, 1, 2 * BAND, HD), lambda head: (0, head, 0, 0))


MASKS = (
    float_array(2, ROWS, ROWS),
    float_array(2, HW, HW),
    float_array(PMAX, ROWS),
)


def whole(array):
    return pl.BlockSpec(array.shape, lambda head: (0,) * len(array.shape))


def cost(micros):
    return pl.CostEstimate(flops=micros * 10**9, bytes_accessed=8 << 20, transcendentals=0)


def window(starts, lens, bias, queries, cotangent, key_rows, values, low, high):
    rows = head_rows()
    return pl.pallas_call(
        window_kernel,
        grid=(HEADS,),
        out_shape=(float_array(HEADS, 8, ROWS), *MASKS),
        in_specs=[SMEM, SMEM, SMEM, rows, rows, rows, rows, head_halo(), head_halo()],
        out_specs=(head_tile(8, ROWS), *(whole(mask) for mask in MASKS)),
        compiler_params=PARAMS,
        cost_estimate=cost(20),
        name="window",
    )(starts, lens, bias, queries, cotangent, key_rows, values, low, high)


def prompt_kernel(
    bias_ref, q_ref, d_ref, prompt_ref, stats_ref, mask_ref, grad_hbm, final_hbm, grad_ref, final_ref, sems
):
    mask = mask_ref[...]
    rows = [(q_ref[0, :, columns(head)], d_ref[0, :, columns(head)]) for head in range(HEADS)]
    all_sums, terms, stores = [], [], []
    for first in range(0, HEADS, STAGED):
        heads = range(first, first + STAGED)
        raw = [
            products(
                prompt_ref[:, head, :BAND, :].reshape(PMAX, HD),
                prompt_ref[:, head, BAND:, :].reshape(PMAX, HD),
                *rows[head],
            )
            for head in heads
        ]
        for head, (scores, dprobs) in zip(heads, raw):
            x = scores * FACTOR + (mask + bias_ref[head] * LOG2E)
            stats = stats_ref[head]
            top = jnp.maximum(stats[0:1], top_of(x))
            rescale = jnp.exp2(stats[0:1] - top)
            raised = jnp.exp2(x - top)
            inverse = 1.0 / (stats[1:2] * rescale + sum_of(raised))
            delta = (stats[2:3] * rescale + sum_of(raised * dprobs)) * inverse
            probs = raised * inverse
            dscores = (probs * SCALE) * (dprobs - delta)
            terms.append((probs.astype(jnp.bfloat16), dscores.astype(jnp.bfloat16)))
            final_ref[head] = jnp.concatenate(
                [top, inverse, delta, jnp.zeros((5, ROWS), jnp.float32)], axis=0
            )
            sums = stats[3:4] + sum_of(dscores) * (1.0 / SCALE)
            all_sums.append(sums[:, :HW] + sums[:, HW:])

    stores.append(pltpu.make_async_copy(final_ref, final_hbm, sems.at[HEADS // STAGED]))
    stores[0].start()
    sums = jnp.concatenate(all_sums, axis=0)
    sums = sums + pltpu.roll(sums, HW // 2, 1)
    upper = sums.astype(jnp.bfloat16).astype(jnp.float32)
    lane = lax.broadcasted_iota(jnp.int32, (HEADS, HW), 1)
    tile = jnp.where(lane < HW // 2, upper, sums - upper).astype(jnp.bfloat16)
    for first in range(0, HEADS, STAGED):
        for head in range(first, first + STAGED):
            (q, d), (low_probs, low_ds) = rows[head], terms[head]
            gk = nn(low_ds, q).astype(jnp.bfloat16)
            gv = nn(low_probs, d).astype(jnp.bfloat16)
            grad_ref[:, head, :BAND, :] = gk.reshape(BANDS, BAND, HD)
            grad_ref[:, head, BAND : 2 * BAND, :] = gv.reshape(BANDS, BAND, HD)
            for band in range(BANDS):
                grad_ref[band, head, 2 * BAND :, :] = tile
        here = pl.ds(first, STAGED)
        store = pltpu.make_async_copy(
            grad_ref.at[:, here], grad_hbm.at[:, here], sems.at[first // STAGED]
        )
        store.start()
        stores.append(store)
    for store in stores:
        store.wait()


def prompt_part(bias, queries, cotangent, prompt, stats, prompt_mask):
    return pl.pallas_call(
        prompt_kernel,
        out_shape=(low_array(BANDS, HEADS, SENT, HD), float_array(HEADS, 8, ROWS)),
        in_specs=[SMEM, VMEM, VMEM, VMEM, VMEM, VMEM],
        out_specs=(HBM, HBM),
        scratch_shapes=[
            pltpu.VMEM((BANDS, HEADS, SENT, HD), jnp.bfloat16),
            pltpu.VMEM((HEADS, 8, ROWS), jnp.float32),
            pltpu.SemaphoreType.DMA((HEADS // STAGED + 1,)),
        ],
        compiler_params=PARAMS,
        cost_estimate=cost(4),
        name="prompt_part",
    )(bias, queries, cotangent, prompt, stats, prompt_mask)


def products(keys, values, q, d):
    return nt(keys, q), nt(values, d)


def settled(scores, dprobs, added, final):
    probs = jnp.exp2(scores * FACTOR + (added - final[0:1])) * final[1:2]
    dscores = (probs * SCALE) * (dprobs - final[2:3])
    return probs.astype(jnp.bfloat16), dscores.astype(jnp.bfloat16)


def halo_kernel(q_ref, d_ref, low_ref, high_ref, final_ref, mask_ref, glow_ref, ghigh_ref):
    sides = ((low_ref, glow_ref), (high_ref, ghigh_ref))
    for first in range(0, HEADS, STAGED):
        places = [
            (half, slice(half * HW, (half + 1) * HW), head)
            for head in range(first, first + STAGED)
            for half in range(2)
        ]
        rows = [
            (q_ref[0, part, columns(head)], d_ref[0, part, columns(head)])
            for _, part, head in places
        ]
        raw = [
            products(sides[half][0][0, :, columns(head)], sides[half][0][1, :, columns(head)], q, d)
            for (half, _, head), (q, d) in zip(places, rows)
        ]
        terms = [
            settled(*pair, mask_ref[half], final_ref[head, :, part])
            for (half, part, head), pair in zip(places, raw)
        ]
        for (half, _, head), (q, d), (probs, ds) in zip(places, rows, terms):
            out = sides[half][1]
            out[0, :, columns(head)] = nn(ds, q).astype(jnp.bfloat16)
            out[1, :, columns(head)] = nn(probs, d).astype(jnp.bfloat16)


def halo_grads(queries, cotangent, low, high, final, halo_mask):
    return pl.pallas_call(
        halo_kernel,
        out_shape=(low_array(2, HW, WIDTH), low_array(2, HW, WIDTH)),
        in_specs=[VMEM] * 6,
        out_specs=(VMEM, VMEM),
        compiler_params=PARAMS,
        cost_estimate=cost(4),
        name="halo_grads",
    )(queries, cotangent, low, high, final, halo_mask)


def own_kernel(
    bias_ref,
    q_ref,
    d_ref,
    k_ref,
    v_ref,
    low_ref,
    high_ref,
    prompt_ref,
    final_ref,
    own_mask,
    halo_mask,
    prompt_mask,
    attended_ref,
    gq_ref,
    gk_ref,
    gv_ref,
):
    members = range(GROUP)
    step = pl.program_id(0)
    blocks = []
    for member in members:
        cols = columns(member)
        q, d = q_ref[0, :, cols], d_ref[0, :, cols]
        kp = prompt_ref[:, member, :BAND, :].reshape(PMAX, HD)
        vp = prompt_ref[:, member, BAND:, :].reshape(PMAX, HD)
        blocks.append(
            (
                (k_ref[0, :, cols], v_ref[0, :, cols], q, d),
                (kp, vp, q, d),
                (low_ref[0, :, cols], low_ref[1, :, cols], q[:HW], d[:HW]),
                (high_ref[0, :, cols], high_ref[1, :, cols], q[HW:], d[HW:]),
            )
        )
    raw = [[products(*block) for block in parts] for parts in blocks]
    terms = []
    for member in members:
        bias = bias_ref[step * GROUP + member] * LOG2E
        final = final_ref[member]
        added = (
            own_mask[0] + own_mask[1] * bias,
            prompt_mask[...] + bias,
            halo_mask[0],
            halo_mask[1],
        )
        finals = (final, final, final[:, :HW], final[:, HW:])
        terms.append(
            [settled(*pair, x, y) for pair, x, y in zip(raw[member], added, finals)]
        )
    for member in members:
        cols = columns(member)
        own, prompt, low, high = blocks[member]
        (probs, ds), (probs_p, ds_p), (probs_l, ds_l), (probs_h, ds_h) = terms[member]
        gk_ref[:, cols] = nn(ds, own[2])
        gv_ref[:, cols] = nn(probs, own[3])
        attended = tn(probs, own[1]) + tn(probs_p, prompt[1])
        attended += jnp.concatenate([tn(probs_l, low[1]), tn(probs_h, high[1])], axis=0)
        attended_ref[0, :, cols] = attended.astype(jnp.bfloat16)
        grad_q = tn(ds, own[0]) + tn(ds_p, prompt[0])
        grad_q += jnp.concatenate([tn(ds_l, low[0]), tn(ds_h, high[0])], axis=0)
        gq_ref[0, :, cols] = grad_q.astype(jnp.bfloat16)


def own_part(bias, queries, cotangent, key_rows, values, low, high, prompt, final, masks):
    rows = pl.BlockSpec((1, ROWS, GROUP * HD), lambda step: (0, 0, step))
    halo = pl.BlockSpec((2, HW, GROUP * HD), lambda step: (0, 0, step))
    pieces = pl.BlockSpec((BANDS, GROUP, 2 * BAND, HD), lambda step: (0, step, 0, 0))
    tile = pl.BlockSpec((GROUP, 8, ROWS), lambda step: (step, 0, 0))
    total = pl.BlockSpec((ROWS, GROUP * HD), lambda step: (0, step))
    return pl.pallas_call(
        own_kernel,
        grid=(HEADS // GROUP,),
        out_shape=(
            low_array(1, ROWS, WIDTH),
            low_array(1, ROWS, WIDTH),
            float_array(ROWS, WIDTH),
            float_array(ROWS, WIDTH),
        ),
        in_specs=[SMEM, rows, rows, rows, rows, halo, halo, pieces, tile]
        + [whole(mask) for mask in MASKS],
        out_specs=(rows, rows, total, total),
        compiler_params=NEARLY,
        cost_estimate=cost(10),
        name="own_part",
    )(bias, queries, cotangent, key_rows, values, low, high, prompt, final, *masks)


def merge_kernel(gk_ref, gv_ref, left_ref, right_ref, outk_ref, outv_ref, sums_ref):
    for part, (ref, out) in enumerate(((gk_ref, outk_ref), (gv_ref, outv_ref))):
        for half, side in enumerate((left_ref, right_ref)):
            rows = slice(half * HW, (half + 1) * HW)
            total = ref[rows, :] + side[part].astype(jnp.float32)
            sums_ref[part, rows, :] = total
            out[0, rows, :] = total.astype(jnp.bfloat16)


def merge(gk, gv, left, right):
    total = pl.BlockSpec((ROWS, GROUP * HD), lambda step: (0, step))
    rows = pl.BlockSpec((1, ROWS, GROUP * HD), lambda step: (0, 0, step))
    side = pl.BlockSpec((2, HW, GROUP * HD), lambda step: (0, 0, step))
    both = pl.BlockSpec((2, ROWS, GROUP * HD), lambda step: (0, 0, step))
    return pl.pallas_call(
        merge_kernel,
        grid=(HEADS // GROUP,),
        out_shape=(low_array(1, ROWS, WIDTH),) * 2 + (float_array(2, ROWS, WIDTH),),
        in_specs=[total, total, side, side],
        out_specs=(rows, rows, both),
        compiler_params=NEARLY,
        cost_estimate=cost(MERGE),
        name="merge",
    )(gk, gv, left, right)


def finish_kernel(
    starts_ref,
    sums_hbm,
    prompt_ref,
    _ink,
    _inv,
    outk_hbm,
    outv_hbm,
    sums_ref,
    rows_ref,
    load_sems,
    store_sems,
):
    me = lax.axis_index("ctx")
    begins, offset = own_start(starts_ref, me)

    @pl.when(begins)
    def _():
        base = pl.multiple_of(jnp.minimum(offset // BAND * BAND, ROWS - SPAN), BAND)
        span = pl.ds(base, SPAN)
        loads = [
            pltpu.make_async_copy(sums_hbm.at[part, span, :], sums_ref.at[part], load_sems.at[part])
            for part in range(2)
        ]
        stores = [
            pltpu.make_async_copy(rows_ref.at[part], ref.at[0, span, :], store_sems.at[part])
            for part, ref in enumerate((outk_hbm, outv_hbm))
        ]
        for copy in loads:
            copy.start()
        frame, row = grid_of(SPAN, PMAX)
        place = (frame == row + (offset - base)).astype(jnp.bfloat16)
        for part in range(2):
            loads[part].wait()
            for head in range(HEADS):
                cols = columns(head)
                piece = prompt_ref[:, head, part * BAND : (part + 1) * BAND, :].reshape(PMAX, HD)
                total = sums_ref[part, :, cols] + nn(place, piece)
                rows_ref[part, :, cols] = total.astype(jnp.bfloat16)
            stores[part].start()
        for copy in stores:
            copy.wait()


def finish(starts, outk, outv, sums, prompt):
    return pl.pallas_call(
        finish_kernel,
        out_shape=(low_array(1, ROWS, WIDTH),) * 2,
        in_specs=[SMEM, HBM, VMEM, HBM, HBM],
        out_specs=(HBM, HBM),
        input_output_aliases={3: 0, 4: 1},
        scratch_shapes=[
            pltpu.VMEM((2, SPAN, WIDTH), jnp.float32),
            pltpu.VMEM((2, SPAN, WIDTH), jnp.bfloat16),
            pltpu.SemaphoreType.DMA((2,)),
            pltpu.SemaphoreType.DMA((2,)),
        ],
        compiler_params=NEARLY,
        name="finish",
    )(starts, sums, prompt, outk, outv)


def exchange(pieces):
    return lax.all_to_all(pieces, "ctx", 0, 0, tiled=True)


def shifted(x, by):
    peers = lax.axis_size("ctx")
    return lax.ppermute(x, "ctx", [(i, i + by) for i in range(peers) if 0 <= i + by < peers])


def partners(x, axis, steps):
    peers = lax.axis_size(axis)
    return [lax.ppermute(x, axis, [(i, i ^ step) for i in range(peers)]) for step in steps]


def summed(x, axis, low, high):
    first, second, third = partners(x, axis, (low, high, low | high))
    return (x + first) + (second + third)


def local(queries, key_rows, values, cotangent, starts, lens, bias):
    count = lax.axis_size("ctx")
    cut, last, first = cut_prompt(starts, key_rows, values)
    held = exchange(cut.reshape(count, 2 * BAND, HD))
    low = shifted(last, 1)
    high = shifted(first, -1)
    stats, *masks = window(
        starts, lens, bias, queries, cotangent, key_rows, values, low, high
    )
    prompt = exchange(route(starts, held)).reshape(BANDS, HEADS, 2 * BAND, HD)
    gprompt, final = prompt_part(bias, queries, cotangent, prompt, stats, masks[2])
    held = exchange(gprompt.reshape(count, SENT, HD))
    attended, grad_q, gk, gv = own_part(
        bias, queries, cotangent, key_rows, values, low, high, prompt, final, masks
    )
    final, gk = lax.optimization_barrier((final, gk))
    glow, ghigh = halo_grads(queries, cotangent, low, high, final, masks[1])
    right = shifted(glow, -1)
    left = shifted(ghigh, 1)
    held, glow, ghigh = lax.optimization_barrier((held, glow, ghigh))
    owned, sums = gather(starts, held)
    returned = exchange(owned).reshape(BANDS, HEADS, 2 * BAND, HD)
    grad_bias = jnp.sum(summed(sums, "dp", 1, 2), axis=1)
    outk, outv, both = merge(gk, gv, left, right)
    grad_k, grad_v = finish(starts, outk, outv, both, returned)
    return attended, grad_q, grad_k, grad_v, grad_bias


def solution(mesh):
    split = P("dp", "ctx", None)
    return jax.shard_map(
        local,
        mesh=mesh,
        in_specs=(split, split, split, split, P("dp", None), P("dp", None), P()),
        out_specs=(split, split, split, split, P()),
        check_vma=False,
    )
```

```python
import math

import jax
import jax.numpy as jnp
from jax import lax
from jax.experimental import pallas as pl
from jax.experimental.pallas import tpu as pltpu
from jax.sharding import PartitionSpec as P

HW = 128
PMAX = 128
ROWS = 256
HD = 128
HEADS = 8
WIDTH = HEADS * HD
BANDS = 8
BAND = PMAX // BANDS
SENT = 2 * BAND + HEADS
SPAN = PMAX + BAND
GROUP = 2
STAGED = 4
MERGE = 8
NEG = -1e30
LOG2E = math.log2(math.e)
SCALE = 1.0 / math.sqrt(HD)
FACTOR = SCALE * LOG2E

SMEM = pl.BlockSpec(memory_space=pltpu.SMEM)
VMEM = pl.BlockSpec(memory_space=pltpu.VMEM)
HBM = pl.BlockSpec(memory_space=pltpu.HBM)
PARAMS = pltpu.CompilerParams(vmem_limit_bytes=20 * 1024 * 1024)
FROM_HBM = pltpu.CompilerParams(vmem_limit_bytes=60 * 1024 * 1024)
NEARLY = pltpu.CompilerParams(vmem_limit_bytes=52 * 1024 * 1024)


def nt(a, b):
    return lax.dot_general(a, b, (((1,), (1,)), ((), ())), preferred_element_type=jnp.float32)


def tn(a, b):
    return lax.dot_general(a, b, (((0,), (0,)), ((), ())), preferred_element_type=jnp.float32)


def nn(a, b):
    return lax.dot_general(a, b, (((1,), (0,)), ((), ())), preferred_element_type=jnp.float32)


def own_start(starts_ref, me):
    start = starts_ref[0, me]
    return start >= 0, jnp.where(start >= 0, start - me * ROWS, 0)


def columns(head):
    return slice(head * HD, (head + 1) * HD)


def float_array(*shape):
    return jax.ShapeDtypeStruct(shape, jnp.float32)


def low_array(*shape):
    return jax.ShapeDtypeStruct(shape, jnp.bfloat16)


def cut_kernel(
    starts_ref,
    k_hbm,
    v_hbm,
    out_hbm,
    last_hbm,
    first_hbm,
    k_ref,
    v_ref,
    out_ref,
    sems,
    edge_sems,
    out_sems,
):
    me = lax.axis_index("ctx")
    offset = own_start(starts_ref, me)[1]
    sources = (k_hbm, v_hbm)
    scratch = (k_ref, v_ref)
    loads = [
        pltpu.make_async_copy(source.at[0], ref, sems.at[part])
        for part, (source, ref) in enumerate(zip(sources, scratch))
    ]
    stores = [
        pltpu.make_async_copy(ref.at[rows, :], target.at[part], edge_sems.at[part, half])
        for part, ref in enumerate(scratch)
        for half, (rows, target) in enumerate(
            ((slice(0, HW), first_hbm), (slice(HW, ROWS), last_hbm))
        )
    ]
    for copy in loads:
        copy.start()
    row = lax.broadcasted_iota(jnp.int32, (PMAX, ROWS), 0)
    frame = lax.broadcasted_iota(jnp.int32, (PMAX, ROWS), 1)
    pick = (frame == row + offset).astype(jnp.bfloat16)
    for part, ref in enumerate(scratch):
        loads[part].wait()
        stores[2 * part].start()
        stores[2 * part + 1].start()
        here = pl.ds(part * BAND, BAND)
        for first in range(0, HEADS, GROUP):
            cols = slice(first * HD, (first + GROUP) * HD)
            rows = nn(pick, ref[:, cols]).astype(jnp.bfloat16)
            for member in range(GROUP):
                piece = rows[:, columns(member)].reshape(BANDS, BAND, HD)
                out_ref[:, first + member, here, :] = piece
        store = pltpu.make_async_copy(
            out_ref.at[:, :, here, :], out_hbm.at[:, :, here, :], out_sems.at[part]
        )
        store.start()
        stores.append(store)
    for store in stores:
        store.wait()


def cut_prompt(starts, key_rows, values):
    return pl.pallas_call(
        cut_kernel,
        out_shape=(
            low_array(BANDS, HEADS, 2 * BAND, HD),
            low_array(2, HW, WIDTH),
            low_array(2, HW, WIDTH),
        ),
        in_specs=[SMEM, HBM, HBM],
        out_specs=(HBM, HBM, HBM),
        scratch_shapes=[
            pltpu.VMEM((ROWS, WIDTH), jnp.bfloat16),
            pltpu.VMEM((ROWS, WIDTH), jnp.bfloat16),
            pltpu.VMEM((BANDS, HEADS, 2 * BAND, HD), jnp.bfloat16),
            pltpu.SemaphoreType.DMA((2,)),
            pltpu.SemaphoreType.DMA((2, 2)),
            pltpu.SemaphoreType.DMA((2,)),
        ],
        compiler_params=FROM_HBM,
        name="cut_prompt",
    )(starts, key_rows, values)


def route_kernel(starts_ref, in_ref, out_ref):
    count = in_ref.shape[0]

    def step(target, source):
        out_ref[target] = in_ref[source]
        return jnp.where(starts_ref[0, target] >= 0, target, source)

    lax.fori_loop(0, count, step, jnp.int32(0), unroll=8)


def route(starts, pieces):
    return pl.pallas_call(
        route_kernel,
        out_shape=jax.ShapeDtypeStruct(pieces.shape, pieces.dtype),
        in_specs=[SMEM, VMEM],
        out_specs=VMEM,
        compiler_params=PARAMS,
        name="route",
    )(starts, pieces)


def gather_kernel(starts_ref, in_ref, out_ref, sums_ref):
    count = in_ref.shape[0]
    out_ref[...] = jnp.zeros_like(out_ref)

    def step(target, carry):
        source, total, sums = carry
        block = in_ref[target].astype(jnp.float32)
        total = total + block[: 2 * BAND]
        sums = sums + block[2 * BAND :]
        out_ref[source] = total.astype(jnp.bfloat16)
        begins = starts_ref[0, target] >= 0
        return jnp.where(begins, target, source), jnp.where(begins, 0.0, total), sums

    sums = in_ref[0].astype(jnp.float32)[2 * BAND :]
    carry = (jnp.int32(0), jnp.zeros((2 * BAND, HD), jnp.float32), sums)
    sums_ref[...] = lax.fori_loop(1, count, step, carry, unroll=7)[2]


def gather(starts, pieces):
    return pl.pallas_call(
        gather_kernel,
        out_shape=(low_array(pieces.shape[0], 2 * BAND, HD), float_array(HEADS, HD)),
        in_specs=[SMEM, VMEM],
        out_specs=(VMEM, VMEM),
        compiler_params=PARAMS,
        name="gather",
    )(starts, pieces)


def carried_prompt(starts_ref, lens_ref, me):
    def later(index, found):
        used = starts_ref[0, index] >= 0
        return (
            jnp.where(used, starts_ref[0, index], found[0]),
            jnp.where(used, lens_ref[0, index], found[1]),
        )

    return lax.fori_loop(0, me, later, (jnp.int32(0), jnp.int32(0)))


def grid_of(keys, rows):
    key = lax.broadcasted_iota(jnp.int32, (keys, rows), 0)
    return key, lax.broadcasted_iota(jnp.int32, (keys, rows), 1)


def hold(ref, allowed):
    ref[...] = jnp.where(allowed, 0.0, NEG)


def hold_masks(starts_ref, lens_ref, own_mask, halo_mask, prompt_mask):
    me = lax.axis_index("ctx")
    last = starts_ref.shape[1] - 1
    begins, offset = own_start(starts_ref, me)
    offset = jnp.where(begins, offset, ROWS)
    own_len = jnp.where(begins, lens_ref[0, me], 0)
    key, row = grid_of(ROWS, ROWS)
    prompt = (key >= offset) & (key < offset + own_len)
    near = jnp.abs(row - key) <= HW
    hold(own_mask.at[0], ((row >= offset) == (key >= offset)) & (prompt | near))
    own_mask[1] = prompt.astype(jnp.float32)
    start, length = carried_prompt(starts_ref, lens_ref, me)
    prompt_end = start + length - (me * ROWS - HW)
    next_begins, next_offset = own_start(starts_ref, jnp.minimum(me + 1, last))
    next_offset = jnp.where(next_begins, next_offset, HW)
    next_offset = jnp.where(me < last, next_offset, 0)
    key, row = grid_of(HW, HW)
    hold(halo_mask.at[0], (key >= row) & (row < offset) & (key >= prompt_end) & (me > 0))
    hold(halo_mask.at[1], (key <= row) & (key < next_offset))
    key, row = grid_of(PMAX, ROWS)
    hold(prompt_mask, (row < offset) & (key < length))


def top_of(x):
    return jnp.max(x, axis=0, keepdims=True)


def sum_of(x):
    return jnp.sum(x, axis=0, keepdims=True)


def window_kernel(
    starts_ref,
    lens_ref,
    bias_ref,
    q_ref,
    d_ref,
    k_ref,
    v_ref,
    low_ref,
    high_ref,
    stats_ref,
    own_mask,
    halo_mask,
    prompt_mask,
):
    head = pl.program_id(0)

    @pl.when(head == 0)
    def _():
        hold_masks(starts_ref, lens_ref, own_mask, halo_mask, prompt_mask)

    q, d, k, v = q_ref[0], d_ref[0], k_ref[0], v_ref[0]
    bias = bias_ref[head] * LOG2E
    flag = own_mask[1]
    x_own = nt(k, q) * FACTOR + (own_mask[0] + flag * bias)
    x_low = nt(low_ref[0], q[:HW]) * FACTOR + halo_mask[0]
    x_high = nt(high_ref[0], q[HW:]) * FACTOR + halo_mask[1]
    tops = jnp.concatenate([top_of(x_low), top_of(x_high)], axis=1)
    top = jnp.maximum(top_of(x_own), tops)
    e_own = jnp.exp2(x_own - top)
    e_low = jnp.exp2(x_low - top[:, :HW])
    e_high = jnp.exp2(x_high - top[:, HW:])
    w_own = e_own * nt(v, d)
    w_low = e_low * nt(low_ref[1], d[:HW])
    w_high = e_high * nt(high_ref[1], d[HW:])
    total = sum_of(e_own) + jnp.concatenate([sum_of(e_low), sum_of(e_high)], axis=1)
    weighted = sum_of(w_own) + jnp.concatenate([sum_of(w_low), sum_of(w_high)], axis=1)
    inverse = 1.0 / total
    own_bias = (sum_of(w_own * flag) - weighted * inverse * sum_of(e_own * flag)) * inverse
    stats_ref[0] = jnp.concatenate(
        [top, total, weighted, own_bias, jnp.zeros((4, ROWS), jnp.float32)], axis=0
    )


def head_rows(part=ROWS):
    return pl.BlockSpec((1, part, HD), lambda head: (0, 0, head))


def head_halo():
    return pl.BlockSpec((2, HW, HD), lambda head: (0, 0, head))


def head_tile(*shape):
    return pl.BlockSpec((1, *shape), lambda head: (head,) + (0,) * len(shape))


def head_pieces():
    return pl.BlockSpec((BANDS, 1, 2 * BAND, HD), lambda head: (0, head, 0, 0))


MASKS = (
    float_array(2, ROWS, ROWS),
    float_array(2, HW, HW),
    float_array(PMAX, ROWS),
)


def whole(array):
    return pl.BlockSpec(array.shape, lambda head: (0,) * len(array.shape))


def cost(micros):
    return pl.CostEstimate(flops=micros * 10**9, bytes_accessed=8 << 20, transcendentals=0)


def window(starts, lens, bias, queries, cotangent, key_rows, values, low, high):
    rows = head_rows()
    return pl.pallas_call(
        window_kernel,
        grid=(HEADS,),
        out_shape=(float_array(HEADS, 8, ROWS), *MASKS),
        in_specs=[SMEM, SMEM, SMEM, rows, rows, rows, rows, head_halo(), head_halo()],
        out_specs=(head_tile(8, ROWS), *(whole(mask) for mask in MASKS)),
        compiler_params=PARAMS,
        cost_estimate=cost(20),
        name="window",
    )(starts, lens, bias, queries, cotangent, key_rows, values, low, high)


def prompt_kernel(
    bias_ref, q_ref, d_ref, prompt_ref, stats_ref, mask_ref, grad_hbm, final_hbm, grad_ref, final_ref, sems
):
    mask = mask_ref[...]
    rows = [(q_ref[0, :, columns(head)], d_ref[0, :, columns(head)]) for head in range(HEADS)]
    all_sums, terms, stores = [], [], []
    for first in range(0, HEADS, STAGED):
        heads = range(first, first + STAGED)
        raw = [
            products(
                prompt_ref[:, head, :BAND, :].reshape(PMAX, HD),
                prompt_ref[:, head, BAND:, :].reshape(PMAX, HD),
                *rows[head],
            )
            for head in heads
        ]
        for head, (scores, dprobs) in zip(heads, raw):
            x = scores * FACTOR + (mask + bias_ref[head] * LOG2E)
            stats = stats_ref[head]
            top = jnp.maximum(stats[0:1], top_of(x))
            rescale = jnp.exp2(stats[0:1] - top)
            raised = jnp.exp2(x - top)
            inverse = 1.0 / (stats[1:2] * rescale + sum_of(raised))
            delta = (stats[2:3] * rescale + sum_of(raised * dprobs)) * inverse
            probs = raised * inverse
            dscores = (probs * SCALE) * (dprobs - delta)
            terms.append((probs.astype(jnp.bfloat16), dscores.astype(jnp.bfloat16)))
            final_ref[head] = jnp.concatenate(
                [top, inverse, delta, jnp.zeros((5, ROWS), jnp.float32)], axis=0
            )
            sums = stats[3:4] + sum_of(dscores) * (1.0 / SCALE)
            all_sums.append(sums[:, :HW] + sums[:, HW:])

    stores.append(pltpu.make_async_copy(final_ref, final_hbm, sems.at[HEADS // STAGED]))
    stores[0].start()
    sums = jnp.concatenate(all_sums, axis=0)
    sums = sums + pltpu.roll(sums, HW // 2, 1)
    upper = sums.astype(jnp.bfloat16).astype(jnp.float32)
    lane = lax.broadcasted_iota(jnp.int32, (HEADS, HW), 1)
    tile = jnp.where(lane < HW // 2, upper, sums - upper).astype(jnp.bfloat16)
    for first in range(0, HEADS, STAGED):
        for head in range(first, first + STAGED):
            (q, d), (low_probs, low_ds) = rows[head], terms[head]
            gk = nn(low_ds, q).astype(jnp.bfloat16)
            gv = nn(low_probs, d).astype(jnp.bfloat16)
            grad_ref[:, head, :BAND, :] = gk.reshape(BANDS, BAND, HD)
            grad_ref[:, head, BAND : 2 * BAND, :] = gv.reshape(BANDS, BAND, HD)
            for band in range(BANDS):
                grad_ref[band, head, 2 * BAND :, :] = tile
        here = pl.ds(first, STAGED)
        store = pltpu.make_async_copy(
            grad_ref.at[:, here], grad_hbm.at[:, here], sems.at[first // STAGED]
        )
        store.start()
        stores.append(store)
    for store in stores:
        store.wait()


def prompt_part(bias, queries, cotangent, prompt, stats, prompt_mask):
    return pl.pallas_call(
        prompt_kernel,
        out_shape=(low_array(BANDS, HEADS, SENT, HD), float_array(HEADS, 8, ROWS)),
        in_specs=[SMEM, VMEM, VMEM, VMEM, VMEM, VMEM],
        out_specs=(HBM, HBM),
        scratch_shapes=[
            pltpu.VMEM((BANDS, HEADS, SENT, HD), jnp.bfloat16),
            pltpu.VMEM((HEADS, 8, ROWS), jnp.float32),
            pltpu.SemaphoreType.DMA((HEADS // STAGED + 1,)),
        ],
        compiler_params=PARAMS,
        cost_estimate=cost(4),
        name="prompt_part",
    )(bias, queries, cotangent, prompt, stats, prompt_mask)


def products(keys, values, q, d):
    return nt(keys, q), nt(values, d)


def settled(scores, dprobs, added, final):
    probs = jnp.exp2(scores * FACTOR + (added - final[0:1])) * final[1:2]
    dscores = (probs * SCALE) * (dprobs - final[2:3])
    return probs.astype(jnp.bfloat16), dscores.astype(jnp.bfloat16)


def halo_kernel(q_ref, d_ref, low_ref, high_ref, final_ref, mask_ref, glow_ref, ghigh_ref):
    sides = ((low_ref, glow_ref), (high_ref, ghigh_ref))
    for first in range(0, HEADS, STAGED):
        places = [
            (half, slice(half * HW, (half + 1) * HW), head)
            for head in range(first, first + STAGED)
            for half in range(2)
        ]
        rows = [
            (q_ref[0, part, columns(head)], d_ref[0, part, columns(head)])
            for _, part, head in places
        ]
        raw = [
            products(sides[half][0][0, :, columns(head)], sides[half][0][1, :, columns(head)], q, d)
            for (half, _, head), (q, d) in zip(places, rows)
        ]
        terms = [
            settled(*pair, mask_ref[half], final_ref[head, :, part])
            for (half, part, head), pair in zip(places, raw)
        ]
        for (half, _, head), (q, d), (probs, ds) in zip(places, rows, terms):
            out = sides[half][1]
            out[0, :, columns(head)] = nn(ds, q).astype(jnp.bfloat16)
            out[1, :, columns(head)] = nn(probs, d).astype(jnp.bfloat16)


def halo_grads(queries, cotangent, low, high, final, halo_mask):
    return pl.pallas_call(
        halo_kernel,
        out_shape=(low_array(2, HW, WIDTH), low_array(2, HW, WIDTH)),
        in_specs=[VMEM] * 6,
        out_specs=(VMEM, VMEM),
        compiler_params=PARAMS,
        cost_estimate=cost(4),
        name="halo_grads",
    )(queries, cotangent, low, high, final, halo_mask)


def own_kernel(
    bias_ref,
    q_ref,
    d_ref,
    k_ref,
    v_ref,
    low_ref,
    high_ref,
    prompt_ref,
    final_ref,
    own_mask,
    halo_mask,
    prompt_mask,
    attended_ref,
    gq_ref,
    gk_ref,
    gv_ref,
):
    members = range(GROUP)
    step = pl.program_id(0)
    blocks = []
    for member in members:
        cols = columns(member)
        q, d = q_ref[0, :, cols], d_ref[0, :, cols]
        kp = prompt_ref[:, member, :BAND, :].reshape(PMAX, HD)
        vp = prompt_ref[:, member, BAND:, :].reshape(PMAX, HD)
        blocks.append(
            (
                (k_ref[0, :, cols], v_ref[0, :, cols], q, d),
                (kp, vp, q, d),
                (low_ref[0, :, cols], low_ref[1, :, cols], q[:HW], d[:HW]),
                (high_ref[0, :, cols], high_ref[1, :, cols], q[HW:], d[HW:]),
            )
        )
    raw = [[products(*block) for block in parts] for parts in blocks]
    terms = []
    for member in members:
        bias = bias_ref[step * GROUP + member] * LOG2E
        final = final_ref[member]
        added = (
            own_mask[0] + own_mask[1] * bias,
            prompt_mask[...] + bias,
            halo_mask[0],
            halo_mask[1],
        )
        finals = (final, final, final[:, :HW], final[:, HW:])
        terms.append(
            [settled(*pair, x, y) for pair, x, y in zip(raw[member], added, finals)]
        )
    for member in members:
        cols = columns(member)
        own, prompt, low, high = blocks[member]
        (probs, ds), (probs_p, ds_p), (probs_l, ds_l), (probs_h, ds_h) = terms[member]
        gk_ref[:, cols] = nn(ds, own[2])
        gv_ref[:, cols] = nn(probs, own[3])
        attended = tn(probs, own[1]) + tn(probs_p, prompt[1])
        attended += jnp.concatenate([tn(probs_l, low[1]), tn(probs_h, high[1])], axis=0)
        attended_ref[0, :, cols] = attended.astype(jnp.bfloat16)
        grad_q = tn(ds, own[0]) + tn(ds_p, prompt[0])
        grad_q += jnp.concatenate([tn(ds_l, low[0]), tn(ds_h, high[0])], axis=0)
        gq_ref[0, :, cols] = grad_q.astype(jnp.bfloat16)


def own_part(bias, queries, cotangent, key_rows, values, low, high, prompt, final, masks):
    rows = pl.BlockSpec((1, ROWS, GROUP * HD), lambda step: (0, 0, step))
    halo = pl.BlockSpec((2, HW, GROUP * HD), lambda step: (0, 0, step))
    pieces = pl.BlockSpec((BANDS, GROUP, 2 * BAND, HD), lambda step: (0, step, 0, 0))
    tile = pl.BlockSpec((GROUP, 8, ROWS), lambda step: (step, 0, 0))
    total = pl.BlockSpec((ROWS, GROUP * HD), lambda step: (0, step))
    return pl.pallas_call(
        own_kernel,
        grid=(HEADS // GROUP,),
        out_shape=(
            low_array(1, ROWS, WIDTH),
            low_array(1, ROWS, WIDTH),
            float_array(ROWS, WIDTH),
            float_array(ROWS, WIDTH),
        ),
        in_specs=[SMEM, rows, rows, rows, rows, halo, halo, pieces, tile]
        + [whole(mask) for mask in MASKS],
        out_specs=(rows, rows, total, total),
        compiler_params=NEARLY,
        cost_estimate=cost(10),
        name="own_part",
    )(bias, queries, cotangent, key_rows, values, low, high, prompt, final, *masks)


def merge_kernel(right_ref, left_ref, gk_ref, gv_ref, outk_ref, outv_ref, sums_ref):
    for part, (ref, out) in enumerate(((gk_ref, outk_ref), (gv_ref, outv_ref))):
        for half, side in enumerate((left_ref, right_ref)):
            rows = slice(half * HW, (half + 1) * HW)
            total = ref[rows, :] + side[part].astype(jnp.float32)
            sums_ref[part, rows, :] = total
            out[0, rows, :] = total.astype(jnp.bfloat16)


def merge(gk, gv, left, right):
    total = pl.BlockSpec((ROWS, GROUP * HD), lambda step: (0, step))
    rows = pl.BlockSpec((1, ROWS, GROUP * HD), lambda step: (0, 0, step))
    side = pl.BlockSpec((2, HW, GROUP * HD), lambda step: (0, 0, step))
    both = pl.BlockSpec((2, ROWS, GROUP * HD), lambda step: (0, 0, step))
    return pl.pallas_call(
        merge_kernel,
        grid=(HEADS // GROUP,),
        out_shape=(low_array(1, ROWS, WIDTH),) * 2 + (float_array(2, ROWS, WIDTH),),
        in_specs=[side, side, total, total],
        out_specs=(rows, rows, both),
        compiler_params=NEARLY,
        cost_estimate=cost(MERGE),
        name="merge",
    )(right, left, gk, gv)


def finish_kernel(
    starts_ref,
    sums_hbm,
    prompt_ref,
    _ink,
    _inv,
    outk_hbm,
    outv_hbm,
    sums_ref,
    rows_ref,
    load_sems,
    store_sems,
):
    me = lax.axis_index("ctx")
    begins, offset = own_start(starts_ref, me)

    @pl.when(begins)
    def _():
        base = pl.multiple_of(jnp.minimum(offset // BAND * BAND, ROWS - SPAN), BAND)
        span = pl.ds(base, SPAN)
        loads = [
            pltpu.make_async_copy(sums_hbm.at[part, span, :], sums_ref.at[part], load_sems.at[part])
            for part in range(2)
        ]
        stores = [
            pltpu.make_async_copy(rows_ref.at[part], ref.at[0, span, :], store_sems.at[part])
            for part, ref in enumerate((outk_hbm, outv_hbm))
        ]
        for copy in loads:
            copy.start()
        frame, row = grid_of(SPAN, PMAX)
        place = (frame == row + (offset - base)).astype(jnp.bfloat16)
        for part in range(2):
            loads[part].wait()
            for head in range(HEADS):
                cols = columns(head)
                piece = prompt_ref[:, head, part * BAND : (part + 1) * BAND, :].reshape(PMAX, HD)
                total = sums_ref[part, :, cols] + nn(place, piece)
                rows_ref[part, :, cols] = total.astype(jnp.bfloat16)
            stores[part].start()
        for copy in stores:
            copy.wait()


def finish(starts, outk, outv, sums, prompt):
    return pl.pallas_call(
        finish_kernel,
        out_shape=(low_array(1, ROWS, WIDTH),) * 2,
        in_specs=[SMEM, HBM, VMEM, HBM, HBM],
        out_specs=(HBM, HBM),
        input_output_aliases={3: 0, 4: 1},
        scratch_shapes=[
            pltpu.VMEM((2, SPAN, WIDTH), jnp.float32),
            pltpu.VMEM((2, SPAN, WIDTH), jnp.bfloat16),
            pltpu.SemaphoreType.DMA((2,)),
            pltpu.SemaphoreType.DMA((2,)),
        ],
        compiler_params=NEARLY,
        name="finish",
    )(starts, sums, prompt, outk, outv)


def exchange(pieces):
    return lax.all_to_all(pieces, "ctx", 0, 0, tiled=True)


def shifted(x, by):
    peers = lax.axis_size("ctx")
    return lax.ppermute(x, "ctx", [(i, i + by) for i in range(peers) if 0 <= i + by < peers])


def partners(x, axis, steps):
    peers = lax.axis_size(axis)
    return [lax.ppermute(x, axis, [(i, i ^ step) for i in range(peers)]) for step in steps]


def summed(x, axis, low, high):
    first, second, third = partners(x, axis, (low, high, low | high))
    return (x + first) + (second + third)


def local(queries, key_rows, values, cotangent, starts, lens, bias):
    count = lax.axis_size("ctx")
    cut, last, first = cut_prompt(starts, key_rows, values)
    held = exchange(cut.reshape(count, 2 * BAND, HD))
    low = shifted(last, 1)
    high = shifted(first, -1)
    stats, *masks = window(
        starts, lens, bias, queries, cotangent, key_rows, values, low, high
    )
    prompt = exchange(route(starts, held)).reshape(BANDS, HEADS, 2 * BAND, HD)
    gprompt, final = prompt_part(bias, queries, cotangent, prompt, stats, masks[2])
    held = exchange(gprompt.reshape(count, SENT, HD))
    attended, grad_q, gk, gv = own_part(
        bias, queries, cotangent, key_rows, values, low, high, prompt, final, masks
    )
    final, gk = lax.optimization_barrier((final, gk))
    glow, ghigh = halo_grads(queries, cotangent, low, high, final, masks[1])
    right = shifted(glow, -1)
    left = shifted(ghigh, 1)
    held, glow, ghigh = lax.optimization_barrier((held, glow, ghigh))
    owned, sums = gather(starts, held)
    returned = exchange(owned).reshape(BANDS, HEADS, 2 * BAND, HD)
    grad_bias = jnp.sum(summed(sums, "dp", 1, 2), axis=1)
    outk, outv, both = merge(gk, gv, left, right)
    grad_k, grad_v = finish(starts, outk, outv, both, returned)
    return attended, grad_q, grad_k, grad_v, grad_bias


def solution(mesh):
    split = P("dp", "ctx", None)
    return jax.shard_map(
        local,
        mesh=mesh,
        in_specs=(split, split, split, split, P("dp", None), P("dp", None), P()),
        out_specs=(split, split, split, split, P()),
        check_vma=False,
    )
```

```python
import functools
import math

import jax
import jax.numpy as jnp
from jax import lax
from jax.experimental import pallas as pl
from jax.experimental.pallas import tpu as pltpu
from jax.sharding import PartitionSpec as P

HW = 128
PMAX = 128
ROWS = 256
HD = 128
HEADS = 8
WIDTH = HEADS * HD
BANDS = 8
BAND = PMAX // BANDS
SENT = 2 * BAND + HEADS
SPAN = PMAX + BAND
GROUP = 2
STAGED = 4
MERGE = 8
OWN = (5, 1)
NEG = -1e30
LOG2E = math.log2(math.e)
SCALE = 1.0 / math.sqrt(HD)
FACTOR = SCALE * LOG2E

SMEM = pl.BlockSpec(memory_space=pltpu.SMEM)
VMEM = pl.BlockSpec(memory_space=pltpu.VMEM)
HBM = pl.BlockSpec(memory_space=pltpu.HBM)
PARAMS = pltpu.CompilerParams(vmem_limit_bytes=20 * 1024 * 1024)
FROM_HBM = pltpu.CompilerParams(vmem_limit_bytes=60 * 1024 * 1024)
NEARLY = pltpu.CompilerParams(vmem_limit_bytes=52 * 1024 * 1024)


def nt(a, b):
    return lax.dot_general(a, b, (((1,), (1,)), ((), ())), preferred_element_type=jnp.float32)


def tn(a, b):
    return lax.dot_general(a, b, (((0,), (0,)), ((), ())), preferred_element_type=jnp.float32)


def nn(a, b):
    return lax.dot_general(a, b, (((1,), (0,)), ((), ())), preferred_element_type=jnp.float32)


def own_start(starts_ref, me):
    start = starts_ref[0, me]
    return start >= 0, jnp.where(start >= 0, start - me * ROWS, 0)


def columns(head):
    return slice(head * HD, (head + 1) * HD)


def float_array(*shape):
    return jax.ShapeDtypeStruct(shape, jnp.float32)


def low_array(*shape):
    return jax.ShapeDtypeStruct(shape, jnp.bfloat16)


def cut_kernel(
    starts_ref,
    k_hbm,
    v_hbm,
    out_hbm,
    last_hbm,
    first_hbm,
    k_ref,
    v_ref,
    out_ref,
    sems,
    edge_sems,
    out_sems,
):
    me = lax.axis_index("ctx")
    offset = own_start(starts_ref, me)[1]
    sources = (k_hbm, v_hbm)
    scratch = (k_ref, v_ref)
    loads = [
        pltpu.make_async_copy(source.at[0], ref, sems.at[part])
        for part, (source, ref) in enumerate(zip(sources, scratch))
    ]
    stores = [
        pltpu.make_async_copy(ref.at[rows, :], target.at[part], edge_sems.at[part, half])
        for part, ref in enumerate(scratch)
        for half, (rows, target) in enumerate(
            ((slice(0, HW), first_hbm), (slice(HW, ROWS), last_hbm))
        )
    ]
    for copy in loads:
        copy.start()
    row = lax.broadcasted_iota(jnp.int32, (PMAX, ROWS), 0)
    frame = lax.broadcasted_iota(jnp.int32, (PMAX, ROWS), 1)
    pick = (frame == row + offset).astype(jnp.bfloat16)
    for part, ref in enumerate(scratch):
        loads[part].wait()
        stores[2 * part].start()
        stores[2 * part + 1].start()
        here = pl.ds(part * BAND, BAND)
        for first in range(0, HEADS, GROUP):
            cols = slice(first * HD, (first + GROUP) * HD)
            rows = nn(pick, ref[:, cols]).astype(jnp.bfloat16)
            for member in range(GROUP):
                piece = rows[:, columns(member)].reshape(BANDS, BAND, HD)
                out_ref[:, first + member, here, :] = piece
        store = pltpu.make_async_copy(
            out_ref.at[:, :, here, :], out_hbm.at[:, :, here, :], out_sems.at[part]
        )
        store.start()
        stores.append(store)
    for store in stores:
        store.wait()


def cut_prompt(starts, key_rows, values):
    return pl.pallas_call(
        cut_kernel,
        out_shape=(
            low_array(BANDS, HEADS, 2 * BAND, HD),
            low_array(2, HW, WIDTH),
            low_array(2, HW, WIDTH),
        ),
        in_specs=[SMEM, HBM, HBM],
        out_specs=(HBM, HBM, HBM),
        scratch_shapes=[
            pltpu.VMEM((ROWS, WIDTH), jnp.bfloat16),
            pltpu.VMEM((ROWS, WIDTH), jnp.bfloat16),
            pltpu.VMEM((BANDS, HEADS, 2 * BAND, HD), jnp.bfloat16),
            pltpu.SemaphoreType.DMA((2,)),
            pltpu.SemaphoreType.DMA((2, 2)),
            pltpu.SemaphoreType.DMA((2,)),
        ],
        compiler_params=FROM_HBM,
        name="cut_prompt",
    )(starts, key_rows, values)


def route_kernel(starts_ref, in_ref, out_ref):
    count = in_ref.shape[0]

    def step(target, source):
        out_ref[target] = in_ref[source]
        return jnp.where(starts_ref[0, target] >= 0, target, source)

    lax.fori_loop(0, count, step, jnp.int32(0), unroll=8)


def route(starts, pieces):
    return pl.pallas_call(
        route_kernel,
        out_shape=jax.ShapeDtypeStruct(pieces.shape, pieces.dtype),
        in_specs=[SMEM, VMEM],
        out_specs=VMEM,
        compiler_params=PARAMS,
        name="route",
    )(starts, pieces)


def gather_kernel(starts_ref, in_ref, out_ref, sums_ref):
    count = in_ref.shape[0]
    out_ref[...] = jnp.zeros_like(out_ref)

    def step(target, carry):
        source, total, sums = carry
        block = in_ref[target].astype(jnp.float32)
        total = total + block[: 2 * BAND]
        sums = sums + block[2 * BAND :]
        out_ref[source] = total.astype(jnp.bfloat16)
        begins = starts_ref[0, target] >= 0
        return jnp.where(begins, target, source), jnp.where(begins, 0.0, total), sums

    sums = in_ref[0].astype(jnp.float32)[2 * BAND :]
    carry = (jnp.int32(0), jnp.zeros((2 * BAND, HD), jnp.float32), sums)
    sums_ref[...] = lax.fori_loop(1, count, step, carry, unroll=7)[2]


def gather(starts, pieces):
    return pl.pallas_call(
        gather_kernel,
        out_shape=(low_array(pieces.shape[0], 2 * BAND, HD), float_array(HEADS, HD)),
        in_specs=[SMEM, VMEM],
        out_specs=(VMEM, VMEM),
        compiler_params=PARAMS,
        name="gather",
    )(starts, pieces)


def carried_prompt(starts_ref, lens_ref, me):
    def later(index, found):
        used = starts_ref[0, index] >= 0
        return (
            jnp.where(used, starts_ref[0, index], found[0]),
            jnp.where(used, lens_ref[0, index], found[1]),
        )

    return lax.fori_loop(0, me, later, (jnp.int32(0), jnp.int32(0)))


def grid_of(keys, rows):
    key = lax.broadcasted_iota(jnp.int32, (keys, rows), 0)
    return key, lax.broadcasted_iota(jnp.int32, (keys, rows), 1)


def hold(ref, allowed):
    ref[...] = jnp.where(allowed, 0.0, NEG)


def hold_masks(starts_ref, lens_ref, own_mask, halo_mask, prompt_mask):
    me = lax.axis_index("ctx")
    last = starts_ref.shape[1] - 1
    begins, offset = own_start(starts_ref, me)
    offset = jnp.where(begins, offset, ROWS)
    own_len = jnp.where(begins, lens_ref[0, me], 0)
    key, row = grid_of(ROWS, ROWS)
    prompt = (key >= offset) & (key < offset + own_len)
    near = jnp.abs(row - key) <= HW
    hold(own_mask.at[0], ((row >= offset) == (key >= offset)) & (prompt | near))
    own_mask[1] = prompt.astype(jnp.float32)
    start, length = carried_prompt(starts_ref, lens_ref, me)
    prompt_end = start + length - (me * ROWS - HW)
    next_begins, next_offset = own_start(starts_ref, jnp.minimum(me + 1, last))
    next_offset = jnp.where(next_begins, next_offset, HW)
    next_offset = jnp.where(me < last, next_offset, 0)
    key, row = grid_of(HW, HW)
    hold(halo_mask.at[0], (key >= row) & (row < offset) & (key >= prompt_end) & (me > 0))
    hold(halo_mask.at[1], (key <= row) & (key < next_offset))
    key, row = grid_of(PMAX, ROWS)
    hold(prompt_mask, (row < offset) & (key < length))


def top_of(x):
    return jnp.max(x, axis=0, keepdims=True)


def sum_of(x):
    return jnp.sum(x, axis=0, keepdims=True)


def window_kernel(
    starts_ref,
    lens_ref,
    bias_ref,
    q_ref,
    d_ref,
    k_ref,
    v_ref,
    low_ref,
    high_ref,
    stats_ref,
    own_mask,
    halo_mask,
    prompt_mask,
):
    head = pl.program_id(0)

    @pl.when(head == 0)
    def _():
        hold_masks(starts_ref, lens_ref, own_mask, halo_mask, prompt_mask)

    q, d, k, v = q_ref[0], d_ref[0], k_ref[0], v_ref[0]
    bias = bias_ref[head] * LOG2E
    flag = own_mask[1]
    x_own = nt(k, q) * FACTOR + (own_mask[0] + flag * bias)
    x_low = nt(low_ref[0], q[:HW]) * FACTOR + halo_mask[0]
    x_high = nt(high_ref[0], q[HW:]) * FACTOR + halo_mask[1]
    tops = jnp.concatenate([top_of(x_low), top_of(x_high)], axis=1)
    top = jnp.maximum(top_of(x_own), tops)
    e_own = jnp.exp2(x_own - top)
    e_low = jnp.exp2(x_low - top[:, :HW])
    e_high = jnp.exp2(x_high - top[:, HW:])
    w_own = e_own * nt(v, d)
    w_low = e_low * nt(low_ref[1], d[:HW])
    w_high = e_high * nt(high_ref[1], d[HW:])
    total = sum_of(e_own) + jnp.concatenate([sum_of(e_low), sum_of(e_high)], axis=1)
    weighted = sum_of(w_own) + jnp.concatenate([sum_of(w_low), sum_of(w_high)], axis=1)
    inverse = 1.0 / total
    own_bias = (sum_of(w_own * flag) - weighted * inverse * sum_of(e_own * flag)) * inverse
    stats_ref[0] = jnp.concatenate(
        [top, total, weighted, own_bias, jnp.zeros((4, ROWS), jnp.float32)], axis=0
    )


def head_rows(part=ROWS):
    return pl.BlockSpec((1, part, HD), lambda head: (0, 0, head))


def head_halo():
    return pl.BlockSpec((2, HW, HD), lambda head: (0, 0, head))


def head_tile(*shape):
    return pl.BlockSpec((1, *shape), lambda head: (head,) + (0,) * len(shape))


def head_pieces():
    return pl.BlockSpec((BANDS, 1, 2 * BAND, HD), lambda head: (0, head, 0, 0))


MASKS = (
    float_array(2, ROWS, ROWS),
    float_array(2, HW, HW),
    float_array(PMAX, ROWS),
)


def whole(array):
    return pl.BlockSpec(array.shape, lambda head: (0,) * len(array.shape))


def cost(micros):
    return pl.CostEstimate(flops=micros * 10**9, bytes_accessed=8 << 20, transcendentals=0)


def window(starts, lens, bias, queries, cotangent, key_rows, values, low, high):
    rows = head_rows()
    return pl.pallas_call(
        window_kernel,
        grid=(HEADS,),
        out_shape=(float_array(HEADS, 8, ROWS), *MASKS),
        in_specs=[SMEM, SMEM, SMEM, rows, rows, rows, rows, head_halo(), head_halo()],
        out_specs=(head_tile(8, ROWS), *(whole(mask) for mask in MASKS)),
        compiler_params=PARAMS,
        cost_estimate=cost(20),
        name="window",
    )(starts, lens, bias, queries, cotangent, key_rows, values, low, high)


def prompt_kernel(
    bias_ref, q_ref, d_ref, prompt_ref, stats_ref, mask_ref, grad_hbm, final_hbm, grad_ref, final_ref, sems
):
    mask = mask_ref[...]
    rows = [(q_ref[0, :, columns(head)], d_ref[0, :, columns(head)]) for head in range(HEADS)]
    all_sums, terms, stores = [], [], []
    for first in range(0, HEADS, STAGED):
        heads = range(first, first + STAGED)
        raw = [
            products(
                prompt_ref[:, head, :BAND, :].reshape(PMAX, HD),
                prompt_ref[:, head, BAND:, :].reshape(PMAX, HD),
                *rows[head],
            )
            for head in heads
        ]
        for head, (scores, dprobs) in zip(heads, raw):
            x = scores * FACTOR + (mask + bias_ref[head] * LOG2E)
            stats = stats_ref[head]
            top = jnp.maximum(stats[0:1], top_of(x))
            rescale = jnp.exp2(stats[0:1] - top)
            raised = jnp.exp2(x - top)
            inverse = 1.0 / (stats[1:2] * rescale + sum_of(raised))
            delta = (stats[2:3] * rescale + sum_of(raised * dprobs)) * inverse
            probs = raised * inverse
            dscores = (probs * SCALE) * (dprobs - delta)
            terms.append((probs.astype(jnp.bfloat16), dscores.astype(jnp.bfloat16)))
            final_ref[head] = jnp.concatenate(
                [top, inverse, delta, jnp.zeros((5, ROWS), jnp.float32)], axis=0
            )
            sums = stats[3:4] + sum_of(dscores) * (1.0 / SCALE)
            all_sums.append(sums[:, :HW] + sums[:, HW:])

    stores.append(pltpu.make_async_copy(final_ref, final_hbm, sems.at[HEADS // STAGED]))
    stores[0].start()
    sums = jnp.concatenate(all_sums, axis=0)
    sums = sums + pltpu.roll(sums, HW // 2, 1)
    upper = sums.astype(jnp.bfloat16).astype(jnp.float32)
    lane = lax.broadcasted_iota(jnp.int32, (HEADS, HW), 1)
    tile = jnp.where(lane < HW // 2, upper, sums - upper).astype(jnp.bfloat16)
    for first in range(0, HEADS, STAGED):
        for head in range(first, first + STAGED):
            (q, d), (low_probs, low_ds) = rows[head], terms[head]
            gk = nn(low_ds, q).astype(jnp.bfloat16)
            gv = nn(low_probs, d).astype(jnp.bfloat16)
            grad_ref[:, head, :BAND, :] = gk.reshape(BANDS, BAND, HD)
            grad_ref[:, head, BAND : 2 * BAND, :] = gv.reshape(BANDS, BAND, HD)
            for band in range(BANDS):
                grad_ref[band, head, 2 * BAND :, :] = tile
        here = pl.ds(first, STAGED)
        store = pltpu.make_async_copy(
            grad_ref.at[:, here], grad_hbm.at[:, here], sems.at[first // STAGED]
        )
        store.start()
        stores.append(store)
    for store in stores:
        store.wait()


def prompt_part(bias, queries, cotangent, prompt, stats, prompt_mask):
    return pl.pallas_call(
        prompt_kernel,
        out_shape=(low_array(BANDS, HEADS, SENT, HD), float_array(HEADS, 8, ROWS)),
        in_specs=[SMEM, VMEM, VMEM, VMEM, VMEM, VMEM],
        out_specs=(HBM, HBM),
        scratch_shapes=[
            pltpu.VMEM((BANDS, HEADS, SENT, HD), jnp.bfloat16),
            pltpu.VMEM((HEADS, 8, ROWS), jnp.float32),
            pltpu.SemaphoreType.DMA((HEADS // STAGED + 1,)),
        ],
        compiler_params=PARAMS,
        cost_estimate=cost(4),
        name="prompt_part",
    )(bias, queries, cotangent, prompt, stats, prompt_mask)


def products(keys, values, q, d):
    return nt(keys, q), nt(values, d)


def settled(scores, dprobs, added, final):
    probs = jnp.exp2(scores * FACTOR + (added - final[0:1])) * final[1:2]
    dscores = (probs * SCALE) * (dprobs - final[2:3])
    return probs.astype(jnp.bfloat16), dscores.astype(jnp.bfloat16)


def halo_kernel(q_ref, d_ref, low_ref, high_ref, final_ref, mask_ref, glow_ref, ghigh_ref):
    sides = ((low_ref, glow_ref), (high_ref, ghigh_ref))
    for first in range(0, HEADS, STAGED):
        places = [
            (half, slice(half * HW, (half + 1) * HW), head)
            for head in range(first, first + STAGED)
            for half in range(2)
        ]
        rows = [
            (q_ref[0, part, columns(head)], d_ref[0, part, columns(head)])
            for _, part, head in places
        ]
        raw = [
            products(sides[half][0][0, :, columns(head)], sides[half][0][1, :, columns(head)], q, d)
            for (half, _, head), (q, d) in zip(places, rows)
        ]
        terms = [
            settled(*pair, mask_ref[half], final_ref[head, :, part])
            for (half, part, head), pair in zip(places, raw)
        ]
        for (half, _, head), (q, d), (probs, ds) in zip(places, rows, terms):
            out = sides[half][1]
            out[0, :, columns(head)] = nn(ds, q).astype(jnp.bfloat16)
            out[1, :, columns(head)] = nn(probs, d).astype(jnp.bfloat16)


def halo_grads(queries, cotangent, low, high, final, halo_mask):
    return pl.pallas_call(
        halo_kernel,
        out_shape=(low_array(2, HW, WIDTH), low_array(2, HW, WIDTH)),
        in_specs=[VMEM] * 6,
        out_specs=(VMEM, VMEM),
        compiler_params=PARAMS,
        cost_estimate=cost(4),
        name="halo_grads",
    )(queries, cotangent, low, high, final, halo_mask)


def own_kernel(
    first,
    bias_ref,
    q_ref,
    d_ref,
    k_ref,
    v_ref,
    low_ref,
    high_ref,
    prompt_ref,
    final_ref,
    own_mask,
    halo_mask,
    prompt_mask,
    *rest,
):
    attended_ref, gq_ref, gk_ref, gv_ref = rest[-4:]
    members = range(GROUP)
    step = first + pl.program_id(0)
    blocks = []
    for member in members:
        cols = columns(member)
        q, d = q_ref[0, :, cols], d_ref[0, :, cols]
        kp = prompt_ref[:, member, :BAND, :].reshape(PMAX, HD)
        vp = prompt_ref[:, member, BAND:, :].reshape(PMAX, HD)
        blocks.append(
            (
                (k_ref[0, :, cols], v_ref[0, :, cols], q, d),
                (kp, vp, q, d),
                (low_ref[0, :, cols], low_ref[1, :, cols], q[:HW], d[:HW]),
                (high_ref[0, :, cols], high_ref[1, :, cols], q[HW:], d[HW:]),
            )
        )
    raw = [[products(*block) for block in parts] for parts in blocks]
    terms = []
    for member in members:
        bias = bias_ref[step * GROUP + member] * LOG2E
        final = final_ref[member]
        added = (
            own_mask[0] + own_mask[1] * bias,
            prompt_mask[...] + bias,
            halo_mask[0],
            halo_mask[1],
        )
        finals = (final, final, final[:, :HW], final[:, HW:])
        terms.append(
            [settled(*pair, x, y) for pair, x, y in zip(raw[member], added, finals)]
        )
    for member in members:
        cols = columns(member)
        own, prompt, low, high = blocks[member]
        (probs, ds), (probs_p, ds_p), (probs_l, ds_l), (probs_h, ds_h) = terms[member]
        gk_ref[:, cols] = nn(ds, own[2])
        gv_ref[:, cols] = nn(probs, own[3])
        attended = tn(probs, own[1]) + tn(probs_p, prompt[1])
        attended += jnp.concatenate([tn(probs_l, low[1]), tn(probs_h, high[1])], axis=0)
        attended_ref[0, :, cols] = attended.astype(jnp.bfloat16)
        grad_q = tn(ds, own[0]) + tn(ds_p, prompt[0])
        grad_q += jnp.concatenate([tn(ds_l, low[0]), tn(ds_h, high[0])], axis=0)
        gq_ref[0, :, cols] = grad_q.astype(jnp.bfloat16)


def own_part(half, bias, queries, cotangent, key_rows, values, low, high, prompt, final, masks, begun):
    steps = HEADS // GROUP // 2
    first = half * steps
    rows = pl.BlockSpec((1, ROWS, GROUP * HD), lambda step: (0, 0, first + step))
    halo = pl.BlockSpec((2, HW, GROUP * HD), lambda step: (0, 0, first + step))
    pieces = pl.BlockSpec((BANDS, GROUP, 2 * BAND, HD), lambda step: (0, first + step, 0, 0))
    tile = pl.BlockSpec((GROUP, 8, ROWS), lambda step: (first + step, 0, 0))
    total = pl.BlockSpec((ROWS, GROUP * HD), lambda step: (0, first + step))
    specs = [SMEM, rows, rows, rows, rows, halo, halo, pieces, tile]
    specs += [whole(mask) for mask in MASKS]
    return pl.pallas_call(
        functools.partial(own_kernel, first),
        grid=(steps,),
        out_shape=(
            low_array(1, ROWS, WIDTH),
            low_array(1, ROWS, WIDTH),
            float_array(ROWS, WIDTH),
            float_array(ROWS, WIDTH),
        ),
        in_specs=specs + [HBM] * len(begun),
        out_specs=(rows, rows, total, total),
        input_output_aliases={len(specs) + index: index for index in range(len(begun))},
        compiler_params=NEARLY,
        cost_estimate=cost(OWN[half]),
        name="own_part",
    )(bias, queries, cotangent, key_rows, values, low, high, prompt, final, *masks, *begun)


def merge_kernel(right_ref, left_ref, gk_ref, gv_ref, outk_ref, outv_ref, sums_ref):
    for part, (ref, out) in enumerate(((gk_ref, outk_ref), (gv_ref, outv_ref))):
        for half, side in enumerate((left_ref, right_ref)):
            rows = slice(half * HW, (half + 1) * HW)
            total = ref[rows, :] + side[part].astype(jnp.float32)
            sums_ref[part, rows, :] = total
            out[0, rows, :] = total.astype(jnp.bfloat16)


def merge(gk, gv, left, right):
    total = pl.BlockSpec((ROWS, GROUP * HD), lambda step: (0, step))
    rows = pl.BlockSpec((1, ROWS, GROUP * HD), lambda step: (0, 0, step))
    side = pl.BlockSpec((2, HW, GROUP * HD), lambda step: (0, 0, step))
    both = pl.BlockSpec((2, ROWS, GROUP * HD), lambda step: (0, 0, step))
    return pl.pallas_call(
        merge_kernel,
        grid=(HEADS // GROUP,),
        out_shape=(low_array(1, ROWS, WIDTH),) * 2 + (float_array(2, ROWS, WIDTH),),
        in_specs=[side, side, total, total],
        out_specs=(rows, rows, both),
        compiler_params=NEARLY,
        cost_estimate=cost(MERGE),
        name="merge",
    )(right, left, gk, gv)


def finish_kernel(
    starts_ref,
    sums_hbm,
    prompt_ref,
    _ink,
    _inv,
    outk_hbm,
    outv_hbm,
    sums_ref,
    rows_ref,
    load_sems,
    store_sems,
):
    me = lax.axis_index("ctx")
    begins, offset = own_start(starts_ref, me)

    @pl.when(begins)
    def _():
        base = pl.multiple_of(jnp.minimum(offset // BAND * BAND, ROWS - SPAN), BAND)
        span = pl.ds(base, SPAN)
        loads = [
            pltpu.make_async_copy(sums_hbm.at[part, span, :], sums_ref.at[part], load_sems.at[part])
            for part in range(2)
        ]
        stores = [
            pltpu.make_async_copy(rows_ref.at[part], ref.at[0, span, :], store_sems.at[part])
            for part, ref in enumerate((outk_hbm, outv_hbm))
        ]
        for copy in loads:
            copy.start()
        frame, row = grid_of(SPAN, PMAX)
        place = (frame == row + (offset - base)).astype(jnp.bfloat16)
        for part in range(2):
            loads[part].wait()
            for head in range(HEADS):
                cols = columns(head)
                piece = prompt_ref[:, head, part * BAND : (part + 1) * BAND, :].reshape(PMAX, HD)
                total = sums_ref[part, :, cols] + nn(place, piece)
                rows_ref[part, :, cols] = total.astype(jnp.bfloat16)
            stores[part].start()
        for copy in stores:
            copy.wait()


def finish(starts, outk, outv, sums, prompt):
    return pl.pallas_call(
        finish_kernel,
        out_shape=(low_array(1, ROWS, WIDTH),) * 2,
        in_specs=[SMEM, HBM, VMEM, HBM, HBM],
        out_specs=(HBM, HBM),
        input_output_aliases={3: 0, 4: 1},
        scratch_shapes=[
            pltpu.VMEM((2, SPAN, WIDTH), jnp.float32),
            pltpu.VMEM((2, SPAN, WIDTH), jnp.bfloat16),
            pltpu.SemaphoreType.DMA((2,)),
            pltpu.SemaphoreType.DMA((2,)),
        ],
        compiler_params=NEARLY,
        name="finish",
    )(starts, sums, prompt, outk, outv)


def exchange(pieces):
    return lax.all_to_all(pieces, "ctx", 0, 0, tiled=True)


def shifted(x, by):
    peers = lax.axis_size("ctx")
    return lax.ppermute(x, "ctx", [(i, i + by) for i in range(peers) if 0 <= i + by < peers])


def partners(x, axis, steps):
    peers = lax.axis_size(axis)
    return [lax.ppermute(x, axis, [(i, i ^ step) for i in range(peers)]) for step in steps]


def summed(x, axis, low, high):
    first, second, third = partners(x, axis, (low, high, low | high))
    return (x + first) + (second + third)


def local(queries, key_rows, values, cotangent, starts, lens, bias):
    count = lax.axis_size("ctx")
    cut, last, first = cut_prompt(starts, key_rows, values)
    held = exchange(cut.reshape(count, 2 * BAND, HD))
    low = shifted(last, 1)
    high = shifted(first, -1)
    stats, *masks = window(
        starts, lens, bias, queries, cotangent, key_rows, values, low, high
    )
    prompt = exchange(route(starts, held)).reshape(BANDS, HEADS, 2 * BAND, HD)
    gprompt, final = prompt_part(bias, queries, cotangent, prompt, stats, masks[2])
    held = exchange(gprompt.reshape(count, SENT, HD))
    arrays = (queries, cotangent, key_rows, values, low, high, prompt)
    begun = own_part(0, bias, *arrays, final, masks, ())
    final, begun = lax.optimization_barrier((final, begun))
    glow, ghigh = halo_grads(queries, cotangent, low, high, final, masks[1])
    right = shifted(glow, -1)
    left = shifted(ghigh, 1)
    held, glow, ghigh = lax.optimization_barrier((held, glow, ghigh))
    owned, sums = gather(starts, held)
    returned = exchange(owned).reshape(BANDS, HEADS, 2 * BAND, HD)
    grad_bias = jnp.sum(summed(sums, "dp", 1, 2), axis=1)
    final, _ = lax.optimization_barrier((final, sums))
    attended, grad_q, gk, gv = own_part(1, bias, *arrays, final, masks, begun)
    outk, outv, both = merge(gk, gv, left, right)
    grad_k, grad_v = finish(starts, outk, outv, both, returned)
    return attended, grad_q, grad_k, grad_v, grad_bias


def solution(mesh):
    split = P("dp", "ctx", None)
    return jax.shard_map(
        local,
        mesh=mesh,
        in_specs=(split, split, split, split, P("dp", None), P("dp", None), P()),
        out_specs=(split, split, split, split, P()),
        check_vma=False,
    )
```

```python
import functools
import math

import jax
import jax.numpy as jnp
from jax import lax
from jax.experimental import pallas as pl
from jax.experimental.pallas import tpu as pltpu
from jax.sharding import PartitionSpec as P

HW = 128
PMAX = 128
ROWS = 256
HD = 128
HEADS = 8
WIDTH = HEADS * HD
BANDS = 8
BAND = PMAX // BANDS
SENT = 2 * BAND + HEADS
SPAN = PMAX + BAND
GROUP = 2
STAGED = 4
MERGE = 8
OWN = (5, 1)
NEG = -1e30
LOG2E = math.log2(math.e)
SCALE = 1.0 / math.sqrt(HD)
FACTOR = SCALE * LOG2E

SMEM = pl.BlockSpec(memory_space=pltpu.SMEM)
VMEM = pl.BlockSpec(memory_space=pltpu.VMEM)
HBM = pl.BlockSpec(memory_space=pltpu.HBM)
PARAMS = pltpu.CompilerParams(vmem_limit_bytes=20 * 1024 * 1024)
FROM_HBM = pltpu.CompilerParams(vmem_limit_bytes=60 * 1024 * 1024)
NEARLY = pltpu.CompilerParams(vmem_limit_bytes=52 * 1024 * 1024)


def nt(a, b):
    return lax.dot_general(a, b, (((1,), (1,)), ((), ())), preferred_element_type=jnp.float32)


def tn(a, b):
    return lax.dot_general(a, b, (((0,), (0,)), ((), ())), preferred_element_type=jnp.float32)


def nn(a, b):
    return lax.dot_general(a, b, (((1,), (0,)), ((), ())), preferred_element_type=jnp.float32)


def own_start(starts_ref, me):
    start = starts_ref[0, me]
    return start >= 0, jnp.where(start >= 0, start - me * ROWS, 0)


def columns(head):
    return slice(head * HD, (head + 1) * HD)


def float_array(*shape):
    return jax.ShapeDtypeStruct(shape, jnp.float32)


def low_array(*shape):
    return jax.ShapeDtypeStruct(shape, jnp.bfloat16)


def cut_kernel(
    starts_ref,
    k_hbm,
    v_hbm,
    out_hbm,
    last_hbm,
    first_hbm,
    k_ref,
    v_ref,
    out_ref,
    sems,
    edge_sems,
    out_sems,
):
    me = lax.axis_index("ctx")
    offset = own_start(starts_ref, me)[1]
    sources = (k_hbm, v_hbm)
    scratch = (k_ref, v_ref)
    loads = [
        pltpu.make_async_copy(source.at[0], ref, sems.at[part])
        for part, (source, ref) in enumerate(zip(sources, scratch))
    ]
    stores = [
        pltpu.make_async_copy(ref.at[rows, :], target.at[part], edge_sems.at[part, half])
        for part, ref in enumerate(scratch)
        for half, (rows, target) in enumerate(
            ((slice(0, HW), first_hbm), (slice(HW, ROWS), last_hbm))
        )
    ]
    for copy in loads:
        copy.start()
    row = lax.broadcasted_iota(jnp.int32, (PMAX, ROWS), 0)
    frame = lax.broadcasted_iota(jnp.int32, (PMAX, ROWS), 1)
    pick = (frame == row + offset).astype(jnp.bfloat16)
    for part, ref in enumerate(scratch):
        loads[part].wait()
        stores[2 * part].start()
        stores[2 * part + 1].start()
        here = pl.ds(part * BAND, BAND)
        for first in range(0, HEADS, GROUP):
            cols = slice(first * HD, (first + GROUP) * HD)
            rows = nn(pick, ref[:, cols]).astype(jnp.bfloat16)
            for member in range(GROUP):
                piece = rows[:, columns(member)].reshape(BANDS, BAND, HD)
                out_ref[:, first + member, here, :] = piece
        store = pltpu.make_async_copy(
            out_ref.at[:, :, here, :], out_hbm.at[:, :, here, :], out_sems.at[part]
        )
        store.start()
        stores.append(store)
    for store in stores:
        store.wait()


def cut_prompt(starts, key_rows, values):
    return pl.pallas_call(
        cut_kernel,
        out_shape=(
            low_array(BANDS, HEADS, 2 * BAND, HD),
            low_array(2, HW, WIDTH),
            low_array(2, HW, WIDTH),
        ),
        in_specs=[SMEM, HBM, HBM],
        out_specs=(HBM, HBM, HBM),
        scratch_shapes=[
            pltpu.VMEM((ROWS, WIDTH), jnp.bfloat16),
            pltpu.VMEM((ROWS, WIDTH), jnp.bfloat16),
            pltpu.VMEM((BANDS, HEADS, 2 * BAND, HD), jnp.bfloat16),
            pltpu.SemaphoreType.DMA((2,)),
            pltpu.SemaphoreType.DMA((2, 2)),
            pltpu.SemaphoreType.DMA((2,)),
        ],
        compiler_params=FROM_HBM,
        name="cut_prompt",
    )(starts, key_rows, values)


def route_kernel(starts_ref, in_ref, out_ref):
    count = in_ref.shape[0]

    def step(target, source):
        out_ref[target] = in_ref[source]
        return jnp.where(starts_ref[0, target] >= 0, target, source)

    lax.fori_loop(0, count, step, jnp.int32(0), unroll=8)


def route(starts, pieces):
    return pl.pallas_call(
        route_kernel,
        out_shape=jax.ShapeDtypeStruct(pieces.shape, pieces.dtype),
        in_specs=[SMEM, VMEM],
        out_specs=VMEM,
        compiler_params=PARAMS,
        name="route",
    )(starts, pieces)


def gather_kernel(starts_ref, in_ref, out_ref, sums_ref):
    count = in_ref.shape[0]
    out_ref[...] = jnp.zeros_like(out_ref)

    def step(target, carry):
        source, total, sums = carry
        block = in_ref[target].astype(jnp.float32)
        total = total + block[: 2 * BAND]
        sums = sums + block[2 * BAND :]
        out_ref[source] = total.astype(jnp.bfloat16)
        begins = starts_ref[0, target] >= 0
        return jnp.where(begins, target, source), jnp.where(begins, 0.0, total), sums

    sums = in_ref[0].astype(jnp.float32)[2 * BAND :]
    carry = (jnp.int32(0), jnp.zeros((2 * BAND, HD), jnp.float32), sums)
    sums_ref[...] = lax.fori_loop(1, count, step, carry, unroll=7)[2]


def gather(starts, pieces):
    return pl.pallas_call(
        gather_kernel,
        out_shape=(low_array(pieces.shape[0], 2 * BAND, HD), float_array(HEADS, HD)),
        in_specs=[SMEM, VMEM],
        out_specs=(VMEM, VMEM),
        compiler_params=PARAMS,
        name="gather",
    )(starts, pieces)


def carried_prompt(starts_ref, lens_ref, me):
    def later(index, found):
        used = starts_ref[0, index] >= 0
        return (
            jnp.where(used, starts_ref[0, index], found[0]),
            jnp.where(used, lens_ref[0, index], found[1]),
        )

    return lax.fori_loop(0, me, later, (jnp.int32(0), jnp.int32(0)))


def grid_of(keys, rows):
    key = lax.broadcasted_iota(jnp.int32, (keys, rows), 0)
    return key, lax.broadcasted_iota(jnp.int32, (keys, rows), 1)


def hold(ref, allowed):
    ref[...] = jnp.where(allowed, 0.0, NEG)


def hold_masks(starts_ref, lens_ref, own_mask, halo_mask, prompt_mask):
    me = lax.axis_index("ctx")
    last = starts_ref.shape[1] - 1
    begins, offset = own_start(starts_ref, me)
    offset = jnp.where(begins, offset, ROWS)
    own_len = jnp.where(begins, lens_ref[0, me], 0)
    key, row = grid_of(ROWS, ROWS)
    prompt = (key >= offset) & (key < offset + own_len)
    near = jnp.abs(row - key) <= HW
    hold(own_mask.at[0], ((row >= offset) == (key >= offset)) & (prompt | near))
    own_mask[1] = prompt.astype(jnp.float32)
    start, length = carried_prompt(starts_ref, lens_ref, me)
    prompt_end = start + length - (me * ROWS - HW)
    next_begins, next_offset = own_start(starts_ref, jnp.minimum(me + 1, last))
    next_offset = jnp.where(next_begins, next_offset, HW)
    next_offset = jnp.where(me < last, next_offset, 0)
    key, row = grid_of(HW, HW)
    hold(halo_mask.at[0], (key >= row) & (row < offset) & (key >= prompt_end) & (me > 0))
    hold(halo_mask.at[1], (key <= row) & (key < next_offset))
    key, row = grid_of(PMAX, ROWS)
    hold(prompt_mask, (row < offset) & (key < length))


def top_of(x):
    return jnp.max(x, axis=0, keepdims=True)


def sum_of(x):
    return jnp.sum(x, axis=0, keepdims=True)


def window_kernel(
    starts_ref,
    lens_ref,
    bias_ref,
    q_ref,
    d_ref,
    k_ref,
    v_ref,
    low_ref,
    high_ref,
    stats_ref,
    own_mask,
    halo_mask,
    prompt_mask,
):
    head = pl.program_id(0)

    @pl.when(head == 0)
    def _():
        hold_masks(starts_ref, lens_ref, own_mask, halo_mask, prompt_mask)

    q, d, k, v = q_ref[0], d_ref[0], k_ref[0], v_ref[0]
    bias = bias_ref[head] * LOG2E
    flag = own_mask[1]
    x_own = nt(k, q) * FACTOR + (own_mask[0] + flag * bias)
    x_low = nt(low_ref[0], q[:HW]) * FACTOR + halo_mask[0]
    x_high = nt(high_ref[0], q[HW:]) * FACTOR + halo_mask[1]
    tops = jnp.concatenate([top_of(x_low), top_of(x_high)], axis=1)
    top = jnp.maximum(top_of(x_own), tops)
    e_own = jnp.exp2(x_own - top)
    e_low = jnp.exp2(x_low - top[:, :HW])
    e_high = jnp.exp2(x_high - top[:, HW:])
    w_own = e_own * nt(v, d)
    w_low = e_low * nt(low_ref[1], d[:HW])
    w_high = e_high * nt(high_ref[1], d[HW:])
    total = sum_of(e_own) + jnp.concatenate([sum_of(e_low), sum_of(e_high)], axis=1)
    weighted = sum_of(w_own) + jnp.concatenate([sum_of(w_low), sum_of(w_high)], axis=1)
    inverse = 1.0 / total
    own_bias = (sum_of(w_own * flag) - weighted * inverse * sum_of(e_own * flag)) * inverse
    stats_ref[0] = jnp.concatenate(
        [top, total, weighted, own_bias, jnp.zeros((4, ROWS), jnp.float32)], axis=0
    )


def head_rows(part=ROWS):
    return pl.BlockSpec((1, part, HD), lambda head: (0, 0, head))


def head_halo():
    return pl.BlockSpec((2, HW, HD), lambda head: (0, 0, head))


def head_tile(*shape):
    return pl.BlockSpec((1, *shape), lambda head: (head,) + (0,) * len(shape))


def head_pieces():
    return pl.BlockSpec((BANDS, 1, 2 * BAND, HD), lambda head: (0, head, 0, 0))


MASKS = (
    float_array(2, ROWS, ROWS),
    float_array(2, HW, HW),
    float_array(PMAX, ROWS),
)


def whole(array):
    return pl.BlockSpec(array.shape, lambda head: (0,) * len(array.shape))


def cost(micros):
    return pl.CostEstimate(flops=micros * 10**9, bytes_accessed=8 << 20, transcendentals=0)


def window(starts, lens, bias, queries, cotangent, key_rows, values, low, high):
    rows = head_rows()
    return pl.pallas_call(
        window_kernel,
        grid=(HEADS,),
        out_shape=(float_array(HEADS, 8, ROWS), *MASKS),
        in_specs=[SMEM, SMEM, SMEM, rows, rows, rows, rows, head_halo(), head_halo()],
        out_specs=(head_tile(8, ROWS), *(whole(mask) for mask in MASKS)),
        compiler_params=PARAMS,
        cost_estimate=cost(20),
        name="window",
    )(starts, lens, bias, queries, cotangent, key_rows, values, low, high)


def prompt_kernel(
    bias_ref, q_ref, d_ref, prompt_ref, stats_ref, mask_ref, grad_hbm, final_hbm, grad_ref, final_ref, sems
):
    mask = mask_ref[...]
    rows = [(q_ref[0, :, columns(head)], d_ref[0, :, columns(head)]) for head in range(HEADS)]
    all_sums, terms, stores = [], [], []
    for first in range(0, HEADS, STAGED):
        heads = range(first, first + STAGED)
        raw = [
            products(
                prompt_ref[:, head, :BAND, :].reshape(PMAX, HD),
                prompt_ref[:, head, BAND:, :].reshape(PMAX, HD),
                *rows[head],
            )
            for head in heads
        ]
        for head, (scores, dprobs) in zip(heads, raw):
            x = scores * FACTOR + (mask + bias_ref[head] * LOG2E)
            stats = stats_ref[head]
            top = jnp.maximum(stats[0:1], top_of(x))
            rescale = jnp.exp2(stats[0:1] - top)
            raised = jnp.exp2(x - top)
            inverse = 1.0 / (stats[1:2] * rescale + sum_of(raised))
            delta = (stats[2:3] * rescale + sum_of(raised * dprobs)) * inverse
            probs = raised * inverse
            dscores = (probs * SCALE) * (dprobs - delta)
            terms.append((probs.astype(jnp.bfloat16), dscores.astype(jnp.bfloat16)))
            final_ref[head] = jnp.concatenate(
                [top, inverse, delta, jnp.zeros((5, ROWS), jnp.float32)], axis=0
            )
            sums = stats[3:4] + sum_of(dscores) * (1.0 / SCALE)
            all_sums.append(sums[:, :HW] + sums[:, HW:])

    stores.append(pltpu.make_async_copy(final_ref, final_hbm, sems.at[HEADS // STAGED]))
    stores[0].start()
    sums = jnp.concatenate(all_sums, axis=0)
    sums = sums + pltpu.roll(sums, HW // 2, 1)
    upper = sums.astype(jnp.bfloat16).astype(jnp.float32)
    lane = lax.broadcasted_iota(jnp.int32, (HEADS, HW), 1)
    tile = jnp.where(lane < HW // 2, upper, sums - upper).astype(jnp.bfloat16)
    for first in range(0, HEADS, STAGED):
        for head in range(first, first + STAGED):
            (q, d), (low_probs, low_ds) = rows[head], terms[head]
            gk = nn(low_ds, q).astype(jnp.bfloat16)
            gv = nn(low_probs, d).astype(jnp.bfloat16)
            grad_ref[:, head, :BAND, :] = gk.reshape(BANDS, BAND, HD)
            grad_ref[:, head, BAND : 2 * BAND, :] = gv.reshape(BANDS, BAND, HD)
            for band in range(BANDS):
                grad_ref[band, head, 2 * BAND :, :] = tile
        here = pl.ds(first, STAGED)
        store = pltpu.make_async_copy(
            grad_ref.at[:, here], grad_hbm.at[:, here], sems.at[first // STAGED]
        )
        store.start()
        stores.append(store)
    for store in stores:
        store.wait()


def prompt_part(bias, queries, cotangent, prompt, stats, prompt_mask):
    return pl.pallas_call(
        prompt_kernel,
        out_shape=(low_array(BANDS, HEADS, SENT, HD), float_array(HEADS, 8, ROWS)),
        in_specs=[SMEM, VMEM, VMEM, VMEM, VMEM, VMEM],
        out_specs=(HBM, HBM),
        scratch_shapes=[
            pltpu.VMEM((BANDS, HEADS, SENT, HD), jnp.bfloat16),
            pltpu.VMEM((HEADS, 8, ROWS), jnp.float32),
            pltpu.SemaphoreType.DMA((HEADS // STAGED + 1,)),
        ],
        compiler_params=PARAMS,
        cost_estimate=cost(4),
        name="prompt_part",
    )(bias, queries, cotangent, prompt, stats, prompt_mask)


def products(keys, values, q, d):
    return nt(keys, q), nt(values, d)


def settled(scores, dprobs, added, final):
    probs = jnp.exp2(scores * FACTOR + (added - final[0:1])) * final[1:2]
    dscores = (probs * SCALE) * (dprobs - final[2:3])
    return probs.astype(jnp.bfloat16), dscores.astype(jnp.bfloat16)


def halo_kernel(q_ref, d_ref, low_ref, high_ref, final_ref, mask_ref, glow_ref, ghigh_ref):
    sides = ((low_ref, glow_ref), (high_ref, ghigh_ref))
    for first in range(0, HEADS, STAGED):
        places = [
            (half, slice(half * HW, (half + 1) * HW), head)
            for head in range(first, first + STAGED)
            for half in range(2)
        ]
        rows = [
            (q_ref[0, part, columns(head)], d_ref[0, part, columns(head)])
            for _, part, head in places
        ]
        raw = [
            products(sides[half][0][0, :, columns(head)], sides[half][0][1, :, columns(head)], q, d)
            for (half, _, head), (q, d) in zip(places, rows)
        ]
        terms = [
            settled(*pair, mask_ref[half], final_ref[head, :, part])
            for (half, part, head), pair in zip(places, raw)
        ]
        for (half, _, head), (q, d), (probs, ds) in zip(places, rows, terms):
            out = sides[half][1]
            out[0, :, columns(head)] = nn(ds, q).astype(jnp.bfloat16)
            out[1, :, columns(head)] = nn(probs, d).astype(jnp.bfloat16)


def halo_grads(queries, cotangent, low, high, final, halo_mask):
    return pl.pallas_call(
        halo_kernel,
        out_shape=(low_array(2, HW, WIDTH), low_array(2, HW, WIDTH)),
        in_specs=[VMEM] * 6,
        out_specs=(VMEM, VMEM),
        compiler_params=PARAMS,
        cost_estimate=cost(4),
        name="halo_grads",
    )(queries, cotangent, low, high, final, halo_mask)


def own_kernel(
    first,
    bias_ref,
    q_ref,
    d_ref,
    k_ref,
    v_ref,
    low_ref,
    high_ref,
    prompt_ref,
    final_ref,
    own_mask,
    halo_mask,
    prompt_mask,
    *rest,
):
    attended_ref, gq_ref, gk_ref, gv_ref = rest[-4:]
    members = range(GROUP)
    step = first + pl.program_id(0)
    blocks = []
    for member in members:
        cols = columns(member)
        q, d = q_ref[0, :, cols], d_ref[0, :, cols]
        kp = prompt_ref[:, member, :BAND, :].reshape(PMAX, HD)
        vp = prompt_ref[:, member, BAND:, :].reshape(PMAX, HD)
        blocks.append(
            (
                (k_ref[0, :, cols], v_ref[0, :, cols], q, d),
                (kp, vp, q, d),
                (low_ref[0, :, cols], low_ref[1, :, cols], q[:HW], d[:HW]),
                (high_ref[0, :, cols], high_ref[1, :, cols], q[HW:], d[HW:]),
            )
        )
    raw = [[products(*block) for block in parts] for parts in blocks]
    terms = []
    for member in members:
        bias = bias_ref[step * GROUP + member] * LOG2E
        final = final_ref[member]
        added = (
            own_mask[0] + own_mask[1] * bias,
            prompt_mask[...] + bias,
            halo_mask[0],
            halo_mask[1],
        )
        finals = (final, final, final[:, :HW], final[:, HW:])
        terms.append(
            [settled(*pair, x, y) for pair, x, y in zip(raw[member], added, finals)]
        )
    for member in members:
        cols = columns(member)
        own, prompt, low, high = blocks[member]
        (probs, ds), (probs_p, ds_p), (probs_l, ds_l), (probs_h, ds_h) = terms[member]
        gk_ref[:, cols] = nn(ds, own[2])
        gv_ref[:, cols] = nn(probs, own[3])
        attended = tn(probs, own[1]) + tn(probs_p, prompt[1])
        attended += jnp.concatenate([tn(probs_l, low[1]), tn(probs_h, high[1])], axis=0)
        attended_ref[0, :, cols] = attended.astype(jnp.bfloat16)
        grad_q = tn(ds, own[0]) + tn(ds_p, prompt[0])
        grad_q += jnp.concatenate([tn(ds_l, low[0]), tn(ds_h, high[0])], axis=0)
        gq_ref[0, :, cols] = grad_q.astype(jnp.bfloat16)


def own_part(half, bias, queries, cotangent, key_rows, values, low, high, prompt, final, masks, begun):
    steps = HEADS // GROUP // 2
    first = half * steps
    rows = pl.BlockSpec((1, ROWS, GROUP * HD), lambda step: (0, 0, first + step))
    halo = pl.BlockSpec((2, HW, GROUP * HD), lambda step: (0, 0, first + step))
    pieces = pl.BlockSpec((BANDS, GROUP, 2 * BAND, HD), lambda step: (0, first + step, 0, 0))
    tile = pl.BlockSpec((GROUP, 8, ROWS), lambda step: (first + step, 0, 0))
    total = pl.BlockSpec((ROWS, GROUP * HD), lambda step: (0, first + step))
    specs = [SMEM, rows, rows, rows, rows, halo, halo, pieces, tile]
    specs += [whole(mask) for mask in MASKS]
    return pl.pallas_call(
        functools.partial(own_kernel, first),
        grid=(steps,),
        out_shape=(
            low_array(1, ROWS, WIDTH),
            low_array(1, ROWS, WIDTH),
            float_array(ROWS, WIDTH),
            float_array(ROWS, WIDTH),
        ),
        in_specs=specs + [HBM] * len(begun),
        out_specs=(rows, rows, total, total),
        input_output_aliases={len(specs) + index: index for index in range(len(begun))},
        compiler_params=NEARLY,
        cost_estimate=cost(OWN[half]),
        name="own_part",
    )(bias, queries, cotangent, key_rows, values, low, high, prompt, final, *masks, *begun)


def merge_kernel(right_ref, left_ref, gk_ref, gv_ref, outk_ref, outv_ref, sums_ref):
    for part, (ref, out) in enumerate(((gk_ref, outk_ref), (gv_ref, outv_ref))):
        for half, side in enumerate((left_ref, right_ref)):
            rows = slice(half * HW, (half + 1) * HW)
            total = ref[rows, :] + side[part].astype(jnp.float32)
            sums_ref[part, rows, :] = total
            out[0, rows, :] = total.astype(jnp.bfloat16)


def merge(gk, gv, left, right):
    total = pl.BlockSpec((ROWS, GROUP * HD), lambda step: (0, step))
    rows = pl.BlockSpec((1, ROWS, GROUP * HD), lambda step: (0, 0, step))
    side = pl.BlockSpec((2, HW, GROUP * HD), lambda step: (0, 0, step))
    both = pl.BlockSpec((2, ROWS, GROUP * HD), lambda step: (0, 0, step))
    return pl.pallas_call(
        merge_kernel,
        grid=(HEADS // GROUP,),
        out_shape=(low_array(1, ROWS, WIDTH),) * 2 + (float_array(2, ROWS, WIDTH),),
        in_specs=[side, side, total, total],
        out_specs=(rows, rows, both),
        compiler_params=NEARLY,
        cost_estimate=cost(MERGE),
        name="merge",
    )(right, left, gk, gv)


def finish_kernel(
    starts_ref,
    sums_hbm,
    prompt_ref,
    _ink,
    _inv,
    outk_hbm,
    outv_hbm,
    sums_ref,
    rows_ref,
    placed_ref,
    load_sems,
    store_sems,
):
    me = lax.axis_index("ctx")
    begins, offset = own_start(starts_ref, me)

    @pl.when(begins)
    def _():
        base = pl.multiple_of(jnp.minimum(offset // BAND * BAND, ROWS - SPAN), BAND)
        span = pl.ds(base, SPAN)
        loads = [
            pltpu.make_async_copy(sums_hbm.at[part, span, :], sums_ref.at[part], load_sems.at[part])
            for part in range(2)
        ]
        stores = [
            pltpu.make_async_copy(rows_ref.at[part], ref.at[0, span, :], store_sems.at[part])
            for part, ref in enumerate((outk_hbm, outv_hbm))
        ]
        for copy in loads:
            copy.start()
        frame, row = grid_of(SPAN, PMAX)
        place = (frame == row + (offset - base)).astype(jnp.bfloat16)
        for part in range(2):
            for head in range(HEADS):
                piece = prompt_ref[:, head, part * BAND : (part + 1) * BAND, :].reshape(PMAX, HD)
                placed_ref[part, :, columns(head)] = nn(place, piece)
        for part in range(2):
            loads[part].wait()
            rows_ref[part] = (sums_ref[part] + placed_ref[part]).astype(jnp.bfloat16)
            stores[part].start()
        for copy in stores:
            copy.wait()


def finish(starts, outk, outv, sums, prompt):
    return pl.pallas_call(
        finish_kernel,
        out_shape=(low_array(1, ROWS, WIDTH),) * 2,
        in_specs=[SMEM, HBM, VMEM, HBM, HBM],
        out_specs=(HBM, HBM),
        input_output_aliases={3: 0, 4: 1},
        scratch_shapes=[
            pltpu.VMEM((2, SPAN, WIDTH), jnp.float32),
            pltpu.VMEM((2, SPAN, WIDTH), jnp.bfloat16),
            pltpu.VMEM((2, SPAN, WIDTH), jnp.float32),
            pltpu.SemaphoreType.DMA((2,)),
            pltpu.SemaphoreType.DMA((2,)),
        ],
        compiler_params=NEARLY,
        name="finish",
    )(starts, sums, prompt, outk, outv)


def exchange(pieces):
    return lax.all_to_all(pieces, "ctx", 0, 0, tiled=True)


def shifted(x, by):
    peers = lax.axis_size("ctx")
    return lax.ppermute(x, "ctx", [(i, i + by) for i in range(peers) if 0 <= i + by < peers])


def partners(x, axis, steps):
    peers = lax.axis_size(axis)
    return [lax.ppermute(x, axis, [(i, i ^ step) for i in range(peers)]) for step in steps]


def summed(x, axis, low, high):
    first, second, third = partners(x, axis, (low, high, low | high))
    return (x + first) + (second + third)


def local(queries, key_rows, values, cotangent, starts, lens, bias):
    count = lax.axis_size("ctx")
    cut, last, first = cut_prompt(starts, key_rows, values)
    held = exchange(cut.reshape(count, 2 * BAND, HD))
    low = shifted(last, 1)
    high = shifted(first, -1)
    stats, *masks = window(
        starts, lens, bias, queries, cotangent, key_rows, values, low, high
    )
    prompt = exchange(route(starts, held)).reshape(BANDS, HEADS, 2 * BAND, HD)
    gprompt, final = prompt_part(bias, queries, cotangent, prompt, stats, masks[2])
    held = exchange(gprompt.reshape(count, SENT, HD))
    arrays = (queries, cotangent, key_rows, values, low, high, prompt)
    begun = own_part(0, bias, *arrays, final, masks, ())
    final, begun = lax.optimization_barrier((final, begun))
    glow, ghigh = halo_grads(queries, cotangent, low, high, final, masks[1])
    right = shifted(glow, -1)
    left = shifted(ghigh, 1)
    held, glow, ghigh = lax.optimization_barrier((held, glow, ghigh))
    owned, sums = gather(starts, held)
    returned = exchange(owned).reshape(BANDS, HEADS, 2 * BAND, HD)
    grad_bias = jnp.sum(summed(sums, "dp", 1, 2), axis=1)
    final, _ = lax.optimization_barrier((final, sums))
    attended, grad_q, gk, gv = own_part(1, bias, *arrays, final, masks, begun)
    outk, outv, both = merge(gk, gv, left, right)
    grad_k, grad_v = finish(starts, outk, outv, both, returned)
    return attended, grad_q, grad_k, grad_v, grad_bias


def solution(mesh):
    split = P("dp", "ctx", None)
    return jax.shard_map(
        local,
        mesh=mesh,
        in_specs=(split, split, split, split, P("dp", None), P("dp", None), P()),
        out_specs=(split, split, split, split, P()),
        check_vma=False,
    )
```
